32 devices in a mesh: dp: 8 (over y, x, core), section: 4 (over z).
Axes of the slice: x: 2, y: 2, z: 4, core: 2. Of those that a mesh axis runs over, the one named last changes fastest.
Arguments:
- x_in: bfloat16 [6144, 768], P('dp'), may hold values from -6 to 6
- lengths: int32 [24, 6], P('dp'), may hold values from 1 to 128, 256 in all within a row
- keep_mask: int32 [6144], P('dp'), may hold values 0 or 1
- w_in: bfloat16 [4, 768, 3072], P('section'), may hold values from -0.6531275 to 0.6531275
- w_down: bfloat16 [4, 1536, 768], P('section'), may hold values from -0.109375 to 0.109375
- vectors: bfloat16 [4, 6, 768], P('section'), may hold values from -1 to 1.5
- cotangent: bfloat16 [6144, 768], P('dp'), may hold values from -6 to 6
Outputs:
- activations: bfloat16 [4, 6144, 768], P('section', 'dp')
- input_grads: bfloat16 [4, 6144, 768], P('section', 'dp')
- grad_w_in: float32 [4, 768, 3072], P('section')
- grad_w_down: float32 [4, 1536, 768], P('section')
- grad_vectors: float32 [4, 6, 768], P('section')
The draws below stay inside these ranges and needn't reach their ends.
Inputs may be any that keep to these rules, and one draw needn't show every extreme that they name: Each row's 6 lengths add up to 256, and the largest of each row is 128.
All inputs are finite; a program needn't handle non-finite values. No bound on the sum of `keep_mask` on one device may be relied on, other than what follows from the above.
Results may differ from the reference program's by a relative error of at most 0.019.
Values may be sent and summed in bfloat16 or wider, within the bound.
No kernel may reach another device: no remote copies, remote signals or barrier semaphores. Data moves between devices by JAX's collectives and lax.ppermute only.
A program may use at most 512 MiB of HBM per device.

```python
import math
import jax
import jax.numpy as jnp
import numpy as np
from jax import lax

D = 768
HEADS = 12
FF = 3072
HEAD_DIM = 64
MICRO = 3
TOK_MB = 256
SEQS = 6
MOST = 128
TOKENS = 6144
N_DP = 8


def draw_w_in(key, part):
    key = jax.random.fold_in(key, 11)
    shape = (4, D, 4 * D)
    base = jax.random.truncated_normal(key, -3.0, 3.0, shape, jnp.float32)
    section_ids = jnp.arange(4)[:, None, None]
    column = jnp.arange(4 * D)[None, None, :]
    boost = jnp.where((section_ids % 2 == 0) & (column >= 3 * D), 6.0, 1.0)
    return (base * boost * D ** (-0.5)).astype(jnp.bfloat16)


def draw_vectors(key, part):
    key = jax.random.fold_in(key, 12)
    shape = (4, 6, D)
    noise = jax.random.truncated_normal(key, -3.0, 3.0, shape, jnp.float32)
    section_ids = jnp.arange(4)[:, None, None]
    row_ids = jnp.arange(6)[None, :, None]
    gain_row = jnp.where(section_ids % 2 == 0, 3, 4)
    values = jnp.where(row_ids == gain_row, 1.0 + 0.1 * noise, 0.3 * noise)
    return values.astype(jnp.bfloat16)


def plant(drawn, own_key, least, top_value):
    place = [jax.random.randint(jax.random.fold_in(own_key, axis), (), 0, length) for axis, length in enumerate(drawn.shape)]
    widest = drawn.shape.index(max(drawn.shape))
    neighbour = place[:widest] + [(place[widest] + 1) % drawn.shape[widest]] + place[widest + 1:]
    return drawn.at[tuple(place)].set(least).at[tuple(neighbour)].set(top_value)


def block_scale(rng, shape, split, least, top_value):
    def one(dim, blocks):
        steps = jax.random.uniform(jax.random.fold_in(jax.random.fold_in(rng, 6), dim), (blocks,), jnp.float32, least / len(split), top_value / len(split))
        return jnp.repeat(jnp.exp(steps), shape[dim] // blocks).reshape((-1,) + (1,) * (len(shape) - dim - 1))

    loudness = one(*split[0])
    for cut in split[1:]:
        loudness = loudness * one(*cut)
    return loudness


def length_profile(amount, total, most, skew):
    weights = [(1 << 20) // math.isqrt(rank ** skew) + 1 for rank in range(2, amount + 1)]
    rest, given = total - most - (amount - 1), [1] * (amount - 1)
    while rest > 0:
        candidates = [i for i in range(amount - 1) if given[i] < most]
        mass, budget = sum([weights[i] for i in candidates]), rest
        for i in candidates:
            addition = min(most - given[i], max(1, budget * weights[i] // mass), rest)
            given[i] = given[i] + addition
            rest = rest - addition
    return np.array([most] + given)


def ragged_sizes(key, number_of, total, reach, lean):
    if number_of == 2:
        one = jax.random.randint(key, (), max(1, total - reach), min(reach, total - 1) + 1)
        return jnp.stack([one, total - one])
    sizes = jnp.asarray(length_profile(number_of, total, reach, lean), jnp.int32)
    couples = (number_of - 1) // 2
    giver, receiver = sizes[1:1 + 2 * couples:2], sizes[2:2 + 2 * couples:2]
    margin = jnp.minimum(giver - 1, reach - receiver)
    passed = jax.random.randint(jax.random.fold_in(key, 1), (couples,), 0, 1 << 20) % (margin + 1)
    sizes = sizes.at[1:1 + 2 * couples:2].set(giver - passed).at[2:2 + 2 * couples:2].set(receiver + passed)
    return sizes[jax.random.permutation(jax.random.fold_in(key, 2), number_of)]


def bell_draw(rng, extent, scale, most, shards=(), kind=jnp.bfloat16):
    values = scale * jax.random.normal(rng, extent, jnp.float32)
    if shards:
        values = values * block_scale(rng, extent, shards, -0.22, 0.18)
    return jnp.clip(values, -most, most).astype(kind)


def setup_inputs(seed: int = 0) -> dict:
    keys = jax.random.split(jax.random.key(seed), 8)
    x_in = bell_draw(keys[0], (TOKENS, D), 1.0, 6.0, ((0, 8),))
    lengths = jax.vmap(lambda own: ragged_sizes(own, SEQS, TOK_MB, MOST, 2))(jax.random.split(keys[1], (N_DP * MICRO))).reshape((N_DP * MICRO, SEQS)).astype(jnp.int32)
    keep_mask = plant((jax.random.randint(keys[2], (TOKENS,), 0, 8) < 7).astype(jnp.int32), jax.random.fold_in(keys[2], 1), 0, 1)
    w_in = draw_w_in(jax.random.fold_in(keys[7], 71), 0)
    w_down = bell_draw(keys[4], (4, 2 * D, D), FF ** -0.5, 0.109375, ((0, 4),))
    vectors = draw_vectors(jax.random.fold_in(keys[7], 71), 0)
    cotangent = bell_draw(keys[6], (TOKENS, D), 1.0, 6.0, ((0, 8),))
    return dict(x_in=x_in, lengths=lengths, keep_mask=keep_mask, w_in=w_in, w_down=w_down, vectors=vectors, cotangent=cotangent)


ln_eps = 1e-05
neg_big = -1000000000.0

@jax.custom_vjp
def low(v):
    return lax.optimization_barrier(v.astype(jnp.bfloat16)).astype(jnp.float32)

@jax.custom_vjp
def low_back(v):
    return v

def low_keep(v):
    return (low(v), None)

def low_pass(kept, grad):
    return (grad,)

def back_keep(v):
    return (v, None)

def back_low(kept, grad):
    return (low(grad),)
low.defvjp(low_keep, low_pass)
low_back.defvjp(back_keep, back_low)

def dense(left_mat, right_mat):
    return jnp.dot(left_mat, right_mat, precision=lax.Precision.HIGHEST, preferred_element_type=jnp.float32)

def layer_norm(residual, ln_gain, ln_shift):
    row_mean = lax.optimization_barrier(jnp.mean(residual, -1, keepdims=True))
    centred = residual - row_mean
    row_var = lax.optimization_barrier(jnp.mean(centred * centred, -1, keepdims=True))
    return centred * lax.rsqrt(row_var + ln_eps) * ln_gain + ln_shift

def segments(seq_lens, row_count):
    seq_ends = jnp.cumsum(seq_lens)
    position = jnp.arange(row_count, dtype=jnp.int32)
    return lax.optimization_barrier(jnp.sum((position[None, :] >= seq_ends[:, None]).astype(jnp.int32), 0))

def allow_mask(segment_ids, keep_row, block_start, block_rows):
    row_count = segment_ids.shape[0]
    query_seg = lax.dynamic_slice_in_dim(segment_ids, block_start, block_rows)
    query_pos = block_start + jnp.arange(block_rows, dtype=jnp.int32)
    key_pos = jnp.arange(row_count, dtype=jnp.int32)
    same_seq = query_seg[:, None] == segment_ids[None, :]
    usable = (keep_row[None, :] == 1) | (query_pos[:, None] == key_pos[None, :])
    return same_seq & usable

def attention(section_in, weights, vector, segment_ids, keep_row):
    row_count, model_width = section_in.shape
    head_scale = HEAD_DIM ** (-0.5)
    qkv_bias = jnp.concatenate([vector[0], jnp.zeros_like(vector[0]), vector[1]])
    qkv_low = low(low_back(dense(section_in, weights[:, :3 * model_width]) + qkv_bias))
    queries = qkv_low[:, :model_width].reshape(row_count, HEADS, HEAD_DIM)
    keys_all = qkv_low[:, model_width:2 * model_width].reshape(row_count, HEADS, HEAD_DIM)
    values = qkv_low[:, 2 * model_width:].reshape(row_count, HEADS, HEAD_DIM)
    block_rows = min(512, row_count)

    def one_block(block_start):
        query_block = lax.dynamic_slice_in_dim(queries, block_start, block_rows)
        scores = jnp.einsum('qhd,khd->hqk', query_block, keys_all, precision=lax.Precision.HIGHEST) * head_scale
        scores = low_back(scores)
        allowed = allow_mask(segment_ids, keep_row, block_start, block_rows)
        scores = jnp.where(allowed[None], scores, neg_big)
        probabilities = low(jax.nn.softmax(scores, axis=-1))
        return jnp.einsum('hqk,khd->qhd', probabilities, values, precision=lax.Precision.HIGHEST)
    starts = jnp.arange(row_count // block_rows, dtype=jnp.int32) * block_rows
    context = lax.map(jax.checkpoint(one_block), starts).reshape(row_count, model_width)
    context = low(low_back(context))
    branch = low_back(dense(context, weights[:, 3 * model_width:]) + vector[2])
    return low(layer_norm(section_in + branch, vector[3], vector[4]))

def feed_forward(section_in, w_up, w_down_full, b_up, b_down, ln_gain, ln_shift):
    pre_act = low_back(dense(section_in, w_up) + b_up)
    hidden = low(jax.nn.gelu(pre_act, approximate=False))
    branch = low_back(dense(hidden, w_down_full) + b_down)
    return low(layer_norm(section_in + branch, ln_gain, ln_shift))

def run_row(w_in, w_down, vectors, x_row, probe_row, seq_lens, keep_row):
    segment_ids = segments(seq_lens, x_row.shape[0])
    section_one = attention(low_back(x_row), w_in[0], vectors[0], segment_ids, keep_row)
    section_two = feed_forward(low_back(section_one + probe_row[0]), w_in[1], jnp.concatenate([w_down[0], w_down[1]], 0), vectors[1, 0:4].reshape(-1), vectors[0, 5], vectors[1, 4], vectors[1, 5])
    section_three = attention(low_back(section_two + probe_row[1]), w_in[2], vectors[2], segment_ids, keep_row)
    section_four = feed_forward(low_back(section_three + probe_row[2]), w_in[3], jnp.concatenate([w_down[2], w_down[3]], 0), vectors[3, 0:4].reshape(-1), vectors[2, 5], vectors[3, 4], vectors[3, 5])
    return jnp.stack([section_one, section_two, section_three, section_four])

def reference(x_in, lengths, keep_mask, w_in, w_down, vectors, cotangent):
    row_total = lengths.shape[0]
    row_count = keep_mask.shape[0] // row_total
    model_width = x_in.shape[1]
    x_rows = x_in.astype(jnp.float32).reshape(row_total, row_count, model_width)
    keep_rows = keep_mask.reshape(row_total, row_count)
    probes = jnp.zeros((row_total, 3, row_count, model_width), jnp.float32)
    row_step = jax.checkpoint(run_row)

    def forward(w_full, w_half, vector_all, x_all, probe_all):

        def scan_step(carry, item):
            x_row, probe_row, seq_lens, keep_row = item
            return (carry, row_step(w_full, w_half, vector_all, x_row, probe_row, seq_lens, keep_row))
        return lax.scan(scan_step, jnp.zeros((), jnp.float32), (x_all, probe_all, lengths, keep_rows))[1]
    acts, pullback = jax.vjp(forward, w_in.astype(jnp.float32), w_down.astype(jnp.float32), vectors.astype(jnp.float32), x_rows, probes)
    cot_rows = cotangent.astype(jnp.float32).reshape(row_total, row_count, model_width)
    seeds = jnp.zeros_like(acts).at[:, 3].set(cot_rows)
    grad_full, grad_half, grad_vector, grad_x, grad_probe = pullback(seeds)
    section_grads = jnp.concatenate([grad_x[:, None], grad_probe], 1)
    activations = jnp.transpose(acts, (1, 0, 2, 3)).reshape(4, row_total * row_count, model_width).astype(jnp.bfloat16)
    input_grads = jnp.transpose(section_grads, (1, 0, 2, 3)).reshape(4, row_total * row_count, model_width).astype(jnp.bfloat16)
    return (activations, input_grads, grad_full, grad_half, grad_vector)
```

```python
import functools

import jax
import jax.numpy as jnp
from jax import lax
from jax.experimental import pallas as pl
from jax.experimental.pallas import tpu as pltpu
from jax.sharding import PartitionSpec as P

HEADS = 12
HEAD_DIM = 64
QUAD = 4 * HEAD_DIM
LANES = 128

ln_eps = 1e-05
neg_big = -1000000000.0
root_half = 0.7071067811865476
root_two_pi = 0.3989422804014327

f32 = jnp.float32
bf16 = jnp.bfloat16

HBM = pl.BlockSpec(memory_space=pl.ANY)
VMEM = pl.BlockSpec(memory_space=pltpu.VMEM)
SMEM = pl.BlockSpec(memory_space=pltpu.SMEM)
VMEM_LIMIT = 48 * 1024 * 1024


def dot(a, b):
    return jnp.dot(a, b, preferred_element_type=f32)


def dot_nt(a, b):
    return lax.dot_general(a, b, (((1,), (1,)), ((), ())), preferred_element_type=f32)


def dot_tn(a, b):
    return lax.dot_general(a, b, (((0,), (0,)), ((), ())), preferred_element_type=f32)


def normalise(residual):
    mean = jnp.mean(residual, -1, keepdims=True)
    centred = residual - mean
    rstd = lax.rsqrt(jnp.mean(centred * centred, -1, keepdims=True) + ln_eps)
    return centred * rstd, rstd


def norm_back(grad, normed, rstd, gain):
    e = grad * gain
    return (e - jnp.mean(e, -1, keepdims=True) - normed * jnp.mean(e * normed, -1, keepdims=True)) * rstd


def gelu_and_slope(pre):
    size = jnp.abs(pre)
    t = 1.0 / (1.0 + (0.3275911 * root_half) * size)
    poly = t * (
        0.5 * 0.254829592
        + t * (0.5 * -0.284496736 + t * (0.5 * 1.421413741 + t * (0.5 * -1.453152027 + t * (0.5 * 1.061405429))))
    )
    bell = jnp.exp(-0.5 * pre * pre)
    tail = poly * bell
    cdf = jnp.where(pre >= 0.0, 1.0 - tail, tail)
    return pre * cdf, cdf + pre * (bell * root_two_pi)


def total_rows(value):
    return jnp.sum(value, 0, keepdims=True)


class Copies:
    def __init__(self, sems):
        self.sems = sems
        self.used = 0
        self.open = []

    def start(self, src, dst):
        copy = pltpu.make_async_copy(src, dst, self.sems.at[self.used])
        self.used += 1
        copy.start()
        return copy

    def out(self, src, dst):
        self.open.append(self.start(src, dst))

    def drain(self):
        for copy in self.open:
            copy.wait()


def head_lanes(rows):
    return lax.broadcasted_iota(jnp.int32, (rows, QUAD), 1) // HEAD_DIM


def attn_forward_body(slot, lens, keep_ref, vec_ref, x_v, w_v, wait_w, sa_v, p_v, emit):
    rows, width = x_v.shape
    ends, end = [], 0
    for k in range(lens.shape[1]):
        end = end + lens[slot, k]
        ends.append(end)
    query_pos = lax.broadcasted_iota(jnp.int32, (rows, 1), 0)
    key_pos = lax.broadcasted_iota(jnp.int32, (1, rows), 1)
    query_seg = sum((query_pos >= end).astype(jnp.int32) for end in ends)
    key_seg = sum((key_pos >= end).astype(jnp.int32) for end in ends)
    keep = keep_ref[slot : slot + 1, :] == 1
    allowed = (query_seg == key_seg) & (keep | (query_pos == key_pos))

    x = x_v[...]
    for c, bias_row in enumerate((0, None, 1)):
        wait_w(c)
        part = dot(x, w_v[:, c * width : (c + 1) * width])
        if bias_row is not None:
            part = part + vec_ref[bias_row : bias_row + 1, :].astype(f32)
        sa_v[:, c * width : (c + 1) * width] = part.astype(bf16)
    emit("qkv")
    lane_row = lax.broadcasted_iota(jnp.int32, (1, QUAD), 1) // HEAD_DIM
    for j in range(width // QUAD):
        lo = j * QUAD
        q4 = sa_v[:, lo : lo + QUAD]
        k4 = sa_v[:, width + lo : width + lo + QUAD]
        v4 = sa_v[:, 2 * width + lo : 2 * width + lo + QUAD]
        spread = []
        for h in range(4):
            pick = (lane_row == h).astype(f32)
            scores = dot_nt(q4 * (pick * HEAD_DIM**-0.5).astype(bf16), k4)
            scores = jnp.where(allowed, scores, neg_big)
            raised = jnp.exp(scores - jnp.max(scores, -1, keepdims=True))
            probs = raised * (1.0 / jnp.sum(raised, -1, keepdims=True))
            at = (4 * j + h) * rows
            p_v[:, at : at + rows] = probs.astype(bf16)
            spread.append(v4 * pick.astype(bf16))
        context = dot(p_v[:, 4 * j * rows : 4 * (j + 1) * rows], jnp.concatenate(spread, 0))
        sa_v[:, 3 * width + lo : 3 * width + lo + QUAD] = context.astype(bf16)
        emit("probs", j)
    wait_w(3)
    branch = dot(sa_v[:, 3 * width :], w_v[:, 3 * width :]) + vec_ref[2:3, :].astype(f32)
    return x.astype(f32) + branch


def attn_forward_kernel(
    stage, slot, first, from_start, meta, lens, keep_ref, vec_ref, x_src, w_hbm, *refs
):
    ins = 0 if first else 6
    send, xs, acts, nb, rb, sa, sb = refs[ins : ins + 7]
    x_v, w_v, sa_v, p_v, n_v, r_v, o_v, sems = refs[ins + 7 :]
    rows, width = x_v.shape
    here = pl.ds(slot * rows, rows)

    @pl.when(meta[0] == stage)
    def _():
        copies = Copies(sems)
        x_copy = copies.start(x_src.at[here] if from_start else x_src, x_v)
        w_copies = [
            copies.start(w_hbm.at[:, pl.ds(c * width, width)], w_v.at[:, pl.ds(c * width, width)])
            for c in range(4)
        ]
        x_copy.wait()
        copies.out(x_v, xs.at[here])

        def emit(what, j=0):
            if what == "qkv":
                cut = pl.ds(0, 3 * width)
                copies.out(sa_v.at[:, cut], sa.at[here, cut])
            else:
                cut = pl.ds(4 * j * rows, 4 * rows)
                copies.out(p_v.at[:, cut], sb.at[here, cut])

        residual = attn_forward_body(
            slot, lens, keep_ref, vec_ref, x_v, w_v, lambda c: w_copies[c].wait(), sa_v, p_v, emit
        )
        cut = pl.ds(3 * width, width)
        copies.out(sa_v.at[:, cut], sa.at[here, cut])
        normed, rstd = normalise(residual)
        out = normed * vec_ref[3:4, :].astype(f32) + vec_ref[4:5, :].astype(f32)
        o_v[...] = out.astype(bf16)
        copies.out(o_v, send)
        copies.out(o_v, acts.at[here])
        n_v[...] = normed
        r_v[...] = jnp.broadcast_to(rstd, r_v.shape)
        copies.out(n_v, nb.at[here])
        copies.out(r_v, rb.at[here])
        copies.drain()


def attn_backward_kernel(
    stage, slot, meta, vec_ref, g_src, w_hbm, nb, rb, sa, sb, *refs
):
    send, gin, dr, vg = refs[3:7]
    g_v, w_v, n_v, r_v, sa_v, p_v, dr_v, o_v, vec_v, sems = refs[7:]
    rows, width = g_v.shape
    here = pl.ds(slot * rows, rows)

    @pl.when(meta[0] == stage)
    def _():
        copies = Copies(sems)
        first = [
            copies.start(g_src, g_v),
            copies.start(nb.at[here], n_v),
            copies.start(rb.at[here], r_v),
        ]
        order = (3, 0, 1, 2)
        w_copies = {}
        cuts = [pl.ds(c * width, width) for c in range(4)]
        w_copies[3] = copies.start(w_hbm.at[:, cuts[3]], w_v.at[:, cuts[3]])
        sa_copy = copies.start(sa.at[here], sa_v)
        p_copy = copies.start(sb.at[here], p_v)
        for c in order[1:]:
            w_copies[c] = copies.start(w_hbm.at[:, cuts[c]], w_v.at[:, cuts[c]])
        for copy in first:
            copy.wait()
        grad = g_v[...].astype(f32)
        normed = n_v[...]
        d_resid = norm_back(grad, normed, r_v[:, 0:1], vec_ref[3:4, :].astype(f32))
        d_branch = d_resid.astype(bf16)
        n_v[...] = d_resid
        dr_v[:, 3 * width :] = d_branch
        vec_v[...] = jnp.zeros_like(vec_v)
        vec_v[2:3, :] = total_rows(d_branch.astype(f32))
        vec_v[3:4, :] = total_rows(grad * normed)
        vec_v[4:5, :] = total_rows(grad)
        copies.out(dr_v.at[:, cuts[3]], dr.at[here, cuts[3]])
        w_copies[3].wait()
        d_context = dot_nt(d_branch, w_v[:, 3 * width :]).astype(bf16)
        sa_copy.wait()
        p_copy.wait()
        lane_row = lax.broadcasted_iota(jnp.int32, (1, QUAD), 1) // HEAD_DIM
        for j in range(width // QUAD):
            lo = j * QUAD
            q4 = sa_v[:, lo : lo + QUAD]
            k4 = sa_v[:, width + lo : width + lo + QUAD]
            v4 = sa_v[:, 2 * width + lo : 2 * width + lo + QUAD]
            c4 = d_context[:, lo : lo + QUAD]
            q_turned = q4.T
            c_turned = c4.T
            spread, d_scores, d_keys, d_values = [], [], [], []
            for h in range(4):
                pick = (lane_row == h).astype(bf16)
                at = (4 * j + h) * rows
                probs_low = p_v[:, at : at + rows]
                probs = probs_low.astype(f32)
                d_probs = dot_nt(c4 * pick, v4)
                weighed = probs * d_probs
                d_score = (weighed - probs * jnp.sum(weighed, -1, keepdims=True)).astype(bf16)
                d_scores.append(d_score)
                spread.append(k4 * pick)
                mine = slice(h * HEAD_DIM, (h + 1) * HEAD_DIM)
                d_keys.append(dot(q_turned[mine], d_score))
                d_values.append(dot(c_turned[mine], probs_low))
            d_query = dot(jnp.concatenate(d_scores, 1), jnp.concatenate(spread, 0))
            scale = HEAD_DIM**-0.5
            d_key = jnp.concatenate(d_keys, 0).T
            d_value = jnp.concatenate(d_values, 0).T
            dr_v[:, lo : lo + QUAD] = (d_query * scale).astype(bf16)
            dr_v[:, width + lo : width + lo + QUAD] = (d_key * scale).astype(bf16)
            dr_v[:, 2 * width + lo : 2 * width + lo + QUAD] = d_value.astype(bf16)
        cut = pl.ds(0, 3 * width)
        copies.out(dr_v.at[:, cut], dr.at[here, cut])
        d_input = n_v[...]
        for c in range(3):
            w_copies[c].wait()
            d_input = d_input + dot_nt(dr_v[:, c * width : (c + 1) * width], w_v[:, c * width : (c + 1) * width])
        o_v[...] = d_input.astype(bf16)
        copies.out(o_v, send)
        copies.out(o_v, gin.at[here])
        vec_v[0:1, :] = total_rows(dr_v[:, 0:width].astype(f32))
        vec_v[1:2, :] = total_rows(dr_v[:, 2 * width : 3 * width].astype(f32))
        copies.out(vec_v, vg.at[pl.ds(slot * 8, 8)])
        copies.drain()


def start_ffn_weights(copies, meta, w_hbm, down_hbm, pieces, masks, w_v, d_v):
    width = w_v.shape[0]
    half = down_hbm.shape[0]
    cuts = [pl.ds(c * width, width) for c in range(4)]
    ups, downs = {}, {}
    for c in (2, 3):
        ups[c] = copies.start(w_hbm.at[:, cuts[c]], w_v.at[:, cuts[c]])
        downs[c] = copies.start(down_hbm.at[pl.ds((c - 2) * width, width)], d_v.at[cuts[c]])
    for c in (0, 1):
        ups[c] = copies.start(w_hbm.at[:, cuts[c]], w_v.at[:, cuts[c]])
    parts = []
    for piece, mask in zip(pieces, masks):
        size = piece.shape[0]
        at = pl.multiple_of((meta[1] ^ mask) * size, 16)
        parts.append(copies.start(piece, d_v.at[pl.ds(at, size)]))
    waited = set()

    def wait_up(c):
        ups[c].wait()

    def wait_down(c):
        if c >= 2:
            downs[c].wait()
        elif not waited:
            waited.add(0)
            for part in parts:
                part.wait()

    return wait_up, wait_down


def ffn_forward_body(x, vec_ref, b2_ref, w_v, d_v, wait_up, wait_down, h_v, s_v, emit):
    width = w_v.shape[0]
    branch = x.astype(f32) + b2_ref[0:1, :].astype(f32)
    for c in (2, 3, 0, 1):
        cut = slice(c * width, (c + 1) * width)
        wait_up(c)
        pre = dot(x, w_v[:, cut]) + vec_ref[c : c + 1, :].astype(f32)
        hidden, slope = gelu_and_slope(pre)
        h_v[:, cut] = hidden.astype(bf16)
        s_v[:, cut] = slope.astype(bf16)
        emit(c)
        wait_down(c)
        branch = branch + dot(h_v[:, cut], d_v[cut, :])
    return branch


def ffn_backward_body(grad, normed, rstd, vec_ref, w_v, d_v, wait_up, wait_down, s_v, db_v, dp_v, vec_v, emit):
    width = w_v.shape[0]
    d_resid = norm_back(grad, normed, rstd, vec_ref[4:5, :].astype(f32))
    d_branch = d_resid.astype(bf16)
    db_v[...] = d_branch
    vec_v[...] = jnp.zeros_like(vec_v)
    vec_v[4:5, :] = total_rows(grad * normed)
    vec_v[5:6, :] = total_rows(grad)
    vec_v[6:7, :] = total_rows(d_branch.astype(f32))
    emit("branch")
    d_input = d_resid
    for c in (2, 3, 0, 1):
        cut = slice(c * width, (c + 1) * width)
        wait_down(c)
        d_pre = (dot_nt(d_branch, d_v[cut, :]) * s_v[:, cut].astype(f32)).astype(bf16)
        dp_v[:, cut] = d_pre
        emit(c)
        vec_v[c : c + 1, :] = total_rows(d_pre.astype(f32))
        wait_up(c)
        d_input = d_input + dot_nt(d_pre, w_v[:, cut])
    return d_input


def ffn_forward_kernel(stage, slot, masks, meta, vec_ref, b2_ref, x_src, w_hbm, down_hbm, *refs):
    pieces = refs[: len(masks)]
    refs = refs[len(masks) + 6 :]
    send, xs, acts, nb, rb, sa, sb = refs[:7]
    x_v, w_v, d_v, h_v, s_v, n_v, r_v, o_v, sems = refs[7:]
    rows, width = x_v.shape
    here = pl.ds(slot * rows, rows)

    @pl.when(meta[0] == stage)
    def _():
        copies = Copies(sems)
        x_copy = copies.start(x_src, x_v)
        wait_up, wait_down = start_ffn_weights(copies, meta, w_hbm, down_hbm, pieces, masks, w_v, d_v)
        x_copy.wait()
        copies.out(x_v, xs.at[here])

        def emit(c):
            cut = pl.ds(c * width, width)
            copies.out(h_v.at[:, cut], sa.at[here, cut])
            copies.out(s_v.at[:, cut], sb.at[here, cut])

        residual = ffn_forward_body(
            x_v[...], vec_ref, b2_ref, w_v, d_v, wait_up, wait_down, h_v, s_v, emit
        )
        normed, rstd = normalise(residual)
        out = normed * vec_ref[4:5, :].astype(f32) + vec_ref[5:6, :].astype(f32)
        o_v[...] = out.astype(bf16)
        copies.out(o_v, send)
        copies.out(o_v, acts.at[here])
        n_v[...] = normed
        r_v[...] = jnp.broadcast_to(rstd, r_v.shape)
        copies.out(n_v, nb.at[here])
        copies.out(r_v, rb.at[here])
        copies.drain()


def ffn_backward_kernel(stage, slot, masks, meta, vec_ref, g_src, w_hbm, down_hbm, nb, rb, sb, *refs):
    pieces = refs[: len(masks)]
    refs = refs[len(masks) + 4 :]
    send, gin, dr, db, vg = refs[:5]
    g_v, w_v, d_v, s_v, n_v, r_v, db_v, dp_v, o_v, vec_v, sems = refs[5:]
    rows, width = g_v.shape
    here = pl.ds(slot * rows, rows)

    @pl.when(meta[0] == stage)
    def _():
        copies = Copies(sems)
        first = [
            copies.start(g_src, g_v),
            copies.start(nb.at[here], n_v),
            copies.start(rb.at[here], r_v),
            copies.start(sb.at[here], s_v),
        ]
        wait_up, wait_down = start_ffn_weights(copies, meta, w_hbm, down_hbm, pieces, masks, w_v, d_v)
        for copy in first:
            copy.wait()

        def emit(c):
            if c == "branch":
                copies.out(db_v, db.at[here])
            else:
                cut = pl.ds(c * width, width)
                copies.out(dp_v.at[:, cut], dr.at[here, cut])

        d_input = ffn_backward_body(
            g_v[...].astype(f32), n_v[...], r_v[:, 0:1], vec_ref, w_v, d_v, wait_up, wait_down, s_v, db_v, dp_v, vec_v, emit
        )
        o_v[...] = d_input.astype(bf16)
        copies.out(o_v, send)
        copies.out(o_v, gin.at[here])
        copies.out(vec_v, vg.at[pl.ds(slot * 8, 8)])
        copies.drain()


def ffn_both_kernel(stage, slot, masks, first, meta, vec_ref, b2_ref, x_src, cot, w_hbm, down_hbm, *refs):
    pieces = refs[: len(masks)]
    refs = refs[len(masks) + (3 if first else 7) :]
    send, xs, acts, sa, gin, dr, db, vg = refs[:8]
    x_v, g_v, w_v, d_v, h_v, s_v, db_v, dp_v, o_v, i_v, vec_v, sems = refs[8:]
    rows, width = x_v.shape
    here = pl.ds(slot * rows, rows)

    @pl.when(meta[0] == stage)
    def _():
        copies = Copies(sems)
        x_copy = copies.start(x_src, x_v)
        wait_up, wait_down = start_ffn_weights(copies, meta, w_hbm, down_hbm, pieces, masks, w_v, d_v)
        g_copy = copies.start(cot.at[here], g_v)
        x_copy.wait()
        copies.out(x_v, xs.at[here])

        def emit(c):
            cut = pl.ds(c * width, width)
            copies.out(h_v.at[:, cut], sa.at[here, cut])

        residual = ffn_forward_body(
            x_v[...], vec_ref, b2_ref, w_v, d_v, wait_up, wait_down, h_v, s_v, emit
        )
        normed, rstd = normalise(residual)
        out = normed * vec_ref[4:5, :].astype(f32) + vec_ref[5:6, :].astype(f32)
        o_v[...] = out.astype(bf16)
        copies.out(o_v, acts.at[here])
        g_copy.wait()

        def emit_back(c):
            if c == "branch":
                copies.out(db_v, db.at[here])
            else:
                cut = pl.ds(c * width, width)
                copies.out(dp_v.at[:, cut], dr.at[here, cut])

        ready = lambda c: None
        d_input = ffn_backward_body(
            g_v[...].astype(f32), normed, rstd, vec_ref, w_v, d_v, ready, ready, s_v, db_v, dp_v, vec_v, emit_back
        )
        i_v[...] = d_input.astype(bf16)
        copies.out(i_v, send)
        copies.out(i_v, gin.at[here])
        copies.out(vec_v, vg.at[pl.ds(slot * 8, 8)])
        copies.drain()


def down_grad_kernel(meta, sa, db, up_out, low_out, a_v, b_v, o_v, sems):
    tokens, width = b_v.shape

    @pl.when(meta[0] % 2 == 1)
    def _():
        copies = Copies(sems)
        b_copy = copies.start(db, b_v)
        cuts = [pl.ds(c * width, width) for c in range(4)]
        a_copies = [copies.start(sa.at[:, cut], a_v.at[:, cut]) for cut in cuts]
        b_copy.wait()
        for c, cut in enumerate(cuts):
            a_copies[c].wait()
            o_v[cut, :] = dot_tn(a_v[:, c * width : (c + 1) * width], b_v[...]).astype(bf16)
            out = up_out if c < 2 else low_out
            copies.out(o_v.at[cut], out.at[pl.ds((c % 2) * width, width)])
        copies.drain()


def in_grad_kernel(meta, xs, sa, dr, out, x_v, r_v, o_v, sems):
    tokens, width = x_v.shape
    copies = Copies(sems)
    x_copy = copies.start(xs, x_v)
    cuts = [pl.ds(c * width, width) for c in range(4)]
    r_copies = [copies.start(dr.at[:, cut], r_v.at[:, cut]) for cut in cuts]
    x_copy.wait()
    for c in range(3):
        r_copies[c].wait()
        o_v[:, c * width : (c + 1) * width] = dot_tn(x_v[...], r_v[:, c * width : (c + 1) * width]).astype(bf16)
        copies.out(o_v.at[:, cuts[c]], out.at[:, cuts[c]])
    r_copies[3].wait()

    @pl.when(meta[0] % 2 == 0)
    def _():
        copies.start(sa.at[:, cuts[3]], x_v).wait()

    o_v[:, 3 * width :] = dot_tn(x_v[...], r_v[:, 3 * width :]).astype(bf16)
    copies.out(o_v.at[:, cuts[3]], out.at[:, cuts[3]])
    copies.drain()


def swap(value, mask, count):
    return lax.ppermute(value, "dp", [(i, i ^ mask) for i in range(count)])


def half_of(value, upper):
    rows = value.shape[0] // 2
    return lax.dynamic_slice_in_dim(value, jnp.where(upper, rows, 0), rows)


def scatter_sum(value, bits, me, count):
    for bit in bits:
        mine = (me >> bit) % 2 == 1
        got = swap(half_of(value, jnp.logical_not(mine)), 1 << bit, count)
        kept = half_of(value, mine)
        value = (kept.astype(f32) + got.astype(f32)).astype(bf16)
    return value


def gather_rows(value, bits, me, count):
    for bit in reversed(bits):
        mine = (me >> bit) % 2 == 1
        got = swap(value, 1 << bit, count)
        value = jnp.concatenate([jnp.where(mine, got, value), jnp.where(mine, value, got)], 0)
    return value


def bit_orders(count):
    far = list(range(1, count.bit_length() - 1))
    return far, far[::-1]


def reduce_over_dp(value, me, count):
    own = scatter_sum(value, [0], me, count)
    rows = own.shape[0] // 2
    orders = bit_orders(count)
    return [scatter_sum(own[s * rows : (s + 1) * rows], orders[s], me, count) for s in range(2)]


def spread_over_dp(shares, me, count):
    orders = bit_orders(count)
    both = [gather_rows(share, order, me, count) for share, order in zip(shares, orders)]
    return gather_rows(jnp.concatenate(both, 0), [0], me, count)


def call(kernel, outs, scratch, ins, specs, aliases=None, out_specs=None, flops=0, copies=1):
    return pl.pallas_call(
        kernel,
        out_shape=outs,
        in_specs=specs,
        out_specs=out_specs or [HBM] * len(outs),
        scratch_shapes=list(scratch) + [pltpu.SemaphoreType.DMA((copies,))],
        input_output_aliases=aliases or {},
        compiler_params=pltpu.CompilerParams(vmem_limit_bytes=VMEM_LIMIT),
        cost_estimate=pl.CostEstimate(flops=flops, bytes_accessed=12_000_000, transcendentals=0),
    )(*ins)


def local(x_in, lengths, keep_mask, w_in, w_down, vectors, cotangent):
    micro_count = lengths.shape[0]
    tokens, width = x_in.shape
    rows = tokens // micro_count
    wide = 4 * width
    count = lax.axis_size("dp")
    sections = lax.axis_size("section")
    section = lax.axis_index("section")
    me = lax.axis_index("dp")
    is_ffn = section % 2 == 1
    meta = jnp.stack([section, me]).astype(jnp.int32)
    weights, down, vec = w_in[0], w_down[0], vectors[0]
    keep = keep_mask.reshape(micro_count, rows)

    def hop(value, stage, step):
        return lax.ppermute(value, "section", [(stage, stage + step)])

    onward = [(s, s + 1) for s in range(0, sections, 2)]
    share = down.shape[0] // count
    own_piece = lax.ppermute(lax.dynamic_slice_in_dim(down, me * share, share), "section", onward)
    b2 = lax.ppermute(vec[5:6], "section", onward)
    pieces, masks = [own_piece], [0]
    for far in range(2, count, 2):
        pieces.append(swap(own_piece, far, count))
        masks.append(far)
    for k in range(len(masks)):
        pieces.append(swap(pieces[k], 1, count))
        masks.append(masks[k] ^ 1)
    masks = tuple(masks)

    def sds(shape, dtype):
        return jax.ShapeDtypeStruct(shape, dtype)

    row_out = sds((rows, width), bf16)
    state = [
        sds((tokens, width), bf16),
        sds((tokens, width), bf16),
        sds((tokens, width), f32),
        sds((tokens, LANES), f32),
        sds((tokens, wide), bf16),
        sds((tokens, HEADS * rows), bf16),
    ]
    v_row = pltpu.VMEM((rows, width), bf16)
    v_row32 = pltpu.VMEM((rows, width), f32)
    v_wide = pltpu.VMEM((rows, wide), bf16)
    v_in = pltpu.VMEM((width, wide), bf16)
    v_down = pltpu.VMEM((wide, width), bf16)
    v_stat = pltpu.VMEM((rows, LANES), f32)
    v_probs = pltpu.VMEM((rows, HEADS * rows), bf16)
    v_vec = pltpu.VMEM((8, width), f32)
    flops = 2 * rows * width * wide

    saved = None

    def attn_forward(stage, slot, source):
        nonlocal saved
        first = saved is None
        ins = [meta, lengths, keep, vec, source, weights] + ([] if first else saved)
        specs = [SMEM, SMEM, VMEM, VMEM] + [HBM] * (len(ins) - 4)
        from_start = stage == 0
        got = call(
            functools.partial(attn_forward_kernel, stage, slot, first, from_start),
            [row_out] + state,
            [v_row, v_in, v_wide, v_probs, v_row32, v_stat, v_row],
            ins,
            specs,
            {} if first else {6 + k: 1 + k for k in range(6)},
            flops=flops,
            copies=16,
        )
        saved = list(got[1:])
        return got[0]

    def ffn_forward(stage, slot, source):
        nonlocal saved
        ins = [meta, vec, b2, source, weights, down] + pieces + saved
        specs = [SMEM, VMEM, VMEM] + [HBM] * (len(ins) - 3)
        base = 6 + len(pieces)
        got = call(
            functools.partial(ffn_forward_kernel, stage, slot, masks),
            [row_out] + state,
            [v_row, v_in, v_down, v_wide, v_wide, v_row32, v_stat, v_row],
            ins,
            specs,
            {base + k: 1 + k for k in range(6)},
            flops=2 * flops,
            copies=20 + len(pieces),
        )
        saved = list(got[1:])
        return got[0]

    grads = None

    def ffn_both(stage, slot, source):
        nonlocal saved, grads
        first = grads is None
        xs, acts, nb, rb, sa, sb = saved
        ins = [meta, vec, b2, source, cotangent, weights, down] + pieces + [xs, acts, sa] + ([] if first else grads)
        specs = [SMEM, VMEM, VMEM] + [HBM] * (len(ins) - 3)
        base = 7 + len(pieces)
        outs = [row_out, state[0], state[1], state[4]] + [
            sds((tokens, width), bf16),
            sds((tokens, wide), bf16),
            sds((tokens, width), bf16),
            sds((8 * micro_count, width), f32),
        ]
        got = call(
            functools.partial(ffn_both_kernel, stage, slot, masks, first),
            outs,
            [v_row, v_row, v_in, v_down, v_wide, v_wide, v_row, v_wide, v_row, v_row, v_vec],
            ins,
            specs,
            {base + k: 1 + k for k in range(3 if first else 7)},
            flops=4 * flops,
            copies=25 + len(pieces),
        )
        saved = [got[1], got[2], nb, rb, got[3], sb]
        grads = list(got[4:])
        return got[0]

    def attn_backward(stage, slot, source):
        nonlocal grads
        xs, acts, nb, rb, sa, sb = saved
        gin, dr, db, vg = grads
        ins = [meta, vec, source, weights, nb, rb, sa, sb, gin, dr, vg]
        specs = [SMEM, VMEM] + [HBM] * (len(ins) - 2)
        got = call(
            functools.partial(attn_backward_kernel, stage, slot),
            [row_out] + [sds(a.shape, a.dtype) for a in (gin, dr, vg)],
            [v_row, v_in, v_row32, v_stat, v_wide, v_probs, v_wide, v_row, v_vec],
            ins,
            specs,
            {8 + k: 1 + k for k in range(3)},
            flops=3 * flops,
            copies=16,
        )
        grads = [got[1], got[2], db, got[3]]
        return got[0]

    def ffn_backward(stage, slot, source):
        nonlocal grads
        xs, acts, nb, rb, sa, sb = saved
        ins = [meta, vec, source, weights, down, nb, rb, sb] + pieces + grads
        specs = [SMEM, VMEM] + [HBM] * (len(ins) - 2)
        base = 8 + len(pieces)
        got = call(
            functools.partial(ffn_backward_kernel, stage, slot, masks),
            [row_out] + [sds(a.shape, a.dtype) for a in grads],
            [v_row, v_in, v_down, v_wide, v_row32, v_stat, v_row, v_wide, v_row, v_vec],
            ins,
            specs,
            {base + k: 1 + k for k in range(4)},
            flops=2 * flops,
            copies=20 + len(pieces),
        )
        grads = list(got[1:])
        return got[0]

    arrived = [x_in] * micro_count
    for stage in range(sections - 1):
        step = ffn_forward if stage % 2 else attn_forward
        arrived = [hop(step(stage, slot, arrived[slot]), stage, 1) for slot in range(micro_count)]
    last = sections - 1
    arrived = [hop(ffn_both(last, slot, arrived[slot]), last, -1) for slot in range(micro_count)]
    for stage in range(last - 1, -1, -1):
        step = ffn_backward if stage % 2 else attn_backward
        for slot in range(micro_count):
            done = step(stage, slot, arrived[slot])
            if stage:
                arrived[slot] = hop(done, stage, -1)
    xs, acts, nb, rb, sa, sb = saved
    gin, dr, db, vg = grads

    half = sds((2 * width, width), bf16)
    up, low = call(
        down_grad_kernel,
        [half, half],
        [pltpu.VMEM((tokens, wide), bf16), pltpu.VMEM((tokens, width), bf16), v_down],
        [meta, sa, db],
        [SMEM, HBM, HBM],
        flops=2 * tokens * width * wide,
        copies=9,
    )
    (grad_in,) = call(
        in_grad_kernel,
        [sds((width, wide), bf16)],
        [pltpu.VMEM((tokens, width), bf16), pltpu.VMEM((tokens, wide), bf16), v_in],
        [meta, xs, sa, dr],
        [SMEM, HBM, HBM, HBM],
        flops=2 * tokens * width * wide,
        copies=12,
    )

    vec_sum = vg.reshape(micro_count, 8, width).sum(0)
    for bit in range(count.bit_length() - 1):
        vec_sum = vec_sum + swap(vec_sum, 1 << bit, count)
    backward = [(s, s - 1) for s in range(1, sections, 2)]
    b2_grad = lax.ppermute(vec_sum[6:7], "section", backward)
    total_vec = jnp.concatenate([vec_sum[0:5], jnp.where(is_ffn, vec_sum[5:6], b2_grad)], 0)

    up_shares = reduce_over_dp(up, me, count)
    low_shares = reduce_over_dp(low, me, count)
    in_shares = reduce_over_dp(grad_in, me, count)
    handed = [lax.ppermute(part, "section", backward) for part in up_shares]
    down_shares = [jnp.where(is_ffn, a, b) for a, b in zip(low_shares, handed)]
    total_down = spread_over_dp(down_shares, me, count).astype(f32)
    total_in = spread_over_dp(in_shares, me, count).astype(f32)
    return (acts[None], gin[None], total_in[None], total_down[None], total_vec[None])


def solution(mesh):
    placed = (
        P("dp", None),
        P("dp", None),
        P("dp"),
        P("section", None, None),
        P("section", None, None),
        P("section", None, None),
        P("dp", None),
    )
    return jax.shard_map(
        local,
        mesh=mesh,
        in_specs=placed,
        out_specs=(
            P("section", "dp", None),
            P("section", "dp", None),
            P("section", None, None),
            P("section", None, None),
            P("section", None, None),
        ),
        check_vma=False,
    )
```

```python
import functools

import jax
import jax.numpy as jnp
from jax import lax
from jax.experimental import pallas as pl
from jax.experimental.pallas import tpu as pltpu
from jax.sharding import PartitionSpec as P

HEADS = 12
HEAD_DIM = 64
QUAD = 4 * HEAD_DIM
LANES = 128

ln_eps = 1e-05
neg_big = -1000000000.0
root_half = 0.7071067811865476
root_two_pi = 0.3989422804014327

f32 = jnp.float32
bf16 = jnp.bfloat16

IN_VMEM = pl.BlockSpec(memory_space=pltpu.VMEM)
IN_HBM = pl.BlockSpec(memory_space=pltpu.HBM)
IN_SMEM = pl.BlockSpec(memory_space=pltpu.SMEM)
ANYWHERE = pl.BlockSpec(memory_space=pl.ANY)
VMEM_LIMIT = 4 * 1024 * 1024
STORE_LIMIT = 16 * 1024 * 1024


def dot(a, b):
    return jnp.dot(a, b, preferred_element_type=f32)


def dot_nt(a, b):
    return lax.dot_general(a, b, (((1,), (1,)), ((), ())), preferred_element_type=f32)


def dot_tn(a, b):
    return lax.dot_general(a, b, (((0,), (0,)), ((), ())), preferred_element_type=f32)


def total_rows(value):
    return jnp.sum(value, 0, keepdims=True)


def kernel_call(body, outs, ins, aliases=None, scratch=(), name=None, plain_ins=(), limit=VMEM_LIMIT):
    specs, placed = [], []
    for n, value in enumerate(ins):
        if n in plain_ins:
            placed.append(pltpu.with_memory_space_constraint(value, pltpu.HBM))
            specs.append(IN_HBM)
            continue
        space = pltpu.SMEM if value.dtype == jnp.int32 and value.ndim == 2 and value.size < 512 else pltpu.VMEM
        placed.append(pltpu.with_memory_space_constraint(value, space))
        specs.append(IN_SMEM if space is pltpu.SMEM else IN_VMEM)
    plain = [isinstance(out, jax.ShapeDtypeStruct) for out in outs]
    return pl.pallas_call(
        body,
        out_shape=list(outs),
        in_specs=specs,
        out_specs=[ANYWHERE if p else IN_VMEM for p in plain],
        input_output_aliases=aliases or {},
        scratch_shapes=list(scratch),
        compiler_params=pltpu.CompilerParams(vmem_limit_bytes=limit),
        cost_estimate=pl.CostEstimate(flops=0, bytes_accessed=0, transcendentals=0),
        name=name,
    )(*placed)


def like(value):
    return pltpu.VMEM(value.shape, value.dtype)


def normalise(residual):
    mean = jnp.mean(residual, -1, keepdims=True)
    centred = residual - mean
    rstd = lax.rsqrt(jnp.mean(centred * centred, -1, keepdims=True) + ln_eps)
    return centred * rstd, rstd


def norm_back(grad, normed, rstd, gain):
    e = grad * gain
    return (e - jnp.mean(e, -1, keepdims=True) - normed * jnp.mean(e * normed, -1, keepdims=True)) * rstd


def gelu_and_slope(pre):
    cdf = 0.5 + 0.5 * lax.erf(pre * root_half)
    return pre * cdf, cdf + pre * (jnp.exp(-0.5 * pre * pre) * root_two_pi)


def finish_section(residual, gain, shift, here, send, acts, nb, rb):
    normed, rstd = normalise(residual)
    out = (normed * gain + shift).astype(bf16)
    if send is not None:
        send[...] = out
    acts[here, :] = out
    nb[here, :] = normed
    rb[here, :] = jnp.broadcast_to(rstd, (rstd.shape[0], LANES))


def start_backward(grad, gain, slot, here, nb, rb, vg):
    normed = nb[here, :]
    vg[8 * slot : 8 * slot + 1, :] = total_rows(grad * normed)
    vg[8 * slot + 1 : 8 * slot + 2, :] = total_rows(grad)
    return norm_back(grad, normed, rb[here, 0:1], gain)


def attn_forward_kernel(stage, slot, first, bias_ref, vec_ref, x_src, w_ref, *refs):
    send, xs, acts, nb, rb, sa, sb = refs[0 if first else 6 :][:7]
    rows, width = send.shape
    here = slice(slot * rows, (slot + 1) * rows)

    @pl.when(lax.axis_index("section") == stage)
    def _():
        bias = bias_ref[here, :]
        x = x_src[...] if x_src.shape[0] == rows else x_src[here, :]
        xs[here, :] = x
        zero = jnp.zeros((1, width), f32)
        qkv_bias = jnp.concatenate([vec_ref[0:1, :].astype(f32), zero, vec_ref[1:2, :].astype(f32)], 1)
        sa[here, : 3 * width] = (dot(x, w_ref[:, : 3 * width]) + qkv_bias).astype(bf16)
        lane_head = lax.broadcasted_iota(jnp.int32, (1, QUAD), 1) // HEAD_DIM
        for j in range(width // QUAD):
            lo = j * QUAD
            q4 = sa[here, lo : lo + QUAD]
            k4 = sa[here, width + lo : width + lo + QUAD]
            v_turned = sa[here, 2 * width + lo : 2 * width + lo + QUAD].T
            turned = []
            for h in range(4):
                pick = jnp.where(lane_head == h, HEAD_DIM**-0.5, 0.0).astype(bf16)
                scores = dot_nt(k4, q4 * pick) + bias
                raised = jnp.exp(scores - jnp.max(scores, 0, keepdims=True))
                probs = (raised * (1.0 / total_rows(raised))).astype(bf16)
                at = (4 * j + h) * rows
                sb[here, at : at + rows] = probs
                turned.append(dot(v_turned[h * HEAD_DIM : (h + 1) * HEAD_DIM], probs))
            sa[here, 3 * width + lo : 3 * width + lo + QUAD] = jnp.concatenate(turned, 0).astype(bf16).T
        branch = dot(sa[here, 3 * width :], w_ref[:, 3 * width :]) + vec_ref[2:3, :].astype(f32)
        finish_section(
            x.astype(f32) + branch, vec_ref[3:4, :].astype(f32), vec_ref[4:5, :].astype(f32), here, send, acts, nb, rb
        )


def attn_backward_kernel(stage, slot, vec_ref, g_src, w_ref, nb, rb, sa, sb, *refs):
    send, gin, dr, vg = refs[3:7]
    rows, width = g_src.shape
    here = slice(slot * rows, (slot + 1) * rows)

    @pl.when(lax.axis_index("section") == stage)
    def _():
        d_resid = start_backward(g_src[...].astype(f32), vec_ref[3:4, :].astype(f32), slot, here, nb, rb, vg)
        d_branch = d_resid.astype(bf16)
        dr[here, 3 * width :] = d_branch
        d_context = dot_nt(d_branch, w_ref[:, 3 * width :]).astype(bf16)
        lane_head = lax.broadcasted_iota(jnp.int32, (1, QUAD), 1) // HEAD_DIM
        scale = HEAD_DIM**-0.5
        for j in range(width // QUAD):
            lo = j * QUAD
            q4 = sa[here, lo : lo + QUAD]
            k4 = sa[here, width + lo : width + lo + QUAD]
            v4 = sa[here, 2 * width + lo : 2 * width + lo + QUAD]
            c4 = d_context[:, lo : lo + QUAD]
            k_turned = k4.T
            d_scores, queries, contexts, turned = [], [], [], []
            for h in range(4):
                pick = jnp.where(lane_head == h, 1.0, 0.0).astype(bf16)
                at = (4 * j + h) * rows
                probs = sb[here, at : at + rows].astype(f32)
                picked = c4 * pick
                d_probs = dot_nt(v4, picked)
                weighed = probs * d_probs
                d_score = (weighed - probs * total_rows(weighed)).astype(bf16)
                d_scores.append(d_score)
                queries.append(q4 * pick)
                contexts.append(picked)
                turned.append(dot(k_turned[h * HEAD_DIM : (h + 1) * HEAD_DIM], d_score))
            at = 4 * j * rows
            d_key = dot(jnp.concatenate(d_scores, 1), jnp.concatenate(queries, 0))
            d_value = dot(sb[here, at : at + 4 * rows], jnp.concatenate(contexts, 0))
            d_query = (jnp.concatenate(turned, 0) * scale).astype(bf16).T
            dr[here, lo : lo + QUAD] = d_query
            dr[here, width + lo : width + lo + QUAD] = (d_key * scale).astype(bf16)
            dr[here, 2 * width + lo : 2 * width + lo + QUAD] = d_value.astype(bf16)
        d_input = (d_resid + dot_nt(dr[here, : 3 * width], w_ref[:, : 3 * width])).astype(bf16)
        send[...] = d_input
        gin[here, :] = d_input


def ffn_forward_body(x, here, vec_ref, b2_ref, w_ref, d_ref, sa, sb):
    width = w_ref.shape[0]
    cuts = [slice(c * width, (c + 1) * width) for c in range(4)]
    branch = x.astype(f32) + b2_ref[0:1, :].astype(f32)
    pre = dot(x, w_ref[:, cuts[0]])
    for c in range(4):
        later = dot(x, w_ref[:, cuts[c + 1]]) if c < 3 else None
        hidden, slope = gelu_and_slope(pre + vec_ref[c : c + 1, :].astype(f32))
        hidden = hidden.astype(bf16)
        sa[here, cuts[c]] = hidden
        sb[here, cuts[c]] = slope.astype(bf16)
        branch = branch + dot(hidden, d_ref[cuts[c], :])
        pre = later
    return branch


def ffn_backward_body(d_resid, here, w_ref, d_ref, sb, dr, db):
    width = w_ref.shape[0]
    cuts = [slice(c * width, (c + 1) * width) for c in range(4)]
    d_branch = d_resid.astype(bf16)
    db[here, :] = d_branch
    d_input = d_resid
    d_hidden = dot_nt(d_branch, d_ref[cuts[0], :])
    for c in range(4):
        later = dot_nt(d_branch, d_ref[cuts[c + 1], :]) if c < 3 else None
        d_pre = (d_hidden * sb[here, cuts[c]].astype(f32)).astype(bf16)
        dr[here, cuts[c]] = d_pre
        d_input = d_input + dot_nt(d_pre, w_ref[:, cuts[c]])
        d_hidden = later
    return d_input.astype(bf16)


def ffn_forward_kernel(stage, slot, vec_ref, b2_ref, x_src, w_ref, d_ref, *refs):
    send, xs, acts, nb, rb, sa, sb = refs[6:13]
    rows, width = x_src.shape
    here = slice(slot * rows, (slot + 1) * rows)

    @pl.when(lax.axis_index("section") == stage)
    def _():
        x = x_src[...]
        xs[here, :] = x
        residual = ffn_forward_body(x, here, vec_ref, b2_ref, w_ref, d_ref, sa, sb)
        finish_section(residual, vec_ref[4:5, :].astype(f32), vec_ref[5:6, :].astype(f32), here, send, acts, nb, rb)


def ffn_backward_kernel(stage, slot, vec_ref, g_src, w_ref, d_ref, nb, rb, sb, *refs):
    send, gin, dr, db, vg = refs[4:9]
    rows, width = g_src.shape
    here = slice(slot * rows, (slot + 1) * rows)

    @pl.when(lax.axis_index("section") == stage)
    def _():
        d_resid = start_backward(g_src[...].astype(f32), vec_ref[4:5, :].astype(f32), slot, here, nb, rb, vg)
        d_input = ffn_backward_body(d_resid, here, w_ref, d_ref, sb, dr, db)
        send[...] = d_input
        gin[here, :] = d_input


def ffn_both_kernel(stage, slot, first, vec_ref, b2_ref, x_src, cot, w_ref, d_ref, *refs):
    send, xs, acts, nb, rb, sa, sb, gin, dr, db, vg = refs[6 if first else 10 :][:11]
    rows, width = x_src.shape
    here = slice(slot * rows, (slot + 1) * rows)

    @pl.when(lax.axis_index("section") == stage)
    def _():
        x = x_src[...]
        xs[here, :] = x
        residual = ffn_forward_body(x, here, vec_ref, b2_ref, w_ref, d_ref, sa, sb)
        gain = vec_ref[4:5, :].astype(f32)
        finish_section(residual, gain, vec_ref[5:6, :].astype(f32), here, None, acts, nb, rb)
        d_resid = start_backward(cot[here, :].astype(f32), gain, slot, here, nb, rb, vg)
        d_input = ffn_backward_body(d_resid, here, w_ref, d_ref, sb, dr, db)
        send[...] = d_input
        gin[here, :] = d_input


LEAD = 16


def piece_kernel(vectors, down, out, vec_v, sems):
    size = out.shape[0] - LEAD
    at = pl.multiple_of(lax.axis_index("dp") * size, 16)
    copies = [
        pltpu.make_async_copy(vectors, vec_v, sems.at[0]),
        pltpu.make_async_copy(down.at[pl.ds(at, size), :], out.at[pl.ds(LEAD, size), :], sems.at[1]),
    ]
    for copy in copies:
        copy.start()
    for copy in copies:
        copy.wait()
    out[:LEAD, :] = jnp.broadcast_to(vec_v[5:6, :], (LEAD, out.shape[1]))


def setup_kernel(sections, lens, keep, vectors, x_in, cot, w_in, w_v, edge_v, vec_v, bias, lens_s, keep_v, sems):
    micro_count = lens.shape[0]
    rows = bias.shape[1]
    section = lax.axis_index("section")
    w_copy = pltpu.make_async_copy(w_in, w_v, sems.at[0])
    vec_copy = pltpu.make_async_copy(vectors, vec_v, sems.at[1])
    w_copy.start()
    vec_copy.start()

    @pl.when(section == 0)
    def _():
        pltpu.make_async_copy(x_in, edge_v, sems.at[2]).start()

    @pl.when(section == sections - 1)
    def _():
        pltpu.make_async_copy(cot, edge_v, sems.at[2]).start()

    @pl.when(section % 2 == 0)
    def _():
        lens_copy = pltpu.make_async_copy(lens, lens_s, sems.at[3])
        keep_copy = pltpu.make_async_copy(keep, keep_v, sems.at[4])
        lens_copy.start()
        keep_copy.start()
        key_pos = lax.broadcasted_iota(jnp.int32, (rows, rows), 0)
        query_pos = lax.broadcasted_iota(jnp.int32, (rows, rows), 1)
        lens_copy.wait()
        keep_copy.wait()
        for slot in range(micro_count):
            key_seg, query_seg, end = 0, 0, 0
            for k in range(lens.shape[1]):
                end = end + lens_s[slot, k]
                key_seg = key_seg + (key_pos >= end).astype(jnp.int32)
                query_seg = query_seg + (query_pos >= end).astype(jnp.int32)
            kept = jnp.broadcast_to(keep_v[slot : slot + 1, :].astype(f32), (rows, rows)).T > 0.5
            allowed = (key_seg == query_seg) & (kept | (key_pos == query_pos))
            bias[slot * rows : (slot + 1) * rows, :] = jnp.where(allowed, 0.0, neg_big)

    w_copy.wait()
    vec_copy.wait()

    @pl.when((section == 0) | (section == sections - 1))
    def _():
        pltpu.make_async_copy(x_in, edge_v, sems.at[2]).wait()


def own_down_kernel(down, out, sems):
    half = down.shape[0]

    @pl.when(lax.axis_index("section") % 2 == 1)
    def _():
        copy = pltpu.make_async_copy(down, out.at[pl.ds(half, half), :], sems.at[0])
        copy.start()
        copy.wait()


def join_down_kernel(masks, *refs):
    out = refs[-1]

    @pl.when(lax.axis_index("section") % 2 == 1)
    def _():
        me = lax.axis_index("dp")
        for block, mask in zip(refs[: len(masks)], masks):
            size = block.shape[0] - LEAD
            out[pl.ds(pl.multiple_of((me ^ mask) * size, 16), size), :] = block[LEAD:, :]


TAIL = 16


def core_half(kept):
    core = lax.axis_index("dp") % 2
    return core if kept else 1 - core


def down_grad_kernel(kept, sa, db, out):
    width = db.shape[1]

    @pl.when(lax.axis_index("section") % 2 == 1)
    def _():
        half = core_half(kept)
        for part in range(2):
            at = pl.multiple_of((2 * part + half) * width, LANES)
            out[part] = dot_tn(sa[:, pl.ds(at, width)], db[...]).astype(bf16)


def in_grad_kernel(kind, kept, micro_count, xs, sa, dr, db, vg, *refs):
    out = refs[-1]
    width = xs.shape[1]

    @pl.when(lax.axis_index("section") % 2 == kind)
    def _():
        half = core_half(kept)
        out[width:, :] = jnp.zeros((TAIL, 2 * width), bf16)
        for k in range(2):
            right = dr[:, pl.ds(pl.multiple_of((2 * half + k) * width, LANES), width)]
            left = xs[...]
            if kind == 0 and k == 1:
                left = jnp.where(half == 1, sa[:, 3 * width :], left)
            here = slice(k * width, (k + 1) * width)
            out[:width, here] = dot_tn(left, right).astype(bf16)
            if k == 0:
                other = total_rows(db[...].astype(f32)) if kind else jnp.zeros((1, width), f32)
            else:
                other = jnp.zeros((1, width), f32)
            norm = sum(vg[8 * m + k : 8 * m + k + 1, :] for m in range(micro_count))
            sums = total_rows(right.astype(f32))
            both = jnp.concatenate([sums, jnp.where(half == 0, norm, other)], 0)
            out[width : width + 2, here] = both.astype(bf16)


def bit_of(bit):
    return (lax.axis_index("dp") >> bit) % 2


def added(a, b):
    return (a.astype(f32) + b.astype(f32)).astype(bf16)


def halve(kept, got, outs, bit, tail, cut=slice(None)):
    rows = (kept.shape[-2] - tail) // 2
    mine = bit_of(bit)
    for out, half in zip(outs, (mine, 1 - mine)):
        at = pl.ds(pl.multiple_of(half * rows, 16), rows)
        if kept.ndim == 3:
            out[...] = added(kept[:, at, cut], got[:, at, cut])
        else:
            out[:rows, :] = added(kept[at, cut], got[at, cut])
    if tail:
        last = slice(2 * rows, 2 * rows + tail)
        total = added(kept[last, cut], got[last, cut])
        for out in outs:
            out[rows:, :] = total


def first_add_kernel(live, bits, tail, kept, got, *outs):
    columns = kept.shape[-1] // 2

    @pl.when(live())
    def _():
        for stream in range(2):
            cut = slice(stream * columns, (stream + 1) * columns)
            halve(kept, got, outs[2 * stream : 2 * stream + 2], bits[stream], tail, cut)


def next_add_kernel(live, bits, tail, *refs):
    ins, outs = refs[:4], refs[4:]

    @pl.when(live())
    def _():
        for stream in range(2):
            halve(*ins[2 * stream : 2 * stream + 2], outs[2 * stream : 2 * stream + 2], bits[stream], tail)


def last_down_kernel(keep_a, got_a, keep_b, got_b, up, low):
    columns = keep_a.shape[-1]

    @pl.when(on_ffn())
    def _():
        for part, out in enumerate((up, low)):
            out[:, :columns] = added(keep_a[part], got_a[part])
            out[:, columns:] = added(keep_b[part], got_b[part])


def last_in_kernel(keep_a, got_a, keep_b, got_b, handed, low, pack_a, pack_b, tails):
    rows = pack_a.shape[0]
    wide = keep_a.shape[1]
    columns = low.shape[1] // 2
    for stream, (kept, got, out) in enumerate(((keep_a, got_a, pack_a), (keep_b, got_b, pack_b))):
        cut = slice(stream * columns, (stream + 1) * columns)
        out[:, :wide] = added(kept[:rows, :], got[:rows, :])
        out[:, wide:] = jnp.where(on_ffn(), low[:, cut], handed[:, cut])
        tails[stream] = added(kept[rows:, :], got[rows:, :])


def stack_kernel(upper, lower, out):
    rows = upper.shape[0]
    out[:rows, :] = upper[...]
    out[rows:, :] = lower[...]


def on_ffn():
    return lax.axis_index("section") % 2 == 1


def everywhere():
    return True


def swap(value, mask, only=None):
    count, sections = lax.axis_size("dp"), lax.axis_size("section")
    if only is None:
        return lax.ppermute(value, "dp", [(i, i ^ mask) for i in range(count)])
    pairs = [(i * sections + s, (i ^ mask) * sections + s) for i in range(count) for s in only]
    return lax.ppermute(value, ("dp", "section"), pairs)


def cut_shape(value, tail, columns=1):
    shape = list(value.shape)
    shape[-2] = (shape[-2] - tail) // 2 + tail
    shape[-1] //= columns
    return pltpu.VMEM(tuple(shape), value.dtype)


def reduce_streams(kept, got, orders, live, only, tail):
    outs = [cut_shape(kept, tail, 2)] * 4
    parts = kernel_call(functools.partial(first_add_kernel, live, [o[0] for o in orders], tail), outs, [kept, got])
    first = parts[0]
    for step in range(len(orders[0])):
        keep_a, send_a, keep_b, send_b = parts
        ins = [keep_a, swap(send_a, 1 << orders[0][step], only), keep_b, swap(send_b, 1 << orders[1][step], only)]
        if step + 1 < len(orders[0]):
            outs = [cut_shape(keep_a, tail)] * 4
            parts = kernel_call(
                functools.partial(next_add_kernel, live, [o[step + 1] for o in orders], tail), outs, ins
            )
    return ins, first


def far_index(owner, order):
    return sum(((owner >> bit) % 2) << (len(order) - 1 - k) for k, bit in enumerate(order))


def store_kernel(orders, masks, others, width, *refs):
    count = len(others)
    blocks = refs[:count]
    total_in, total_down = refs[count + 2 : count + 4] if len(refs) > count + 5 else refs[count : count + 2]
    wide_buf, thin_buf, sems = refs[-3:]
    me = lax.axis_index("dp")
    copies = []

    def send(src, dst):
        copy = pltpu.make_async_copy(src, dst, sems.at[len(copies)])
        copy.start()
        copies.append(copy)

    for n, (block, other) in enumerate(zip(blocks, others)):
        stream = n % 2
        half = (me % 2) ^ (1 if other else 0)
        size = block.shape[0] // len(masks[stream])
        thin = block.shape[1] - width
        lane = pl.multiple_of((2 * half + stream) * width, LANES)
        for k, mask in enumerate(masks[stream]):
            here = slice(k * size, (k + 1) * size)
            row = far_index(me ^ mask, orders[stream]) * size
            wide_buf[n, here, :] = block[here, :width].astype(f32)
            send(
                wide_buf.at[n, here, :],
                total_in.at[pl.ds(pl.multiple_of(row, 16), size), pl.ds(lane, width)],
            )
            thin_buf[n, here, :] = block[here, width:].astype(f32)
            send(
                thin_buf.at[n, here, :],
                total_down.at[
                    pl.ds(pl.multiple_of(half * width + row, 16), size), stream * thin : (stream + 1) * thin
                ],
            )
    for copy in copies:
        copy.wait()


def keep_kernel(acts, gin, acts_out, gin_out, sems):
    copies = [
        pltpu.make_async_copy(acts, acts_out, sems.at[0]),
        pltpu.make_async_copy(gin, gin_out, sems.at[1]),
    ]
    for copy in copies:
        copy.start()
    for copy in copies:
        copy.wait()


def vector_kernel(own, other, b2_ref, out):
    core = lax.axis_index("dp") % 2
    own, other = own[...].astype(f32), other[...].astype(f32)
    first, second = jnp.where(core == 0, own, other), jnp.where(core == 0, other, own)
    sums = [first[0, 0:1], first[1, 0:1], second[0, 0:1], second[1, 0:1]]
    norms = [first[0, 1:2], first[1, 1:2]]

    @pl.when(on_ffn())
    def _():
        out[...] = jnp.concatenate(sums + norms, 0)

    @pl.when(jnp.logical_not(on_ffn()))
    def _():
        out[...] = jnp.concatenate([sums[0], sums[2], sums[3]] + norms + [b2_ref[0, 1:2].astype(f32)], 0)


def gate_kernel(value, after, out):
    pass


def gate(value, after):
    return pl.pallas_call(
        gate_kernel,
        out_shape=jax.ShapeDtypeStruct(value.shape, value.dtype),
        in_specs=[ANYWHERE, ANYWHERE],
        out_specs=ANYWHERE,
        input_output_aliases={0: 0},
        compiler_params=pltpu.CompilerParams(vmem_limit_bytes=1024 * 1024),
        cost_estimate=pl.CostEstimate(flops=0, bytes_accessed=0, transcendentals=0),
    )(value, after)


def local(x_in, lengths, keep_mask, w_in, w_down, vectors, cotangent):
    micro_count = lengths.shape[0]
    tokens, width = x_in.shape
    rows = tokens // micro_count
    wide = 4 * width
    count = lax.axis_size("dp")
    bits = count.bit_length() - 1
    sections = lax.axis_size("section")
    me = lax.axis_index("dp")
    ffns = tuple(range(1, sections, 2))
    down = w_down[0]
    far = list(range(1, bits))
    orders = (far, far[::-1])

    def hop(value, stage, step):
        return lax.ppermute(value, "section", [(stage, stage + step)])

    onward = [(s, s + 1) for s in range(0, sections, 2)]
    share = down.shape[0] // count
    (piece,) = kernel_call(
        piece_kernel,
        [pltpu.VMEM((LEAD + share, width), bf16)],
        [vectors[0], down],
        scratch=[pltpu.VMEM(vectors.shape[1:], bf16), pltpu.SemaphoreType.DMA((2,))],
        plain_ins=(0, 1),
        name="piece",
    )
    piece = lax.ppermute(piece, "section", onward)
    weights, edge, vec, bias = kernel_call(
        functools.partial(setup_kernel, sections),
        [
            pltpu.VMEM((width, wide), bf16),
            pltpu.VMEM((tokens, width), bf16),
            pltpu.VMEM(vectors.shape[1:], bf16),
            pltpu.VMEM((tokens, rows), f32),
        ],
        [lengths, keep_mask.reshape(micro_count, rows), vectors[0], x_in, cotangent, w_in[0]],
        scratch=[
            pltpu.SMEM(lengths.shape, jnp.int32),
            pltpu.VMEM((micro_count, rows), jnp.int32),
            pltpu.SemaphoreType.DMA((5,)),
        ],
        plain_ins=range(6),
        name="setup",
    )
    (own_down,) = kernel_call(
        own_down_kernel,
        [pltpu.VMEM((wide, width), bf16)],
        [down],
        scratch=[pltpu.SemaphoreType.DMA((1,))],
        plain_ins=(0,),
        name="own_down",
    )

    row_out = pltpu.VMEM((rows, width), bf16)
    state = [
        pltpu.VMEM((tokens, width), bf16),
        pltpu.VMEM((tokens, width), bf16),
        pltpu.VMEM((tokens, width), f32),
        pltpu.VMEM((tokens, LANES), f32),
        pltpu.VMEM((tokens, wide), bf16),
        pltpu.VMEM((tokens, HEADS * rows), bf16),
    ]
    saved, grads = None, None

    def attn_forward(stage, slot, source):
        nonlocal saved
        first = saved is None
        got = kernel_call(
            functools.partial(attn_forward_kernel, stage, slot, first),
            [row_out] + state,
            [bias, vec, source, weights] + (saved or []),
            {} if first else {4 + k: 1 + k for k in range(6)},
            name=f"attn_forward_{stage}_{slot}",
        )
        saved = list(got[1:])
        return got[0]

    def ffn_forward(stage, slot, source):
        nonlocal saved
        got = kernel_call(
            functools.partial(ffn_forward_kernel, stage, slot),
            [row_out] + state,
            [vec, b2, source, weights, down_full] + saved,
            {5 + k: 1 + k for k in range(6)},
            name=f"ffn_forward_{stage}_{slot}",
        )
        saved = list(got[1:])
        return got[0]

    def ffn_both(stage, slot, source):
        nonlocal saved, grads
        first = grads is None
        grad_state = [
            pltpu.VMEM((tokens, width), bf16),
            pltpu.VMEM((tokens, wide), bf16),
            pltpu.VMEM((tokens, width), bf16),
            pltpu.VMEM((8 * micro_count, width), f32),
        ]
        got = kernel_call(
            functools.partial(ffn_both_kernel, stage, slot, first),
            [row_out] + state + grad_state,
            [vec, b2, source, edge, weights, down_full] + saved + (grads or []),
            {6 + k: 1 + k for k in range(6 if first else 10)},
            name=f"ffn_both_{stage}_{slot}",
        )
        saved, grads = list(got[1:7]), list(got[7:])
        return got[0]

    def attn_backward(stage, slot, source):
        nonlocal grads
        xs, acts, nb, rb, sa, sb = saved
        gin, dr, db, vg = grads
        got = kernel_call(
            functools.partial(attn_backward_kernel, stage, slot),
            [row_out, like(gin), like(dr), like(vg)],
            [vec, source, weights, nb, rb, sa, sb, gin, dr, vg],
            {7 + k: 1 + k for k in range(3)},
            name=f"attn_backward_{stage}_{slot}",
        )
        grads = [got[1], got[2], db, got[3]]
        return got[0]

    def ffn_backward(stage, slot, source):
        nonlocal grads
        xs, acts, nb, rb, sa, sb = saved
        got = kernel_call(
            functools.partial(ffn_backward_kernel, stage, slot),
            [row_out] + [like(a) for a in grads],
            [vec, source, weights, down_full, nb, rb, sb] + grads,
            {7 + k: 1 + k for k in range(4)},
            name=f"ffn_backward_{stage}_{slot}",
        )
        grads = list(got[1:])
        return got[0]

    sent = [attn_forward(0, slot, edge) for slot in range(micro_count)]
    arrived = [hop(value, 0, 1) for value in sent]
    piece = gate(piece, sent[0])
    near = [piece] + [swap(piece, mask, ffns) for mask in range(2, count, 2)]
    near_masks = list(range(0, count, 2))
    masks = near_masks + [m ^ 1 for m in near_masks]
    (down_full,) = kernel_call(
        functools.partial(join_down_kernel, masks),
        [pltpu.VMEM((wide, width), bf16)],
        near + [swap(block, 1, ffns) for block in near] + [own_down],
        {len(masks): 0},
    )
    b2 = piece
    for stage in range(1, sections - 1):
        step = ffn_forward if stage % 2 else attn_forward
        arrived = [hop(step(stage, slot, arrived[slot]), stage, 1) for slot in range(micro_count)]
    last = sections - 1
    arrived = [hop(ffn_both(last, slot, arrived[slot]), last, -1) for slot in range(micro_count)]
    for stage in range(last - 1, 0, -1):
        step = ffn_backward if stage % 2 else attn_backward
        arrived = [hop(step(stage, slot, arrived[slot]), stage, -1) for slot in range(micro_count)]
    xs, acts, nb, rb, sa, sb = saved

    down_shape = pltpu.VMEM((2, width, width), bf16)
    in_shape = pltpu.VMEM((width + TAIL, 2 * width), bf16)
    (down_sent,) = kernel_call(functools.partial(down_grad_kernel, False), [down_shape], [sa, grads[2]], name="down_send")
    (down_kept,) = kernel_call(functools.partial(down_grad_kernel, True), [down_shape], [sa, grads[2]], name="down_keep")

    def in_grad(kind, kept, before=None, after=None):
        gin, dr, db, vg = grads
        ins = [xs, sa, dr, db, vg] + [value for value in (before, after) if value is not None]
        body = functools.partial(in_grad_kernel, kind, kept, micro_count)
        name = f"in_grad_{kind}_{int(kept)}"
        return kernel_call(body, [in_shape], ins, {} if before is None else {5: 0}, name=name)[0]

    in_parts = [in_grad(1, kept, after=down_kept) for kept in (False, True)]
    down_ins, first = reduce_streams(down_kept, swap(down_sent, 1, ffns), orders, on_ffn, ffns, 0)

    for slot in range(micro_count):
        attn_backward(0, slot, gate(arrived[slot], in_parts[1]) if slot == 0 else arrived[slot])
    in_sent, in_kept = in_grad(0, False, in_parts[0]), in_grad(0, True, in_parts[1])
    gin = grads[0]

    in_ins, _ = reduce_streams(in_kept, swap(in_sent, 1), orders, everywhere, None, TAIL)
    share_rows = down_kept.shape[1] // (count // 2)
    up, low = kernel_call(
        last_down_kernel, [pltpu.VMEM((share_rows, width), bf16)] * 2, down_ins, name="last_down"
    )
    backward = [(s, s - 1) for s in ffns]
    handed = lax.ppermute(up, "section", backward)
    share_rows = in_ins[0].shape[0] - TAIL
    packed = pltpu.VMEM((share_rows, width + width // 2), bf16)
    pack_a, pack_b, tails = kernel_call(
        last_in_kernel,
        [packed, packed, pltpu.VMEM((2, TAIL, width), bf16)],
        in_ins + [handed, low],
        name="last_in",
    )

    other_tails = swap(tails, 1)
    b2_part = lax.ppermute(jnp.where(me % 2 == 0, other_tails, tails), "section", backward)
    (total_vec,) = kernel_call(vector_kernel, [pltpu.VMEM((6, width), f32)], [tails, other_tails, b2_part], name="vectors")

    blocks, masks = [pack_a, pack_b], [[0], [0]]
    for step in range(len(far)):
        bit = [orders[stream][len(far) - 1 - step] for stream in range(2)]
        got = [swap(blocks[stream], 1 << bit[stream]) for stream in range(2)]
        got_masks = [[m ^ (1 << bit[stream]) for m in masks[stream]] for stream in range(2)]
        if step + 1 < len(far):
            for stream in range(2):
                rows_now, cols_now = got[stream].shape
                (blocks[stream],) = kernel_call(
                    stack_kernel, [pltpu.VMEM((2 * rows_now, cols_now), bf16)], [blocks[stream], got[stream]]
                )
                masks[stream] = masks[stream] + got_masks[stream]
    outs = [jax.ShapeDtypeStruct((width, wide), f32), jax.ShapeDtypeStruct((2 * width, width), f32)]

    def store(blocks, masks, others, totals, name):
        shape = (len(blocks), blocks[0].shape[0])
        return kernel_call(
            functools.partial(store_kernel, orders, masks, others, width),
            outs,
            blocks + totals,
            {len(blocks) + k: k for k in range(len(totals))},
            scratch=[
                pltpu.VMEM(shape + (width,), f32),
                pltpu.VMEM(shape + (width // 2,), f32),
                pltpu.SemaphoreType.DMA((2 * len(blocks) * len(masks[0]),)),
            ],
            name=name,
            plain_ins=range(len(blocks), len(blocks) + len(totals)),
            limit=STORE_LIMIT,
        )

    totals = list(store(blocks + [swap(b, 1) for b in blocks], masks, (False, False, True, True), [], "store_early"))
    totals = list(store(got, got_masks, (False, False), totals, "store_own"))
    total_in, total_down = store([swap(b, 1) for b in got], got_masks, (True, True), totals, "store_other")
    acts, gin = kernel_call(
        keep_kernel,
        [jax.ShapeDtypeStruct(a.shape, a.dtype) for a in (acts, gin)],
        [acts, gin],
        scratch=[pltpu.SemaphoreType.DMA((2,))],
        name="keep",
    )
    return (acts[None], gin[None], total_in[None], total_down[None], total_vec[None])


def solution(mesh):
    placed = (
        P("dp", None),
        P("dp", None),
        P("dp"),
        P("section", None, None),
        P("section", None, None),
        P("section", None, None),
        P("dp", None),
    )
    return jax.shard_map(
        local,
        mesh=mesh,
        in_specs=placed,
        out_specs=(
            P("section", "dp", None),
            P("section", "dp", None),
            P("section", None, None),
            P("section", None, None),
            P("section", None, None),
        ),
        check_vma=False,
    )
```

```python
import functools

import jax
import jax.numpy as jnp
from jax import lax
from jax.experimental import pallas as pl
from jax.experimental.pallas import tpu as pltpu
from jax.sharding import PartitionSpec as P

HEADS = 12
HEAD_DIM = 64
QUAD = 4 * HEAD_DIM
LANES = 128

ln_eps = 1e-05
neg_big = -1000000000.0
root_half = 0.7071067811865476
root_two_pi = 0.3989422804014327

f32 = jnp.float32
bf16 = jnp.bfloat16

IN_VMEM = pl.BlockSpec(memory_space=pltpu.VMEM)
IN_HBM = pl.BlockSpec(memory_space=pltpu.HBM)
IN_SMEM = pl.BlockSpec(memory_space=pltpu.SMEM)
ANYWHERE = pl.BlockSpec(memory_space=pl.ANY)
VMEM_LIMIT = 4 * 1024 * 1024
STORE_LIMIT = 16 * 1024 * 1024
STORE_COST = dict(store_early=8_000_000_000, store_own=60_000_000_000, store_other=0)


def dot(a, b):
    return jnp.dot(a, b, preferred_element_type=f32)


def dot_nt(a, b):
    return lax.dot_general(a, b, (((1,), (1,)), ((), ())), preferred_element_type=f32)


def dot_tn(a, b):
    return lax.dot_general(a, b, (((0,), (0,)), ((), ())), preferred_element_type=f32)


def total_rows(value):
    return jnp.sum(value, 0, keepdims=True)


def kernel_call(body, outs, ins, aliases=None, scratch=(), name=None, plain_ins=(), limit=VMEM_LIMIT, flops=0):
    specs, placed = [], []
    for n, value in enumerate(ins):
        if n in plain_ins:
            placed.append(pltpu.with_memory_space_constraint(value, pltpu.HBM))
            specs.append(IN_HBM)
            continue
        space = pltpu.SMEM if value.dtype == jnp.int32 and value.ndim == 2 and value.size < 512 else pltpu.VMEM
        placed.append(pltpu.with_memory_space_constraint(value, space))
        specs.append(IN_SMEM if space is pltpu.SMEM else IN_VMEM)
    plain = [isinstance(out, jax.ShapeDtypeStruct) for out in outs]
    return pl.pallas_call(
        body,
        out_shape=list(outs),
        in_specs=specs,
        out_specs=[ANYWHERE if p else IN_VMEM for p in plain],
        input_output_aliases=aliases or {},
        scratch_shapes=list(scratch),
        compiler_params=pltpu.CompilerParams(vmem_limit_bytes=limit),
        cost_estimate=pl.CostEstimate(flops=flops, bytes_accessed=0, transcendentals=0),
        name=name,
    )(*placed)


def like(value):
    return pltpu.VMEM(value.shape, value.dtype)


def normalise(residual):
    mean = jnp.mean(residual, -1, keepdims=True)
    centred = residual - mean
    rstd = lax.rsqrt(jnp.mean(centred * centred, -1, keepdims=True) + ln_eps)
    return centred * rstd, rstd


def norm_back(grad, normed, rstd, gain):
    e = grad * gain
    return (e - jnp.mean(e, -1, keepdims=True) - normed * jnp.mean(e * normed, -1, keepdims=True)) * rstd


def gelu_and_slope(pre):
    cdf = 0.5 + 0.5 * lax.erf(pre * root_half)
    return pre * cdf, cdf + pre * (jnp.exp(-0.5 * pre * pre) * root_two_pi)


def finish_section(residual, gain, shift, here, send, acts, nb, rb):
    normed, rstd = normalise(residual)
    out = (normed * gain + shift).astype(bf16)
    if send is not None:
        send[...] = out
    acts[here, :] = out
    nb[here, :] = normed
    rb[here, :] = jnp.broadcast_to(rstd, (rstd.shape[0], LANES))


def start_backward(grad, gain, slot, here, nb, rb, vg):
    normed = nb[here, :]
    vg[8 * slot : 8 * slot + 1, :] = total_rows(grad * normed)
    vg[8 * slot + 1 : 8 * slot + 2, :] = total_rows(grad)
    return norm_back(grad, normed, rb[here, 0:1], gain)


def attn_forward_kernel(stage, slot, first, bias_ref, vec_ref, x_src, w_ref, *refs):
    send, xs, acts, nb, rb, sa, sb = refs[0 if first else 6 :][:7]
    rows, width = send.shape
    here = slice(slot * rows, (slot + 1) * rows)

    @pl.when(lax.axis_index("section") == stage)
    def _():
        bias = bias_ref[here, :]
        x = x_src[...] if x_src.shape[0] == rows else x_src[here, :]
        xs[here, :] = x
        zero = jnp.zeros((1, width), f32)
        qkv_bias = jnp.concatenate([vec_ref[0:1, :].astype(f32), zero, vec_ref[1:2, :].astype(f32)], 1)
        sa[here, : 3 * width] = (dot(x, w_ref[:, : 3 * width]) + qkv_bias).astype(bf16)
        lane_head = lax.broadcasted_iota(jnp.int32, (1, QUAD), 1) // HEAD_DIM
        for j in range(width // QUAD):
            lo = j * QUAD
            q4 = sa[here, lo : lo + QUAD]
            k4 = sa[here, width + lo : width + lo + QUAD]
            v_turned = sa[here, 2 * width + lo : 2 * width + lo + QUAD].T
            turned = []
            for h in range(4):
                pick = jnp.where(lane_head == h, HEAD_DIM**-0.5, 0.0).astype(bf16)
                scores = dot_nt(k4, q4 * pick) + bias
                raised = jnp.exp(scores - jnp.max(scores, 0, keepdims=True))
                probs = (raised * (1.0 / total_rows(raised))).astype(bf16)
                at = (4 * j + h) * rows
                sb[here, at : at + rows] = probs
                turned.append(dot(v_turned[h * HEAD_DIM : (h + 1) * HEAD_DIM], probs))
            sa[here, 3 * width + lo : 3 * width + lo + QUAD] = jnp.concatenate(turned, 0).astype(bf16).T
        branch = dot(sa[here, 3 * width :], w_ref[:, 3 * width :]) + vec_ref[2:3, :].astype(f32)
        finish_section(
            x.astype(f32) + branch, vec_ref[3:4, :].astype(f32), vec_ref[4:5, :].astype(f32), here, send, acts, nb, rb
        )


def attn_backward_kernel(stage, slot, vec_ref, g_src, w_ref, nb, rb, sa, sb, *refs):
    send, gin, dr, vg = refs[3:7]
    rows, width = g_src.shape
    here = slice(slot * rows, (slot + 1) * rows)

    @pl.when(lax.axis_index("section") == stage)
    def _():
        d_resid = start_backward(g_src[...].astype(f32), vec_ref[3:4, :].astype(f32), slot, here, nb, rb, vg)
        d_branch = d_resid.astype(bf16)
        dr[here, 3 * width :] = d_branch
        d_context = dot_nt(d_branch, w_ref[:, 3 * width :]).astype(bf16)
        lane_head = lax.broadcasted_iota(jnp.int32, (1, QUAD), 1) // HEAD_DIM
        scale = HEAD_DIM**-0.5
        for j in range(width // QUAD):
            lo = j * QUAD
            q4 = sa[here, lo : lo + QUAD]
            k4 = sa[here, width + lo : width + lo + QUAD]
            v4 = sa[here, 2 * width + lo : 2 * width + lo + QUAD]
            c4 = d_context[:, lo : lo + QUAD]
            k_turned = k4.T
            d_scores, queries, contexts, turned = [], [], [], []
            for h in range(4):
                pick = jnp.where(lane_head == h, 1.0, 0.0).astype(bf16)
                at = (4 * j + h) * rows
                probs = sb[here, at : at + rows].astype(f32)
                picked = c4 * pick
                d_probs = dot_nt(v4, picked)
                weighed = probs * d_probs
                d_score = (weighed - probs * total_rows(weighed)).astype(bf16)
                d_scores.append(d_score)
                queries.append(q4 * pick)
                contexts.append(picked)
                turned.append(dot(k_turned[h * HEAD_DIM : (h + 1) * HEAD_DIM], d_score))
            at = 4 * j * rows
            d_key = dot(jnp.concatenate(d_scores, 1), jnp.concatenate(queries, 0))
            d_value = dot(sb[here, at : at + 4 * rows], jnp.concatenate(contexts, 0))
            d_query = (jnp.concatenate(turned, 0) * scale).astype(bf16).T
            dr[here, lo : lo + QUAD] = d_query
            dr[here, width + lo : width + lo + QUAD] = (d_key * scale).astype(bf16)
            dr[here, 2 * width + lo : 2 * width + lo + QUAD] = d_value.astype(bf16)
        d_input = (d_resid + dot_nt(dr[here, : 3 * width], w_ref[:, : 3 * width])).astype(bf16)
        send[...] = d_input
        gin[here, :] = d_input


def ffn_forward_body(x, here, vec_ref, b2_ref, w_ref, d_ref, sa, sb):
    width = w_ref.shape[0]
    cuts = [slice(c * width, (c + 1) * width) for c in range(4)]
    branch = x.astype(f32) + b2_ref[0:1, :].astype(f32)
    pre = dot(x, w_ref[:, cuts[0]])
    for c in range(4):
        later = dot(x, w_ref[:, cuts[c + 1]]) if c < 3 else None
        hidden, slope = gelu_and_slope(pre + vec_ref[c : c + 1, :].astype(f32))
        hidden = hidden.astype(bf16)
        sa[here, cuts[c]] = hidden
        sb[here, cuts[c]] = slope.astype(bf16)
        branch = branch + dot(hidden, d_ref[cuts[c], :])
        pre = later
    return branch


def ffn_backward_body(d_resid, here, w_ref, d_ref, sb, dr, db):
    width = w_ref.shape[0]
    cuts = [slice(c * width, (c + 1) * width) for c in range(4)]
    d_branch = d_resid.astype(bf16)
    db[here, :] = d_branch
    d_input = d_resid
    d_hidden = dot_nt(d_branch, d_ref[cuts[0], :])
    for c in range(4):
        later = dot_nt(d_branch, d_ref[cuts[c + 1], :]) if c < 3 else None
        d_pre = (d_hidden * sb[here, cuts[c]].astype(f32)).astype(bf16)
        dr[here, cuts[c]] = d_pre
        d_input = d_input + dot_nt(d_pre, w_ref[:, cuts[c]])
        d_hidden = later
    return d_input.astype(bf16)


def ffn_forward_kernel(stage, slot, vec_ref, b2_ref, x_src, w_ref, d_ref, *refs):
    send, xs, acts, nb, rb, sa, sb = refs[6:13]
    rows, width = x_src.shape
    here = slice(slot * rows, (slot + 1) * rows)

    @pl.when(lax.axis_index("section") == stage)
    def _():
        x = x_src[...]
        xs[here, :] = x
        residual = ffn_forward_body(x, here, vec_ref, b2_ref, w_ref, d_ref, sa, sb)
        finish_section(residual, vec_ref[4:5, :].astype(f32), vec_ref[5:6, :].astype(f32), here, send, acts, nb, rb)


def ffn_backward_kernel(stage, slot, vec_ref, g_src, w_ref, d_ref, nb, rb, sb, *refs):
    send, gin, dr, db, vg = refs[4:9]
    rows, width = g_src.shape
    here = slice(slot * rows, (slot + 1) * rows)

    @pl.when(lax.axis_index("section") == stage)
    def _():
        d_resid = start_backward(g_src[...].astype(f32), vec_ref[4:5, :].astype(f32), slot, here, nb, rb, vg)
        d_input = ffn_backward_body(d_resid, here, w_ref, d_ref, sb, dr, db)
        send[...] = d_input
        gin[here, :] = d_input


def ffn_both_kernel(stage, slot, first, vec_ref, b2_ref, x_src, cot, w_ref, d_ref, *refs):
    send, xs, acts, nb, rb, sa, sb, gin, dr, db, vg = refs[6 if first else 10 :][:11]
    rows, width = x_src.shape
    here = slice(slot * rows, (slot + 1) * rows)

    @pl.when(lax.axis_index("section") == stage)
    def _():
        x = x_src[...]
        xs[here, :] = x
        residual = ffn_forward_body(x, here, vec_ref, b2_ref, w_ref, d_ref, sa, sb)
        gain = vec_ref[4:5, :].astype(f32)
        finish_section(residual, gain, vec_ref[5:6, :].astype(f32), here, None, acts, nb, rb)
        d_resid = start_backward(cot[here, :].astype(f32), gain, slot, here, nb, rb, vg)
        d_input = ffn_backward_body(d_resid, here, w_ref, d_ref, sb, dr, db)
        send[...] = d_input
        gin[here, :] = d_input


LEAD = 16


def quarter(spread_out, other_half, other_core):
    me = lax.axis_index("dp")
    core = (me % 2) ^ other_core
    if not spread_out:
        return core
    return 2 * (((me >> 1) ^ (me >> 2)) % 2 ^ other_half) + core


def piece_kernel(spread_out, vectors, down, first, second, vec_v, sems):
    size = second.shape[0]
    at = pl.multiple_of(quarter(spread_out, 0, 0) * 2 * size, 16)
    copies = [
        pltpu.make_async_copy(vectors, vec_v, sems.at[0]),
        pltpu.make_async_copy(down.at[pl.ds(at, size), :], first.at[pl.ds(LEAD, size), :], sems.at[1]),
        pltpu.make_async_copy(down.at[pl.ds(at + size, size), :], second, sems.at[2]),
    ]
    for copy in copies:
        copy.start()
    for copy in copies:
        copy.wait()
    first[:LEAD, :] = jnp.broadcast_to(vec_v[5:6, :], (LEAD, first.shape[1]))


def setup_kernel(sections, lens, keep, vectors, x_in, cot, w_in, w_v, edge_v, vec_v, bias, lens_s, keep_v, sems):
    micro_count = lens.shape[0]
    rows = bias.shape[1]
    section = lax.axis_index("section")
    w_copy = pltpu.make_async_copy(w_in, w_v, sems.at[0])
    vec_copy = pltpu.make_async_copy(vectors, vec_v, sems.at[1])
    w_copy.start()
    vec_copy.start()

    @pl.when(section == 0)
    def _():
        pltpu.make_async_copy(x_in, edge_v, sems.at[2]).start()

    @pl.when(section == sections - 1)
    def _():
        pltpu.make_async_copy(cot, edge_v, sems.at[2]).start()

    @pl.when(section % 2 == 0)
    def _():
        lens_copy = pltpu.make_async_copy(lens, lens_s, sems.at[3])
        keep_copy = pltpu.make_async_copy(keep, keep_v, sems.at[4])
        lens_copy.start()
        keep_copy.start()
        key_pos = lax.broadcasted_iota(jnp.int32, (rows, rows), 0)
        query_pos = lax.broadcasted_iota(jnp.int32, (rows, rows), 1)
        lens_copy.wait()
        keep_copy.wait()
        for slot in range(micro_count):
            key_seg, query_seg, end = 0, 0, 0
            for k in range(lens.shape[1]):
                end = end + lens_s[slot, k]
                key_seg = key_seg + (key_pos >= end).astype(jnp.int32)
                query_seg = query_seg + (query_pos >= end).astype(jnp.int32)
            kept = jnp.broadcast_to(keep_v[slot : slot + 1, :].astype(f32), (rows, rows)).T > 0.5
            allowed = (key_seg == query_seg) & (kept | (key_pos == query_pos))
            bias[slot * rows : (slot + 1) * rows, :] = jnp.where(allowed, 0.0, neg_big)

    w_copy.wait()
    vec_copy.wait()

    @pl.when((section == 0) | (section == sections - 1))
    def _():
        pltpu.make_async_copy(x_in, edge_v, sems.at[2]).wait()


def own_down_kernel(down, out, token, sems):
    half = down.shape[0]
    token[...] = jnp.zeros_like(token)

    @pl.when(lax.axis_index("section") % 2 == 1)
    def _():
        copy = pltpu.make_async_copy(down, out.at[pl.ds(half, half), :], sems.at[0])
        copy.start()
        copy.wait()


def join_down_kernel(spread_out, places, *refs):
    out = refs[-1]

    @pl.when(lax.axis_index("section") % 2 == 1)
    def _():
        for block, (other_half, other_core, part, parts, lead) in zip(refs[: len(places)], places):
            size = block.shape[0] - lead
            at = quarter(spread_out, other_half, other_core) * parts + part
            out[pl.ds(pl.multiple_of(at * size, 16), size), :] = block[lead:, :]


TAIL = 16


def core_half(kept):
    core = lax.axis_index("dp") % 2
    return core if kept else 1 - core


def down_grad_kernel(kept, sa, db, out):
    width = db.shape[1]

    @pl.when(lax.axis_index("section") % 2 == 1)
    def _():
        half = core_half(kept)
        for part in range(2):
            at = pl.multiple_of((2 * part + half) * width, LANES)
            out[part] = dot_tn(sa[:, pl.ds(at, width)], db[...]).astype(bf16)


def in_grad_kernel(kind, kept, micro_count, xs, sa, dr, db, vg, *refs):
    out = refs[-1]
    width = xs.shape[1]

    @pl.when(lax.axis_index("section") % 2 == kind)
    def _():
        half = core_half(kept)
        out[width:, :] = jnp.zeros((TAIL, 2 * width), bf16)
        for k in range(2):
            right = dr[:, pl.ds(pl.multiple_of((2 * half + k) * width, LANES), width)]
            left = xs[...]
            if kind == 0 and k == 1:
                left = jnp.where(half == 1, sa[:, 3 * width :], left)
            here = slice(k * width, (k + 1) * width)
            out[:width, here] = dot_tn(left, right).astype(bf16)
            if k == 0:
                other = total_rows(db[...].astype(f32)) if kind else jnp.zeros((1, width), f32)
            else:
                other = jnp.zeros((1, width), f32)
            norm = sum(vg[8 * m + k : 8 * m + k + 1, :] for m in range(micro_count))
            sums = total_rows(right.astype(f32))
            both = jnp.concatenate([sums, jnp.where(half == 0, norm, other)], 0)
            out[width : width + 2, here] = both.astype(bf16)


def bit_of(bit):
    return (lax.axis_index("dp") >> bit) % 2


def added(a, b):
    return (a.astype(f32) + b.astype(f32)).astype(bf16)


def halve(kept, got, outs, bit, tail, cut=slice(None)):
    rows = (kept.shape[-2] - tail) // 2
    mine = bit_of(bit)
    for out, half in zip(outs, (mine, 1 - mine)):
        at = pl.ds(pl.multiple_of(half * rows, 16), rows)
        if kept.ndim == 3:
            out[...] = added(kept[:, at, cut], got[:, at, cut])
        else:
            out[:rows, :] = added(kept[at, cut], got[at, cut])
    if tail:
        last = slice(2 * rows, 2 * rows + tail)
        total = added(kept[last, cut], got[last, cut])
        for out in outs:
            out[rows:, :] = total


def first_add_kernel(live, bits, tail, kept, got, *outs):
    columns = kept.shape[-1] // 2

    @pl.when(live())
    def _():
        for stream in range(2):
            cut = slice(stream * columns, (stream + 1) * columns)
            halve(kept, got, outs[2 * stream : 2 * stream + 2], bits[stream], tail, cut)


def next_add_kernel(live, bits, tail, *refs):
    ins, outs = refs[:4], refs[4:]

    @pl.when(live())
    def _():
        for stream in range(2):
            halve(*ins[2 * stream : 2 * stream + 2], outs[2 * stream : 2 * stream + 2], bits[stream], tail)


def last_down_kernel(keep_a, got_a, keep_b, got_b, up, low):
    columns = keep_a.shape[-1]

    @pl.when(on_ffn())
    def _():
        for part, out in enumerate((up, low)):
            out[:, :columns] = added(keep_a[part], got_a[part])
            out[:, columns:] = added(keep_b[part], got_b[part])


def last_in_kernel(keep_a, got_a, keep_b, got_b, handed, low, pack_a, pack_b, tails):
    rows = pack_a.shape[0]
    wide = keep_a.shape[1]
    columns = low.shape[1] // 2
    for stream, (kept, got, out) in enumerate(((keep_a, got_a, pack_a), (keep_b, got_b, pack_b))):
        cut = slice(stream * columns, (stream + 1) * columns)
        out[:, :wide] = added(kept[:rows, :], got[:rows, :])
        out[:, wide:] = jnp.where(on_ffn(), low[:, cut], handed[:, cut])
        tails[stream] = added(kept[rows:, :], got[rows:, :])


def stack_kernel(upper, lower, out):
    rows = upper.shape[0]
    out[:rows, :] = upper[...]
    out[rows:, :] = lower[...]


def on_ffn():
    return lax.axis_index("section") % 2 == 1


def everywhere():
    return True


def swap(value, mask, only=None):
    count, sections = lax.axis_size("dp"), lax.axis_size("section")
    if only is None:
        return lax.ppermute(value, "dp", [(i, i ^ mask) for i in range(count)])
    pairs = [(i * sections + s, (i ^ mask) * sections + s) for i in range(count) for s in only]
    return lax.ppermute(value, ("dp", "section"), pairs)


def cut_shape(value, tail, columns=1):
    shape = list(value.shape)
    shape[-2] = (shape[-2] - tail) // 2 + tail
    shape[-1] //= columns
    return pltpu.VMEM(tuple(shape), value.dtype)


def reduce_streams(kept, got, orders, live, only, tail):
    outs = [cut_shape(kept, tail, 2)] * 4
    parts = kernel_call(functools.partial(first_add_kernel, live, [o[0] for o in orders], tail), outs, [kept, got])
    first = parts[0]
    for step in range(len(orders[0])):
        keep_a, send_a, keep_b, send_b = parts
        ins = [keep_a, swap(send_a, 1 << orders[0][step], only), keep_b, swap(send_b, 1 << orders[1][step], only)]
        if step + 1 < len(orders[0]):
            outs = [cut_shape(keep_a, tail)] * 4
            parts = kernel_call(
                functools.partial(next_add_kernel, live, [o[step + 1] for o in orders], tail), outs, ins
            )
    return ins, first


def far_index(owner, order):
    return sum(((owner >> bit) % 2) << (len(order) - 1 - k) for k, bit in enumerate(order))


def store_kernel(orders, masks, others, width, *refs):
    count = len(others)
    blocks = refs[:count]
    total_in, total_down, token, wide_buf, thin_buf, sems = refs[-6:]
    token[...] = jnp.zeros_like(token)
    me = lax.axis_index("dp")
    copies = []

    def send(src, dst):
        copy = pltpu.make_async_copy(src, dst, sems.at[len(copies)])
        copy.start()
        copies.append(copy)

    for n, (block, other) in enumerate(zip(blocks, others)):
        stream = n % 2
        half = (me % 2) ^ (1 if other else 0)
        size = block.shape[0] // len(masks[stream])
        thin = block.shape[1] - width
        lane = pl.multiple_of((2 * half + stream) * width, LANES)
        for k, mask in enumerate(masks[stream]):
            here = slice(k * size, (k + 1) * size)
            row = far_index(me ^ mask, orders[stream]) * size
            wide_buf[n, here, :] = block[here, :width].astype(f32)
            send(
                wide_buf.at[n, here, :],
                total_in.at[pl.ds(pl.multiple_of(row, 16), size), pl.ds(lane, width)],
            )
            thin_buf[n, here, :] = block[here, width:].astype(f32)
            send(
                thin_buf.at[n, here, :],
                total_down.at[
                    pl.ds(pl.multiple_of(half * width + row, 16), size), stream * thin : (stream + 1) * thin
                ],
            )
    for copy in copies:
        copy.wait()


def keep_kernel(acts, gin, acts_out, gin_out, sems):
    copies = [
        pltpu.make_async_copy(acts, acts_out, sems.at[0]),
        pltpu.make_async_copy(gin, gin_out, sems.at[1]),
    ]
    for copy in copies:
        copy.start()
    for copy in copies:
        copy.wait()


def vector_kernel(own, other, b2_ref, out):
    core = lax.axis_index("dp") % 2
    own, other = own[...].astype(f32), other[...].astype(f32)
    first, second = jnp.where(core == 0, own, other), jnp.where(core == 0, other, own)
    sums = [first[0, 0:1], first[1, 0:1], second[0, 0:1], second[1, 0:1]]
    norms = [first[0, 1:2], first[1, 1:2]]

    @pl.when(on_ffn())
    def _():
        out[...] = jnp.concatenate(sums + norms, 0)

    @pl.when(jnp.logical_not(on_ffn()))
    def _():
        out[...] = jnp.concatenate([sums[0], sums[2], sums[3]] + norms + [b2_ref[0, 1:2].astype(f32)], 0)


def gate_kernel(*refs):
    pass


def gate(value, *after):
    return pl.pallas_call(
        gate_kernel,
        out_shape=jax.ShapeDtypeStruct(value.shape, value.dtype),
        in_specs=[ANYWHERE] * (1 + len(after)),
        out_specs=ANYWHERE,
        input_output_aliases={0: 0},
        compiler_params=pltpu.CompilerParams(vmem_limit_bytes=1024 * 1024),
        cost_estimate=pl.CostEstimate(flops=0, bytes_accessed=0, transcendentals=0),
        name="gate",
    )(value, *after)


def local(x_in, lengths, keep_mask, w_in, w_down, vectors, cotangent):
    micro_count = lengths.shape[0]
    tokens, width = x_in.shape
    rows = tokens // micro_count
    wide = 4 * width
    count = lax.axis_size("dp")
    bits = count.bit_length() - 1
    sections = lax.axis_size("section")
    me = lax.axis_index("dp")
    ffns = tuple(range(1, sections, 2))
    down = w_down[0]
    far = list(range(1, bits))
    orders = (far, far[::-1])

    def hop(value, stage, step):
        return lax.ppermute(value, "section", [(stage, stage + step)])

    onward = [(s, s + 1) for s in range(0, sections, 2)]
    spread_out = len(far) == 2
    share = down.shape[0] // (8 if spread_out else 4)
    pieces = kernel_call(
        functools.partial(piece_kernel, spread_out),
        [pltpu.VMEM((LEAD + share, width), bf16), pltpu.VMEM((share, width), bf16)],
        [vectors[0], down],
        scratch=[pltpu.VMEM(vectors.shape[1:], bf16), pltpu.SemaphoreType.DMA((3,))],
        plain_ins=(0, 1),
        name="piece",
    )
    pieces = [lax.ppermute(piece, "section", onward) for piece in pieces]
    weights, edge, vec, bias = kernel_call(
        functools.partial(setup_kernel, sections),
        [
            pltpu.VMEM((width, wide), bf16),
            pltpu.VMEM((tokens, width), bf16),
            pltpu.VMEM(vectors.shape[1:], bf16),
            pltpu.VMEM((tokens, rows), f32),
        ],
        [lengths, keep_mask.reshape(micro_count, rows), vectors[0], x_in, cotangent, w_in[0]],
        scratch=[
            pltpu.SMEM(lengths.shape, jnp.int32),
            pltpu.VMEM((micro_count, rows), jnp.int32),
            pltpu.SemaphoreType.DMA((5,)),
        ],
        plain_ins=range(6),
        name="setup",
    )
    own_down, down_token = kernel_call(
        own_down_kernel,
        [pltpu.VMEM((wide, width), bf16), pltpu.VMEM((8, LANES), f32)],
        [down],
        scratch=[pltpu.SemaphoreType.DMA((1,))],
        plain_ins=(0,),
        name="own_down",
    )

    row_out = pltpu.VMEM((rows, width), bf16)
    state = [
        pltpu.VMEM((tokens, width), bf16),
        pltpu.VMEM((tokens, width), bf16),
        pltpu.VMEM((tokens, width), f32),
        pltpu.VMEM((tokens, LANES), f32),
        pltpu.VMEM((tokens, wide), bf16),
        pltpu.VMEM((tokens, HEADS * rows), bf16),
    ]
    saved, grads = None, None

    def attn_forward(stage, slot, source):
        nonlocal saved
        first = saved is None
        got = kernel_call(
            functools.partial(attn_forward_kernel, stage, slot, first),
            [row_out] + state,
            [bias, vec, source, weights] + (saved or []),
            {} if first else {4 + k: 1 + k for k in range(6)},
            name=f"attn_forward_{stage}_{slot}",
        )
        saved = list(got[1:])
        return got[0]

    def ffn_forward(stage, slot, source):
        nonlocal saved
        got = kernel_call(
            functools.partial(ffn_forward_kernel, stage, slot),
            [row_out] + state,
            [vec, b2, source, weights, down_full] + saved,
            {5 + k: 1 + k for k in range(6)},
            name=f"ffn_forward_{stage}_{slot}",
        )
        saved = list(got[1:])
        return got[0]

    def ffn_both(stage, slot, source):
        nonlocal saved, grads
        first = grads is None
        grad_state = [
            pltpu.VMEM((tokens, width), bf16),
            pltpu.VMEM((tokens, wide), bf16),
            pltpu.VMEM((tokens, width), bf16),
            pltpu.VMEM((8 * micro_count, width), f32),
        ]
        got = kernel_call(
            functools.partial(ffn_both_kernel, stage, slot, first),
            [row_out] + state + grad_state,
            [vec, b2, source, edge, weights, down_full] + saved + (grads or []),
            {6 + k: 1 + k for k in range(6 if first else 10)},
            name=f"ffn_both_{stage}_{slot}",
        )
        saved, grads = list(got[1:7]), list(got[7:])
        return got[0]

    def attn_backward(stage, slot, source):
        nonlocal grads
        xs, acts, nb, rb, sa, sb = saved
        gin, dr, db, vg = grads
        got = kernel_call(
            functools.partial(attn_backward_kernel, stage, slot),
            [row_out, like(gin), like(dr), like(vg)],
            [vec, source, weights, nb, rb, sa, sb, gin, dr, vg],
            {7 + k: 1 + k for k in range(3)},
            name=f"attn_backward_{stage}_{slot}",
        )
        grads = [got[1], got[2], db, got[3]]
        return got[0]

    def ffn_backward(stage, slot, source):
        nonlocal grads
        xs, acts, nb, rb, sa, sb = saved
        got = kernel_call(
            functools.partial(ffn_backward_kernel, stage, slot),
            [row_out] + [like(a) for a in grads],
            [vec, source, weights, down_full, nb, rb, sb] + grads,
            {7 + k: 1 + k for k in range(4)},
            name=f"ffn_backward_{stage}_{slot}",
        )
        grads = list(got[1:])
        return got[0]

    sent = [attn_forward(0, slot, edge) for slot in range(micro_count)]
    arrived = [hop(value, 0, 1) for value in sent]
    blocks = [gate(piece, sent[0], down_token) for piece in pieces]
    b2 = blocks[0]
    places = [(0, 0, part, 2, 0 if part else LEAD) for part in range(2)]
    if spread_out:
        blocks += [swap(block, 1 << bit, ffns) for block, bit in zip(blocks, far)]
        places += [(1, 0, part, 2, 0 if part else LEAD) for part in range(2)]
    others = []
    for n, block in enumerate(blocks):
        last = n + 1 == len(blocks)
        others.append(swap(gate(block, arrived[0], *others) if last else block, 1, ffns))
    places += [(half, 1, part, parts, lead) for half, _, part, parts, lead in places]
    (down_full,) = kernel_call(
        functools.partial(join_down_kernel, spread_out, places),
        [pltpu.VMEM((wide, width), bf16)],
        blocks + others + [own_down],
        {len(places): 0},
        name="join",
    )
    for stage in range(1, sections - 1):
        step = ffn_forward if stage % 2 else attn_forward
        arrived = [hop(step(stage, slot, arrived[slot]), stage, 1) for slot in range(micro_count)]
    last = sections - 1
    arrived = [hop(ffn_both(last, slot, arrived[slot]), last, -1) for slot in range(micro_count)]
    for stage in range(last - 1, 0, -1):
        step = ffn_backward if stage % 2 else attn_backward
        arrived = [hop(step(stage, slot, arrived[slot]), stage, -1) for slot in range(micro_count)]
    xs, acts, nb, rb, sa, sb = saved

    down_shape = pltpu.VMEM((2, width, width), bf16)
    in_shape = pltpu.VMEM((width + TAIL, 2 * width), bf16)
    (down_sent,) = kernel_call(functools.partial(down_grad_kernel, False), [down_shape], [sa, grads[2]], name="down_send")
    (down_kept,) = kernel_call(functools.partial(down_grad_kernel, True), [down_shape], [sa, grads[2]], name="down_keep")

    def in_grad(kind, kept, before=None, after=None):
        gin, dr, db, vg = grads
        ins = [xs, sa, dr, db, vg] + [value for value in (before, after) if value is not None]
        body = functools.partial(in_grad_kernel, kind, kept, micro_count)
        name = f"in_grad_{kind}_{int(kept)}"
        return kernel_call(body, [in_shape], ins, {} if before is None else {5: 0}, name=name)[0]

    in_parts = [in_grad(1, kept, after=down_kept) for kept in (False, True)]
    down_ins, first = reduce_streams(down_kept, swap(down_sent, 1, ffns), orders, on_ffn, ffns, 0)

    for slot in range(micro_count):
        attn_backward(0, slot, gate(arrived[slot], in_parts[1]) if slot == 0 else arrived[slot])
    in_sent, in_kept = in_grad(0, False, in_parts[0]), in_grad(0, True, in_parts[1])
    gin = grads[0]

    in_ins, _ = reduce_streams(in_kept, swap(in_sent, 1), orders, everywhere, None, TAIL)
    share_rows = down_kept.shape[1] // (count // 2)
    up, low = kernel_call(
        last_down_kernel, [pltpu.VMEM((share_rows, width), bf16)] * 2, down_ins, name="last_down"
    )
    backward = [(s, s - 1) for s in ffns]
    handed = lax.ppermute(up, "section", backward)
    share_rows = in_ins[0].shape[0] - TAIL
    packed = pltpu.VMEM((share_rows, width + width // 2), bf16)
    pack_a, pack_b, tails = kernel_call(
        last_in_kernel,
        [packed, packed, pltpu.VMEM((2, TAIL, width), bf16)],
        in_ins + [handed, low],
        name="last_in",
    )

    other_tails = swap(tails, 1)
    b2_part = lax.ppermute(jnp.where(me % 2 == 0, other_tails, tails), "section", backward)
    (total_vec,) = kernel_call(vector_kernel, [pltpu.VMEM((6, width), f32)], [tails, other_tails, b2_part], name="vectors")

    blocks, masks = [pack_a, pack_b], [[0], [0]]
    for step in range(len(far)):
        bit = [orders[stream][len(far) - 1 - step] for stream in range(2)]
        got = [swap(blocks[stream], 1 << bit[stream]) for stream in range(2)]
        got_masks = [[m ^ (1 << bit[stream]) for m in masks[stream]] for stream in range(2)]
        if step + 1 < len(far):
            for stream in range(2):
                rows_now, cols_now = got[stream].shape
                (blocks[stream],) = kernel_call(
                    stack_kernel, [pltpu.VMEM((2 * rows_now, cols_now), bf16)], [blocks[stream], got[stream]]
                )
                masks[stream] = masks[stream] + got_masks[stream]
    outs = [
        jax.ShapeDtypeStruct((width, wide), f32),
        jax.ShapeDtypeStruct((2 * width, width), f32),
        pltpu.VMEM((8, LANES), f32),
    ]

    def store(blocks, masks, others, totals, name):
        shape = (len(blocks), blocks[0].shape[0])
        return kernel_call(
            functools.partial(store_kernel, orders, masks, others, width),
            outs,
            blocks + totals,
            {len(blocks) + k: k for k in range(len(totals))},
            scratch=[
                pltpu.VMEM(shape + (width,), f32),
                pltpu.VMEM(shape + (width // 2,), f32),
                pltpu.SemaphoreType.DMA((2 * len(blocks) * len(masks[0]),)),
            ],
            name=name,
            plain_ins=range(len(blocks), len(blocks) + len(totals)),
            limit=STORE_LIMIT,
            flops=STORE_COST[name],
        )

    acts, gin = kernel_call(
        keep_kernel,
        [jax.ShapeDtypeStruct(a.shape, a.dtype) for a in (acts, gin)],
        [acts, gin],
        scratch=[pltpu.SemaphoreType.DMA((2,))],
        name="keep",
    )
    early = blocks + [swap(b, 1) for b in blocks]
    *totals, token = store(early, masks, (False, False, True, True), [], "store_early")
    got = [gate(g, token) for g in got]
    *totals, token = store(got, got_masks, (False, False), totals, "store_own")
    total_in, total_down, _ = store([swap(g, 1) for g in got], got_masks, (True, True), totals, "store_other")
    return (acts[None], gin[None], total_in[None], total_down[None], total_vec[None])


def solution(mesh):
    placed = (
        P("dp", None),
        P("dp", None),
        P("dp"),
        P("section", None, None),
        P("section", None, None),
        P("section", None, None),
        P("dp", None),
    )
    return jax.shard_map(
        local,
        mesh=mesh,
        in_specs=placed,
        out_specs=(
            P("section", "dp", None),
            P("section", "dp", None),
            P("section", None, None),
            P("section", None, None),
            P("section", None, None),
        ),
        check_vma=False,
    )
```

```python
import functools

import jax
import jax.numpy as jnp
from jax import lax
from jax.experimental import pallas as pl
from jax.experimental.pallas import tpu as pltpu
from jax.sharding import PartitionSpec as P

HEADS = 12
HEAD_DIM = 64
QUAD = 4 * HEAD_DIM
LANES = 128

ln_eps = 1e-05
neg_big = -1000000000.0
root_half = 0.7071067811865476
root_two_pi = 0.3989422804014327

f32 = jnp.float32
bf16 = jnp.bfloat16

IN_VMEM = pl.BlockSpec(memory_space=pltpu.VMEM)
IN_HBM = pl.BlockSpec(memory_space=pltpu.HBM)
IN_SMEM = pl.BlockSpec(memory_space=pltpu.SMEM)
ANYWHERE = pl.BlockSpec(memory_space=pl.ANY)
VMEM_LIMIT = 4 * 1024 * 1024
STORE_LIMIT = 16 * 1024 * 1024
STORE_COST = dict(store_early=8_000_000_000, store_own=60_000_000_000, store_other=0)


def dot(a, b):
    return jnp.dot(a, b, preferred_element_type=f32)


def dot_nt(a, b):
    return lax.dot_general(a, b, (((1,), (1,)), ((), ())), preferred_element_type=f32)


def dot_tn(a, b):
    return lax.dot_general(a, b, (((0,), (0,)), ((), ())), preferred_element_type=f32)


def total_rows(value):
    return jnp.sum(value, 0, keepdims=True)


def kernel_call(body, outs, ins, aliases=None, scratch=(), name=None, plain_ins=(), limit=VMEM_LIMIT, flops=0):
    specs, placed = [], []
    for n, value in enumerate(ins):
        if n in plain_ins:
            placed.append(pltpu.with_memory_space_constraint(value, pltpu.HBM))
            specs.append(IN_HBM)
            continue
        space = pltpu.SMEM if value.dtype == jnp.int32 and value.ndim == 2 and value.size < 512 else pltpu.VMEM
        placed.append(pltpu.with_memory_space_constraint(value, space))
        specs.append(IN_SMEM if space is pltpu.SMEM else IN_VMEM)
    plain = [isinstance(out, jax.ShapeDtypeStruct) for out in outs]
    return pl.pallas_call(
        body,
        out_shape=list(outs),
        in_specs=specs,
        out_specs=[ANYWHERE if p else IN_VMEM for p in plain],
        input_output_aliases=aliases or {},
        scratch_shapes=list(scratch),
        compiler_params=pltpu.CompilerParams(vmem_limit_bytes=limit),
        cost_estimate=pl.CostEstimate(flops=flops, bytes_accessed=0, transcendentals=0),
        name=name,
    )(*placed)


def like(value):
    return pltpu.VMEM(value.shape, value.dtype)


def normalise(residual):
    mean = jnp.mean(residual, -1, keepdims=True)
    centred = residual - mean
    rstd = lax.rsqrt(jnp.mean(centred * centred, -1, keepdims=True) + ln_eps)
    return centred * rstd, rstd


def norm_back(grad, normed, rstd, gain):
    e = grad * gain
    return (e - jnp.mean(e, -1, keepdims=True) - normed * jnp.mean(e * normed, -1, keepdims=True)) * rstd


def gelu_and_slope(pre):
    cdf = 0.5 + 0.5 * lax.erf(pre * root_half)
    return pre * cdf, cdf + pre * (jnp.exp(-0.5 * pre * pre) * root_two_pi)


def finish_section(residual, gain, shift, here, send, acts, nb, rb):
    normed, rstd = normalise(residual)
    out = (normed * gain + shift).astype(bf16)
    if send is not None:
        send[...] = out
    acts[here, :] = out
    nb[here, :] = normed
    rb[here, :] = jnp.broadcast_to(rstd, (rstd.shape[0], LANES))


def start_backward(grad, gain, slot, here, nb, rb, vg):
    normed = nb[here, :]
    vg[8 * slot : 8 * slot + 1, :] = total_rows(grad * normed)
    vg[8 * slot + 1 : 8 * slot + 2, :] = total_rows(grad)
    return norm_back(grad, normed, rb[here, 0:1], gain)


def attn_forward_kernel(stage, slot, first, bias_ref, vec_ref, x_src, w_ref, *refs):
    send, xs, acts, nb, rb, sa, sb = refs[0 if first else 6 :][:7]
    rows, width = send.shape
    here = slice(slot * rows, (slot + 1) * rows)

    @pl.when(lax.axis_index("section") == stage)
    def _():
        bias = bias_ref[here, :]
        x = x_src[...] if x_src.shape[0] == rows else x_src[here, :]
        xs[here, :] = x
        zero = jnp.zeros((1, width), f32)
        qkv_bias = jnp.concatenate([vec_ref[0:1, :].astype(f32), zero, vec_ref[1:2, :].astype(f32)], 1)
        sa[here, : 3 * width] = (dot(x, w_ref[:, : 3 * width]) + qkv_bias).astype(bf16)
        lane_head = lax.broadcasted_iota(jnp.int32, (1, QUAD), 1) // HEAD_DIM
        for j in range(width // QUAD):
            lo = j * QUAD
            q4 = sa[here, lo : lo + QUAD]
            k4 = sa[here, width + lo : width + lo + QUAD]
            v_turned = sa[here, 2 * width + lo : 2 * width + lo + QUAD].T
            turned = []
            for h in range(4):
                pick = jnp.where(lane_head == h, HEAD_DIM**-0.5, 0.0).astype(bf16)
                scores = dot_nt(k4, q4 * pick) + bias
                raised = jnp.exp(scores - jnp.max(scores, 0, keepdims=True))
                probs = (raised * (1.0 / total_rows(raised))).astype(bf16)
                at = (4 * j + h) * rows
                sb[here, at : at + rows] = probs
                turned.append(dot(v_turned[h * HEAD_DIM : (h + 1) * HEAD_DIM], probs))
            sa[here, 3 * width + lo : 3 * width + lo + QUAD] = jnp.concatenate(turned, 0).astype(bf16).T
        branch = dot(sa[here, 3 * width :], w_ref[:, 3 * width :]) + vec_ref[2:3, :].astype(f32)
        finish_section(
            x.astype(f32) + branch, vec_ref[3:4, :].astype(f32), vec_ref[4:5, :].astype(f32), here, send, acts, nb, rb
        )


def attn_backward_kernel(stage, slot, vec_ref, g_src, w_ref, nb, rb, sa, sb, *refs):
    send, gin, dr, vg = refs[3:7]
    rows, width = g_src.shape
    here = slice(slot * rows, (slot + 1) * rows)

    @pl.when(lax.axis_index("section") == stage)
    def _():
        d_resid = start_backward(g_src[...].astype(f32), vec_ref[3:4, :].astype(f32), slot, here, nb, rb, vg)
        d_branch = d_resid.astype(bf16)
        dr[here, 3 * width :] = d_branch
        d_context = dot_nt(d_branch, w_ref[:, 3 * width :]).astype(bf16)
        lane_head = lax.broadcasted_iota(jnp.int32, (1, QUAD), 1) // HEAD_DIM
        scale = HEAD_DIM**-0.5
        for j in range(width // QUAD):
            lo = j * QUAD
            q4 = sa[here, lo : lo + QUAD]
            k4 = sa[here, width + lo : width + lo + QUAD]
            v4 = sa[here, 2 * width + lo : 2 * width + lo + QUAD]
            c4 = d_context[:, lo : lo + QUAD]
            k_turned = k4.T
            d_scores, queries, contexts, turned = [], [], [], []
            for h in range(4):
                pick = jnp.where(lane_head == h, 1.0, 0.0).astype(bf16)
                at = (4 * j + h) * rows
                probs = sb[here, at : at + rows].astype(f32)
                picked = c4 * pick
                d_probs = dot_nt(v4, picked)
                weighed = probs * d_probs
                d_score = (weighed - probs * total_rows(weighed)).astype(bf16)
                d_scores.append(d_score)
                queries.append(q4 * pick)
                contexts.append(picked)
                turned.append(dot(k_turned[h * HEAD_DIM : (h + 1) * HEAD_DIM], d_score))
            at = 4 * j * rows
            d_key = dot(jnp.concatenate(d_scores, 1), jnp.concatenate(queries, 0))
            d_value = dot(sb[here, at : at + 4 * rows], jnp.concatenate(contexts, 0))
            d_query = (jnp.concatenate(turned, 0) * scale).astype(bf16).T
            dr[here, lo : lo + QUAD] = d_query
            dr[here, width + lo : width + lo + QUAD] = (d_key * scale).astype(bf16)
            dr[here, 2 * width + lo : 2 * width + lo + QUAD] = d_value.astype(bf16)
        d_input = (d_resid + dot_nt(dr[here, : 3 * width], w_ref[:, : 3 * width])).astype(bf16)
        send[...] = d_input
        gin[here, :] = d_input


def ffn_forward_body(x, here, vec_ref, b2_ref, w_ref, d_ref, sa, sb):
    width = w_ref.shape[0]
    cuts = [slice(c * width, (c + 1) * width) for c in range(4)]
    branch = x.astype(f32) + b2_ref[0:1, :].astype(f32)
    pre = dot(x, w_ref[:, cuts[0]])
    for c in range(4):
        later = dot(x, w_ref[:, cuts[c + 1]]) if c < 3 else None
        hidden, slope = gelu_and_slope(pre + vec_ref[c : c + 1, :].astype(f32))
        hidden = hidden.astype(bf16)
        sa[here, cuts[c]] = hidden
        sb[here, cuts[c]] = slope.astype(bf16)
        branch = branch + dot(hidden, d_ref[cuts[c], :])
        pre = later
    return branch


def ffn_backward_body(d_resid, here, w_ref, d_ref, sb, dr, db):
    width = w_ref.shape[0]
    cuts = [slice(c * width, (c + 1) * width) for c in range(4)]
    d_branch = d_resid.astype(bf16)
    db[here, :] = d_branch
    d_input = d_resid
    d_hidden = dot_nt(d_branch, d_ref[cuts[0], :])
    for c in range(4):
        later = dot_nt(d_branch, d_ref[cuts[c + 1], :]) if c < 3 else None
        d_pre = (d_hidden * sb[here, cuts[c]].astype(f32)).astype(bf16)
        dr[here, cuts[c]] = d_pre
        d_input = d_input + dot_nt(d_pre, w_ref[:, cuts[c]])
        d_hidden = later
    return d_input.astype(bf16)


def ffn_forward_kernel(stage, slot, vec_ref, b2_ref, x_src, w_ref, d_ref, *refs):
    send, xs, acts, nb, rb, sa, sb = refs[6:13]
    rows, width = x_src.shape
    here = slice(slot * rows, (slot + 1) * rows)

    @pl.when(lax.axis_index("section") == stage)
    def _():
        x = x_src[...]
        xs[here, :] = x
        residual = ffn_forward_body(x, here, vec_ref, b2_ref, w_ref, d_ref, sa, sb)
        finish_section(residual, vec_ref[4:5, :].astype(f32), vec_ref[5:6, :].astype(f32), here, send, acts, nb, rb)


def ffn_backward_kernel(stage, slot, vec_ref, g_src, w_ref, d_ref, nb, rb, sb, *refs):
    send, gin, dr, db, vg = refs[4:9]
    rows, width = g_src.shape
    here = slice(slot * rows, (slot + 1) * rows)

    @pl.when(lax.axis_index("section") == stage)
    def _():
        d_resid = start_backward(g_src[...].astype(f32), vec_ref[4:5, :].astype(f32), slot, here, nb, rb, vg)
        d_input = ffn_backward_body(d_resid, here, w_ref, d_ref, sb, dr, db)
        send[...] = d_input
        gin[here, :] = d_input


def ffn_both_kernel(stage, slot, first, vec_ref, b2_ref, x_src, cot, w_ref, d_ref, *refs):
    send, xs, acts, nb, rb, sa, sb, gin, dr, db, vg = refs[6 if first else 10 :][:11]
    rows, width = x_src.shape
    here = slice(slot * rows, (slot + 1) * rows)

    @pl.when(lax.axis_index("section") == stage)
    def _():
        x = x_src[...]
        xs[here, :] = x
        residual = ffn_forward_body(x, here, vec_ref, b2_ref, w_ref, d_ref, sa, sb)
        gain = vec_ref[4:5, :].astype(f32)
        finish_section(residual, gain, vec_ref[5:6, :].astype(f32), here, None, acts, nb, rb)
        d_resid = start_backward(cot[here, :].astype(f32), gain, slot, here, nb, rb, vg)
        d_input = ffn_backward_body(d_resid, here, w_ref, d_ref, sb, dr, db)
        send[...] = d_input
        gin[here, :] = d_input


LEAD = 16


def quarter(spread_out, other_half, other_core):
    me = lax.axis_index("dp")
    core = (me % 2) ^ other_core
    if not spread_out:
        return core
    return 2 * (((me >> 1) ^ (me >> 2)) % 2 ^ other_half) + core


def piece_kernel(spread_out, vectors, down, first, second, vec_v, sems):
    size = second.shape[0]
    at = pl.multiple_of(quarter(spread_out, 0, 0) * 2 * size, 16)
    copies = [
        pltpu.make_async_copy(vectors, vec_v, sems.at[0]),
        pltpu.make_async_copy(down.at[pl.ds(at, size), :], first.at[pl.ds(LEAD, size), :], sems.at[1]),
        pltpu.make_async_copy(down.at[pl.ds(at + size, size), :], second, sems.at[2]),
    ]
    for copy in copies:
        copy.start()
    for copy in copies:
        copy.wait()
    first[:LEAD, :] = jnp.broadcast_to(vec_v[5:6, :], (LEAD, first.shape[1]))


def setup_kernel(sections, lens, keep, vectors, x_in, cot, w_in, w_v, edge_v, vec_v, bias, lens_s, keep_v, sems):
    micro_count = lens.shape[0]
    rows = bias.shape[1]
    section = lax.axis_index("section")
    w_copy = pltpu.make_async_copy(w_in, w_v, sems.at[0])
    vec_copy = pltpu.make_async_copy(vectors, vec_v, sems.at[1])
    w_copy.start()
    vec_copy.start()

    @pl.when(section == 0)
    def _():
        pltpu.make_async_copy(x_in, edge_v, sems.at[2]).start()

    @pl.when(section == sections - 1)
    def _():
        pltpu.make_async_copy(cot, edge_v, sems.at[2]).start()

    @pl.when(section % 2 == 0)
    def _():
        lens_copy = pltpu.make_async_copy(lens, lens_s, sems.at[3])
        keep_copy = pltpu.make_async_copy(keep, keep_v, sems.at[4])
        lens_copy.start()
        keep_copy.start()
        key_pos = lax.broadcasted_iota(jnp.int32, (rows, rows), 0)
        query_pos = lax.broadcasted_iota(jnp.int32, (rows, rows), 1)
        lens_copy.wait()
        keep_copy.wait()
        for slot in range(micro_count):
            key_seg, query_seg, end = 0, 0, 0
            for k in range(lens.shape[1]):
                end = end + lens_s[slot, k]
                key_seg = key_seg + (key_pos >= end).astype(jnp.int32)
                query_seg = query_seg + (query_pos >= end).astype(jnp.int32)
            kept = jnp.broadcast_to(keep_v[slot : slot + 1, :].astype(f32), (rows, rows)).T > 0.5
            allowed = (key_seg == query_seg) & (kept | (key_pos == query_pos))
            bias[slot * rows : (slot + 1) * rows, :] = jnp.where(allowed, 0.0, neg_big)

    w_copy.wait()
    vec_copy.wait()

    @pl.when((section == 0) | (section == sections - 1))
    def _():
        pltpu.make_async_copy(x_in, edge_v, sems.at[2]).wait()


def own_down_kernel(down, out, token, sems):
    half = down.shape[0]
    token[...] = jnp.zeros_like(token)

    @pl.when(lax.axis_index("section") % 2 == 1)
    def _():
        copy = pltpu.make_async_copy(down, out.at[pl.ds(half, half), :], sems.at[0])
        copy.start()
        copy.wait()


def join_down_kernel(spread_out, places, *refs):
    out = refs[-1]

    @pl.when(lax.axis_index("section") % 2 == 1)
    def _():
        for block, (other_half, other_core, part, parts, lead) in zip(refs[: len(places)], places):
            size = block.shape[0] - lead
            at = quarter(spread_out, other_half, other_core) * parts + part
            out[pl.ds(pl.multiple_of(at * size, 16), size), :] = block[lead:, :]


TAIL = 16


def core_half(kept):
    core = lax.axis_index("dp") % 2
    return core if kept else 1 - core


def down_grad_kernel(kept, sa, db, out):
    width = db.shape[1]

    @pl.when(lax.axis_index("section") % 2 == 1)
    def _():
        half = core_half(kept)
        for part in range(2):
            at = pl.multiple_of((2 * part + half) * width, LANES)
            out[part] = dot_tn(sa[:, pl.ds(at, width)], db[...]).astype(bf16)


def in_grad_kernel(kind, kept, micro_count, xs, sa, dr, db, vg, *refs):
    out = refs[-1]
    width = xs.shape[1]

    @pl.when(lax.axis_index("section") % 2 == kind)
    def _():
        half = core_half(kept)
        out[width:, :] = jnp.zeros((TAIL, 2 * width), bf16)
        for k in range(2):
            right = dr[:, pl.ds(pl.multiple_of((2 * half + k) * width, LANES), width)]
            left = xs[...]
            if kind == 0 and k == 1:
                left = jnp.where(half == 1, sa[:, 3 * width :], left)
            here = slice(k * width, (k + 1) * width)
            out[:width, here] = dot_tn(left, right).astype(bf16)
            if k == 0:
                other = total_rows(db[...].astype(f32)) if kind else jnp.zeros((1, width), f32)
            else:
                other = jnp.zeros((1, width), f32)
            norm = sum(vg[8 * m + k : 8 * m + k + 1, :] for m in range(micro_count))
            sums = total_rows(right.astype(f32))
            both = jnp.concatenate([sums, jnp.where(half == 0, norm, other)], 0)
            out[width : width + 2, here] = both.astype(bf16)


def bit_of(bit):
    return (lax.axis_index("dp") >> bit) % 2


def added(a, b):
    return (a.astype(f32) + b.astype(f32)).astype(bf16)


def halve(kept, got, outs, bit, tail, cut=slice(None)):
    rows = (kept.shape[-2] - tail) // 2
    mine = bit_of(bit)
    for out, half in zip(outs, (mine, 1 - mine)):
        at = pl.ds(pl.multiple_of(half * rows, 16), rows)
        if kept.ndim == 3:
            out[...] = added(kept[:, at, cut], got[:, at, cut])
        else:
            out[:rows, :] = added(kept[at, cut], got[at, cut])
    if tail:
        last = slice(2 * rows, 2 * rows + tail)
        total = added(kept[last, cut], got[last, cut])
        for out in outs:
            out[rows:, :] = total


def first_add_kernel(live, bits, tail, kept, got, *outs):
    columns = kept.shape[-1] // 2

    @pl.when(live())
    def _():
        for stream in range(2):
            cut = slice(stream * columns, (stream + 1) * columns)
            halve(kept, got, outs[2 * stream : 2 * stream + 2], bits[stream], tail, cut)


def next_add_kernel(live, bits, tail, *refs):
    ins, outs = refs[:4], refs[4:]

    @pl.when(live())
    def _():
        for stream in range(2):
            halve(*ins[2 * stream : 2 * stream + 2], outs[2 * stream : 2 * stream + 2], bits[stream], tail)


def last_down_kernel(keep_a, got_a, keep_b, got_b, up, low):
    columns = keep_a.shape[-1]

    @pl.when(on_ffn())
    def _():
        for part, out in enumerate((up, low)):
            out[:, :columns] = added(keep_a[part], got_a[part])
            out[:, columns:] = added(keep_b[part], got_b[part])


def last_in_kernel(keep_a, got_a, keep_b, got_b, handed, low, pack_a, pack_b, tails):
    rows = pack_a.shape[0]
    wide = keep_a.shape[1]
    columns = low.shape[1] // 2
    for stream, (kept, got, out) in enumerate(((keep_a, got_a, pack_a), (keep_b, got_b, pack_b))):
        cut = slice(stream * columns, (stream + 1) * columns)
        out[:, :wide] = added(kept[:rows, :], got[:rows, :])
        out[:, wide:] = jnp.where(on_ffn(), low[:, cut], handed[:, cut])
        tails[stream] = added(kept[rows:, :], got[rows:, :])


def stack_kernel(upper, lower, out):
    rows = upper.shape[0]
    out[:rows, :] = upper[...]
    out[rows:, :] = lower[...]


def on_ffn():
    return lax.axis_index("section") % 2 == 1


def everywhere():
    return True


def swap(value, mask, only=None):
    count, sections = lax.axis_size("dp"), lax.axis_size("section")
    if only is None:
        return lax.ppermute(value, "dp", [(i, i ^ mask) for i in range(count)])
    pairs = [(i * sections + s, (i ^ mask) * sections + s) for i in range(count) for s in only]
    return lax.ppermute(value, ("dp", "section"), pairs)


def cut_shape(value, tail, columns=1):
    shape = list(value.shape)
    shape[-2] = (shape[-2] - tail) // 2 + tail
    shape[-1] //= columns
    return pltpu.VMEM(tuple(shape), value.dtype)


def reduce_streams(kept, got, orders, live, only, tail):
    outs = [cut_shape(kept, tail, 2)] * 4
    parts = kernel_call(functools.partial(first_add_kernel, live, [o[0] for o in orders], tail), outs, [kept, got])
    first = parts[0]
    for step in range(len(orders[0])):
        keep_a, send_a, keep_b, send_b = parts
        ins = [keep_a, swap(send_a, 1 << orders[0][step], only), keep_b, swap(send_b, 1 << orders[1][step], only)]
        if step + 1 < len(orders[0]):
            outs = [cut_shape(keep_a, tail)] * 4
            parts = kernel_call(
                functools.partial(next_add_kernel, live, [o[step + 1] for o in orders], tail), outs, ins
            )
    return ins, first


def far_index(owner, order):
    return sum(((owner >> bit) % 2) << (len(order) - 1 - k) for k, bit in enumerate(order))


def store_kernel(orders, masks, others, width, *refs):
    count = len(others)
    blocks = refs[:count]
    total_in, total_down, token, wide_buf, thin_buf, sems = refs[-6:]
    token[...] = jnp.zeros_like(token)
    me = lax.axis_index("dp")
    copies = []

    def send(src, dst):
        copy = pltpu.make_async_copy(src, dst, sems.at[len(copies)])
        copy.start()
        copies.append(copy)

    for n, (block, other) in enumerate(zip(blocks, others)):
        stream = n % 2
        half = (me % 2) ^ (1 if other else 0)
        size = block.shape[0] // len(masks[stream])
        thin = block.shape[1] - width
        lane = pl.multiple_of((2 * half + stream) * width, LANES)
        for k, mask in enumerate(masks[stream]):
            here = slice(k * size, (k + 1) * size)
            row = far_index(me ^ mask, orders[stream]) * size
            wide_buf[n, here, :] = block[here, :width].astype(f32)
            send(
                wide_buf.at[n, here, :],
                total_in.at[pl.ds(pl.multiple_of(row, 16), size), pl.ds(lane, width)],
            )
            thin_buf[n, here, :] = block[here, width:].astype(f32)
            send(
                thin_buf.at[n, here, :],
                total_down.at[
                    pl.ds(pl.multiple_of(half * width + row, 16), size), stream * thin : (stream + 1) * thin
                ],
            )
    for copy in copies:
        copy.wait()


def keep_kernel(acts, gin, acts_out, gin_out, sems):
    copies = [
        pltpu.make_async_copy(acts, acts_out, sems.at[0]),
        pltpu.make_async_copy(gin, gin_out, sems.at[1]),
    ]
    for copy in copies:
        copy.start()
    for copy in copies:
        copy.wait()


def vector_kernel(own, other, b2_ref, out):
    core = lax.axis_index("dp") % 2
    own, other = own[...].astype(f32), other[...].astype(f32)
    first, second = jnp.where(core == 0, own, other), jnp.where(core == 0, other, own)
    sums = [first[0, 0:1], first[1, 0:1], second[0, 0:1], second[1, 0:1]]
    norms = [first[0, 1:2], first[1, 1:2]]

    @pl.when(on_ffn())
    def _():
        out[...] = jnp.concatenate(sums + norms, 0)

    @pl.when(jnp.logical_not(on_ffn()))
    def _():
        out[...] = jnp.concatenate([sums[0], sums[2], sums[3]] + norms + [b2_ref[0, 1:2].astype(f32)], 0)


def gate_kernel(*refs):
    pass


def gate(value, *after):
    return pl.pallas_call(
        gate_kernel,
        out_shape=jax.ShapeDtypeStruct(value.shape, value.dtype),
        in_specs=[ANYWHERE] * (1 + len(after)),
        out_specs=ANYWHERE,
        input_output_aliases={0: 0},
        compiler_params=pltpu.CompilerParams(vmem_limit_bytes=1024 * 1024),
        cost_estimate=pl.CostEstimate(flops=0, bytes_accessed=0, transcendentals=0),
        name="gate",
    )(value, *after)


def local(x_in, lengths, keep_mask, w_in, w_down, vectors, cotangent):
    micro_count = lengths.shape[0]
    tokens, width = x_in.shape
    rows = tokens // micro_count
    wide = 4 * width
    count = lax.axis_size("dp")
    bits = count.bit_length() - 1
    sections = lax.axis_size("section")
    me = lax.axis_index("dp")
    ffns = tuple(range(1, sections, 2))
    down = w_down[0]
    far = list(range(1, bits))
    orders = (far, far[::-1])

    def hop(value, stage, step):
        return lax.ppermute(value, "section", [(stage, stage + step)])

    onward = [(s, s + 1) for s in range(0, sections, 2)]
    spread_out = len(far) == 2
    share = down.shape[0] // (8 if spread_out else 4)
    pieces = kernel_call(
        functools.partial(piece_kernel, spread_out),
        [pltpu.VMEM((LEAD + share, width), bf16), pltpu.VMEM((share, width), bf16)],
        [vectors[0], down],
        scratch=[pltpu.VMEM(vectors.shape[1:], bf16), pltpu.SemaphoreType.DMA((3,))],
        plain_ins=(0, 1),
        name="piece",
    )
    pieces = [lax.ppermute(piece, "section", onward) for piece in pieces]
    weights, edge, vec, bias = kernel_call(
        functools.partial(setup_kernel, sections),
        [
            pltpu.VMEM((width, wide), bf16),
            pltpu.VMEM((tokens, width), bf16),
            pltpu.VMEM(vectors.shape[1:], bf16),
            pltpu.VMEM((tokens, rows), f32),
        ],
        [lengths, keep_mask.reshape(micro_count, rows), vectors[0], x_in, cotangent, w_in[0]],
        scratch=[
            pltpu.SMEM(lengths.shape, jnp.int32),
            pltpu.VMEM((micro_count, rows), jnp.int32),
            pltpu.SemaphoreType.DMA((5,)),
        ],
        plain_ins=range(6),
        name="setup",
    )
    own_down, down_token = kernel_call(
        own_down_kernel,
        [pltpu.VMEM((wide, width), bf16), pltpu.VMEM((8, LANES), f32)],
        [down],
        scratch=[pltpu.SemaphoreType.DMA((1,))],
        plain_ins=(0,),
        name="own_down",
    )

    row_out = pltpu.VMEM((rows, width), bf16)
    state = [
        pltpu.VMEM((tokens, width), bf16),
        pltpu.VMEM((tokens, width), bf16),
        pltpu.VMEM((tokens, width), f32),
        pltpu.VMEM((tokens, LANES), f32),
        pltpu.VMEM((tokens, wide), bf16),
        pltpu.VMEM((tokens, HEADS * rows), bf16),
    ]
    saved, grads = None, None

    def attn_forward(stage, slot, source):
        nonlocal saved
        first = saved is None
        got = kernel_call(
            functools.partial(attn_forward_kernel, stage, slot, first),
            [row_out] + state,
            [bias, vec, source, weights] + (saved or []),
            {} if first else {4 + k: 1 + k for k in range(6)},
            name=f"attn_forward_{stage}_{slot}",
        )
        saved = list(got[1:])
        return got[0]

    def ffn_forward(stage, slot, source):
        nonlocal saved
        got = kernel_call(
            functools.partial(ffn_forward_kernel, stage, slot),
            [row_out] + state,
            [vec, b2, source, weights, down_full] + saved,
            {5 + k: 1 + k for k in range(6)},
            name=f"ffn_forward_{stage}_{slot}",
        )
        saved = list(got[1:])
        return got[0]

    def ffn_both(stage, slot, source):
        nonlocal saved, grads
        first = grads is None
        grad_state = [
            pltpu.VMEM((tokens, width), bf16),
            pltpu.VMEM((tokens, wide), bf16),
            pltpu.VMEM((tokens, width), bf16),
            pltpu.VMEM((8 * micro_count, width), f32),
        ]
        got = kernel_call(
            functools.partial(ffn_both_kernel, stage, slot, first),
            [row_out] + state + grad_state,
            [vec, b2, source, edge, weights, down_full] + saved + (grads or []),
            {6 + k: 1 + k for k in range(6 if first else 10)},
            name=f"ffn_both_{stage}_{slot}",
        )
        saved, grads = list(got[1:7]), list(got[7:])
        return got[0]

    def attn_backward(stage, slot, source):
        nonlocal grads
        xs, acts, nb, rb, sa, sb = saved
        gin, dr, db, vg = grads
        got = kernel_call(
            functools.partial(attn_backward_kernel, stage, slot),
            [row_out, like(gin), like(dr), like(vg)],
            [vec, source, weights, nb, rb, sa, sb, gin, dr, vg],
            {7 + k: 1 + k for k in range(3)},
            name=f"attn_backward_{stage}_{slot}",
        )
        grads = [got[1], got[2], db, got[3]]
        return got[0]

    def ffn_backward(stage, slot, source):
        nonlocal grads
        xs, acts, nb, rb, sa, sb = saved
        got = kernel_call(
            functools.partial(ffn_backward_kernel, stage, slot),
            [row_out] + [like(a) for a in grads],
            [vec, source, weights, down_full, nb, rb, sb] + grads,
            {7 + k: 1 + k for k in range(4)},
            name=f"ffn_backward_{stage}_{slot}",
        )
        grads = list(got[1:])
        return got[0]

    sent = [attn_forward(0, slot, edge) for slot in range(micro_count)]
    arrived = [hop(value, 0, 1) for value in sent]
    blocks = [gate(piece, sent[0], down_token) for piece in pieces]
    b2 = blocks[0]
    places = [(0, 0, part, 2, 0 if part else LEAD) for part in range(2)]
    if spread_out:
        blocks += [swap(block, 1 << bit, ffns) for block, bit in zip(blocks, far)]
        places += [(1, 0, part, 2, 0 if part else LEAD) for part in range(2)]
    others = []
    for n, block in enumerate(blocks):
        last = n + 1 == len(blocks)
        others.append(swap(gate(block, arrived[0], *others) if last else block, 1, ffns))
    places += [(half, 1, part, parts, lead) for half, _, part, parts, lead in places]
    (down_full,) = kernel_call(
        functools.partial(join_down_kernel, spread_out, places),
        [pltpu.VMEM((wide, width), bf16)],
        blocks + others + [own_down],
        {len(places): 0},
        name="join",
    )
    for stage in range(1, sections - 1):
        step = ffn_forward if stage % 2 else attn_forward
        arrived = [hop(step(stage, slot, arrived[slot]), stage, 1) for slot in range(micro_count)]
    last = sections - 1
    arrived = [hop(ffn_both(last, slot, arrived[slot]), last, -1) for slot in range(micro_count)]
    for stage in range(last - 1, 0, -1):
        step = ffn_backward if stage % 2 else attn_backward
        arrived = [hop(step(stage, slot, arrived[slot]), stage, -1) for slot in range(micro_count)]
    xs, acts, nb, rb, sa, sb = saved

    down_shape = pltpu.VMEM((2, width, width), bf16)
    in_shape = pltpu.VMEM((width + TAIL, 2 * width), bf16)
    (down_sent,) = kernel_call(functools.partial(down_grad_kernel, False), [down_shape], [sa, grads[2]], name="down_send")
    (down_kept,) = kernel_call(functools.partial(down_grad_kernel, True), [down_shape], [sa, grads[2]], name="down_keep")

    def in_grad(kind, kept, before=None, after=None):
        gin, dr, db, vg = grads
        ins = [xs, sa, dr, db, vg] + [value for value in (before, after) if value is not None]
        body = functools.partial(in_grad_kernel, kind, kept, micro_count)
        name = f"in_grad_{kind}_{int(kept)}"
        return kernel_call(body, [in_shape], ins, {} if before is None else {5: 0}, name=name)[0]

    in_sent = in_grad(1, False, after=down_kept)
    down_ins, first = reduce_streams(down_kept, swap(down_sent, 1, ffns), orders, on_ffn, ffns, 0)

    for slot in range(micro_count):
        attn_backward(0, slot, gate(arrived[slot], in_sent) if slot == 0 else arrived[slot])
    in_sent, in_kept = in_grad(0, False, in_sent), in_grad(0, True, in_grad(1, True))
    gin = grads[0]

    in_ins, _ = reduce_streams(in_kept, swap(in_sent, 1), orders, everywhere, None, TAIL)
    share_rows = down_kept.shape[1] // (count // 2)
    up, low = kernel_call(
        last_down_kernel, [pltpu.VMEM((share_rows, width), bf16)] * 2, down_ins, name="last_down"
    )
    backward = [(s, s - 1) for s in ffns]
    handed = lax.ppermute(up, "section", backward)
    share_rows = in_ins[0].shape[0] - TAIL
    packed = pltpu.VMEM((share_rows, width + width // 2), bf16)
    pack_a, pack_b, tails = kernel_call(
        last_in_kernel,
        [packed, packed, pltpu.VMEM((2, TAIL, width), bf16)],
        in_ins + [handed, low],
        name="last_in",
    )

    other_tails = swap(tails, 1)
    b2_part = lax.ppermute(jnp.where(me % 2 == 0, other_tails, tails), "section", backward)
    (total_vec,) = kernel_call(vector_kernel, [pltpu.VMEM((6, width), f32)], [tails, other_tails, b2_part], name="vectors")

    blocks, masks = [pack_a, pack_b], [[0], [0]]
    for step in range(len(far)):
        bit = [orders[stream][len(far) - 1 - step] for stream in range(2)]
        got = [swap(blocks[stream], 1 << bit[stream]) for stream in range(2)]
        got_masks = [[m ^ (1 << bit[stream]) for m in masks[stream]] for stream in range(2)]
        if step + 1 < len(far):
            for stream in range(2):
                rows_now, cols_now = got[stream].shape
                (blocks[stream],) = kernel_call(
                    stack_kernel, [pltpu.VMEM((2 * rows_now, cols_now), bf16)], [blocks[stream], got[stream]]
                )
                masks[stream] = masks[stream] + got_masks[stream]
    outs = [
        jax.ShapeDtypeStruct((width, wide), f32),
        jax.ShapeDtypeStruct((2 * width, width), f32),
        pltpu.VMEM((8, LANES), f32),
    ]

    def store(blocks, masks, others, totals, name):
        shape = (len(blocks), blocks[0].shape[0])
        return kernel_call(
            functools.partial(store_kernel, orders, masks, others, width),
            outs,
            blocks + totals,
            {len(blocks) + k: k for k in range(len(totals))},
            scratch=[
                pltpu.VMEM(shape + (width,), f32),
                pltpu.VMEM(shape + (width // 2,), f32),
                pltpu.SemaphoreType.DMA((2 * len(blocks) * len(masks[0]),)),
            ],
            name=name,
            plain_ins=range(len(blocks), len(blocks) + len(totals)),
            limit=STORE_LIMIT,
            flops=STORE_COST[name],
        )

    acts, gin = kernel_call(
        keep_kernel,
        [jax.ShapeDtypeStruct(a.shape, a.dtype) for a in (acts, gin)],
        [acts, gin],
        scratch=[pltpu.SemaphoreType.DMA((2,))],
        name="keep",
    )
    early = blocks + [swap(b, 1) for b in blocks]
    *totals, token = store(early, masks, (False, False, True, True), [], "store_early")
    got = [gate(g, token) for g in got]
    *totals, token = store(got, got_masks, (False, False), totals, "store_own")
    total_in, total_down, _ = store([swap(g, 1) for g in got], got_masks, (True, True), totals, "store_other")
    return (acts[None], gin[None], total_in[None], total_down[None], total_vec[None])


def solution(mesh):
    placed = (
        P("dp", None),
        P("dp", None),
        P("dp"),
        P("section", None, None),
        P("section", None, None),
        P("section", None, None),
        P("dp", None),
    )
    return jax.shard_map(
        local,
        mesh=mesh,
        in_specs=placed,
        out_specs=(
            P("section", "dp", None),
            P("section", "dp", None),
            P("section", None, None),
            P("section", None, None),
            P("section", None, None),
        ),
        check_vma=False,
    )
```

```python
import functools

import jax
import jax.numpy as jnp
from jax import lax
from jax.experimental import pallas as pl
from jax.experimental.pallas import tpu as pltpu
from jax.sharding import PartitionSpec as P

HEADS = 12
HEAD_DIM = 64
QUAD = 4 * HEAD_DIM
LANES = 128

ln_eps = 1e-05
neg_big = -1000000000.0
root_half = 0.7071067811865476
root_two_pi = 0.3989422804014327

f32 = jnp.float32
bf16 = jnp.bfloat16

IN_VMEM = pl.BlockSpec(memory_space=pltpu.VMEM)
IN_HBM = pl.BlockSpec(memory_space=pltpu.HBM)
IN_SMEM = pl.BlockSpec(memory_space=pltpu.SMEM)
ANYWHERE = pl.BlockSpec(memory_space=pl.ANY)
VMEM_LIMIT = 4 * 1024 * 1024
STORE_LIMIT = 16 * 1024 * 1024
STORE_COST = dict(store_early=8_000_000_000, store_own=60_000_000_000, store_other=0)


def dot(a, b):
    return jnp.dot(a, b, preferred_element_type=f32)


def dot_nt(a, b):
    return lax.dot_general(a, b, (((1,), (1,)), ((), ())), preferred_element_type=f32)


def dot_tn(a, b):
    return lax.dot_general(a, b, (((0,), (0,)), ((), ())), preferred_element_type=f32)


def total_rows(value):
    return jnp.sum(value, 0, keepdims=True)


def kernel_call(body, outs, ins, aliases=None, scratch=(), name=None, plain_ins=(), limit=VMEM_LIMIT, flops=0):
    specs, placed = [], []
    for n, value in enumerate(ins):
        if n in plain_ins:
            placed.append(pltpu.with_memory_space_constraint(value, pltpu.HBM))
            specs.append(IN_HBM)
            continue
        space = pltpu.SMEM if value.dtype == jnp.int32 and value.ndim == 2 and value.size < 512 else pltpu.VMEM
        placed.append(pltpu.with_memory_space_constraint(value, space))
        specs.append(IN_SMEM if space is pltpu.SMEM else IN_VMEM)
    plain = [isinstance(out, jax.ShapeDtypeStruct) for out in outs]
    return pl.pallas_call(
        body,
        out_shape=list(outs),
        in_specs=specs,
        out_specs=[ANYWHERE if p else IN_VMEM for p in plain],
        input_output_aliases=aliases or {},
        scratch_shapes=list(scratch),
        compiler_params=pltpu.CompilerParams(vmem_limit_bytes=limit),
        cost_estimate=pl.CostEstimate(flops=flops, bytes_accessed=0, transcendentals=0),
        name=name,
    )(*placed)


def like(value):
    return pltpu.VMEM(value.shape, value.dtype)


def normalise(residual):
    mean = jnp.mean(residual, -1, keepdims=True)
    centred = residual - mean
    rstd = lax.rsqrt(jnp.mean(centred * centred, -1, keepdims=True) + ln_eps)
    return centred * rstd, rstd


def norm_back(grad, normed, rstd, gain):
    e = grad * gain
    return (e - jnp.mean(e, -1, keepdims=True) - normed * jnp.mean(e * normed, -1, keepdims=True)) * rstd


def gelu_and_slope(pre):
    cdf = 0.5 + 0.5 * lax.erf(pre * root_half)
    return pre * cdf, cdf + pre * (jnp.exp(-0.5 * pre * pre) * root_two_pi)


def finish_section(residual, gain, shift, here, send, acts, nb, rb):
    normed, rstd = normalise(residual)
    out = (normed * gain + shift).astype(bf16)
    if send is not None:
        send[...] = out
    acts[here, :] = out
    nb[here, :] = normed
    rb[here, :] = jnp.broadcast_to(rstd, (rstd.shape[0], LANES))


def start_backward(grad, gain, slot, here, nb, rb, vg):
    normed = nb[here, :]
    vg[8 * slot : 8 * slot + 1, :] = total_rows(grad * normed)
    vg[8 * slot + 1 : 8 * slot + 2, :] = total_rows(grad)
    return norm_back(grad, normed, rb[here, 0:1], gain)


def attn_forward_kernel(stage, slot, first, bias_ref, vec_ref, x_src, w_ref, *refs):
    send, xs, acts, nb, rb, sa, sb = refs[0 if first else 6 :][:7]
    rows, width = send.shape
    here = slice(slot * rows, (slot + 1) * rows)

    @pl.when(lax.axis_index("section") == stage)
    def _():
        bias = bias_ref[here, :]
        x = x_src[...] if x_src.shape[0] == rows else x_src[here, :]
        xs[here, :] = x
        zero = jnp.zeros((1, width), f32)
        qkv_bias = jnp.concatenate([vec_ref[0:1, :].astype(f32), zero, vec_ref[1:2, :].astype(f32)], 1)
        sa[here, : 3 * width] = (dot(x, w_ref[:, : 3 * width]) + qkv_bias).astype(bf16)
        lane_head = lax.broadcasted_iota(jnp.int32, (1, QUAD), 1) // HEAD_DIM
        for j in range(width // QUAD):
            lo = j * QUAD
            q4 = sa[here, lo : lo + QUAD]
            k4 = sa[here, width + lo : width + lo + QUAD]
            v_turned = sa[here, 2 * width + lo : 2 * width + lo + QUAD].T
            turned = []
            for h in range(4):
                pick = jnp.where(lane_head == h, HEAD_DIM**-0.5, 0.0).astype(bf16)
                scores = dot_nt(k4, q4 * pick) + bias
                raised = jnp.exp(scores - jnp.max(scores, 0, keepdims=True))
                probs = (raised * (1.0 / total_rows(raised))).astype(bf16)
                at = (4 * j + h) * rows
                sb[here, at : at + rows] = probs
                turned.append(dot(v_turned[h * HEAD_DIM : (h + 1) * HEAD_DIM], probs))
            sa[here, 3 * width + lo : 3 * width + lo + QUAD] = jnp.concatenate(turned, 0).astype(bf16).T
        branch = dot(sa[here, 3 * width :], w_ref[:, 3 * width :]) + vec_ref[2:3, :].astype(f32)
        finish_section(
            x.astype(f32) + branch, vec_ref[3:4, :].astype(f32), vec_ref[4:5, :].astype(f32), here, send, acts, nb, rb
        )


def attn_backward_kernel(stage, slot, vec_ref, g_src, w_ref, nb, rb, sa, sb, *refs):
    send, gin, dr, vg = refs[3:7]
    rows, width = g_src.shape
    here = slice(slot * rows, (slot + 1) * rows)

    @pl.when(lax.axis_index("section") == stage)
    def _():
        d_resid = start_backward(g_src[...].astype(f32), vec_ref[3:4, :].astype(f32), slot, here, nb, rb, vg)
        d_branch = d_resid.astype(bf16)
        dr[here, 3 * width :] = d_branch
        d_context = dot_nt(d_branch, w_ref[:, 3 * width :]).astype(bf16)
        lane_head = lax.broadcasted_iota(jnp.int32, (1, QUAD), 1) // HEAD_DIM
        scale = HEAD_DIM**-0.5
        for j in range(width // QUAD):
            lo = j * QUAD
            q4 = sa[here, lo : lo + QUAD]
            k4 = sa[here, width + lo : width + lo + QUAD]
            v4 = sa[here, 2 * width + lo : 2 * width + lo + QUAD]
            c4 = d_context[:, lo : lo + QUAD]
            k_turned = k4.T
            d_scores, queries, contexts, turned = [], [], [], []
            for h in range(4):
                pick = jnp.where(lane_head == h, 1.0, 0.0).astype(bf16)
                at = (4 * j + h) * rows
                probs = sb[here, at : at + rows].astype(f32)
                picked = c4 * pick
                d_probs = dot_nt(v4, picked)
                weighed = probs * d_probs
                d_score = (weighed - probs * total_rows(weighed)).astype(bf16)
                d_scores.append(d_score)
                queries.append(q4 * pick)
                contexts.append(picked)
                turned.append(dot(k_turned[h * HEAD_DIM : (h + 1) * HEAD_DIM], d_score))
            at = 4 * j * rows
            d_key = dot(jnp.concatenate(d_scores, 1), jnp.concatenate(queries, 0))
            d_value = dot(sb[here, at : at + 4 * rows], jnp.concatenate(contexts, 0))
            d_query = (jnp.concatenate(turned, 0) * scale).astype(bf16).T
            dr[here, lo : lo + QUAD] = d_query
            dr[here, width + lo : width + lo + QUAD] = (d_key * scale).astype(bf16)
            dr[here, 2 * width + lo : 2 * width + lo + QUAD] = d_value.astype(bf16)
        d_input = (d_resid + dot_nt(dr[here, : 3 * width], w_ref[:, : 3 * width])).astype(bf16)
        send[...] = d_input
        gin[here, :] = d_input


def ffn_forward_body(x, here, vec_ref, b2_ref, w_ref, d_ref, sa, sb):
    width = w_ref.shape[0]
    cuts = [slice(c * width, (c + 1) * width) for c in range(4)]
    branch = x.astype(f32) + b2_ref[0:1, :].astype(f32)
    pre = dot(x, w_ref[:, cuts[0]])
    for c in range(4):
        later = dot(x, w_ref[:, cuts[c + 1]]) if c < 3 else None
        hidden, slope = gelu_and_slope(pre + vec_ref[c : c + 1, :].astype(f32))
        hidden = hidden.astype(bf16)
        sa[here, cuts[c]] = hidden
        sb[here, cuts[c]] = slope.astype(bf16)
        branch = branch + dot(hidden, d_ref[cuts[c], :])
        pre = later
    return branch


def ffn_backward_body(d_resid, here, w_ref, d_ref, sb, dr, db):
    width = w_ref.shape[0]
    cuts = [slice(c * width, (c + 1) * width) for c in range(4)]
    d_branch = d_resid.astype(bf16)
    db[here, :] = d_branch
    d_input = d_resid
    d_hidden = dot_nt(d_branch, d_ref[cuts[0], :])
    for c in range(4):
        later = dot_nt(d_branch, d_ref[cuts[c + 1], :]) if c < 3 else None
        d_pre = (d_hidden * sb[here, cuts[c]].astype(f32)).astype(bf16)
        dr[here, cuts[c]] = d_pre
        d_input = d_input + dot_nt(d_pre, w_ref[:, cuts[c]])
        d_hidden = later
    return d_input.astype(bf16)


def ffn_forward_kernel(stage, slot, vec_ref, b2_ref, x_src, w_ref, d_ref, *refs):
    send, xs, acts, nb, rb, sa, sb = refs[6:13]
    rows, width = x_src.shape
    here = slice(slot * rows, (slot + 1) * rows)

    @pl.when(lax.axis_index("section") == stage)
    def _():
        x = x_src[...]
        xs[here, :] = x
        residual = ffn_forward_body(x, here, vec_ref, b2_ref, w_ref, d_ref, sa, sb)
        finish_section(residual, vec_ref[4:5, :].astype(f32), vec_ref[5:6, :].astype(f32), here, send, acts, nb, rb)


def ffn_backward_kernel(stage, slot, vec_ref, g_src, w_ref, d_ref, nb, rb, sb, *refs):
    send, gin, dr, db, vg = refs[4:9]
    rows, width = g_src.shape
    here = slice(slot * rows, (slot + 1) * rows)

    @pl.when(lax.axis_index("section") == stage)
    def _():
        d_resid = start_backward(g_src[...].astype(f32), vec_ref[4:5, :].astype(f32), slot, here, nb, rb, vg)
        d_input = ffn_backward_body(d_resid, here, w_ref, d_ref, sb, dr, db)
        send[...] = d_input
        gin[here, :] = d_input


def ffn_both_kernel(stage, slot, first, vec_ref, b2_ref, x_src, cot, w_ref, d_ref, *refs):
    send, xs, acts, nb, rb, sa, sb, gin, dr, db, vg = refs[6 if first else 10 :][:11]
    rows, width = x_src.shape
    here = slice(slot * rows, (slot + 1) * rows)

    @pl.when(lax.axis_index("section") == stage)
    def _():
        x = x_src[...]
        xs[here, :] = x
        residual = ffn_forward_body(x, here, vec_ref, b2_ref, w_ref, d_ref, sa, sb)
        gain = vec_ref[4:5, :].astype(f32)
        normed, rstd = normalise(residual)
        acts[here, :] = (normed * gain + vec_ref[5:6, :].astype(f32)).astype(bf16)
        grad = cot[here, :].astype(f32)
        vg[8 * slot : 8 * slot + 1, :] = total_rows(grad * normed)
        vg[8 * slot + 1 : 8 * slot + 2, :] = total_rows(grad)
        d_resid = norm_back(grad, normed, rstd, gain)
        d_input = ffn_backward_body(d_resid, here, w_ref, d_ref, sb, dr, db)
        send[...] = d_input
        gin[here, :] = d_input


LEAD = 16


def quarter(spread_out, other_half, other_core):
    me = lax.axis_index("dp")
    core = (me % 2) ^ other_core
    if not spread_out:
        return core
    return 2 * (((me >> 1) ^ (me >> 2)) % 2 ^ other_half) + core


def piece_kernel(spread_out, vectors, down, first, second, vec_v, sems):
    size = second.shape[0]
    at = pl.multiple_of(quarter(spread_out, 0, 0) * 2 * size, 16)
    copies = [
        pltpu.make_async_copy(vectors, vec_v, sems.at[0]),
        pltpu.make_async_copy(down.at[pl.ds(at, size), :], first.at[pl.ds(LEAD, size), :], sems.at[1]),
        pltpu.make_async_copy(down.at[pl.ds(at + size, size), :], second, sems.at[2]),
    ]
    for copy in copies:
        copy.start()
    for copy in copies:
        copy.wait()
    first[:LEAD, :] = jnp.broadcast_to(vec_v[5:6, :], (LEAD, first.shape[1]))


def setup_kernel(sections, lens, keep, vectors, x_in, cot, w_in, w_v, edge_v, vec_v, bias, lens_s, keep_v, sems):
    micro_count = lens.shape[0]
    rows = bias.shape[1]
    section = lax.axis_index("section")
    w_copy = pltpu.make_async_copy(w_in, w_v, sems.at[0])
    vec_copy = pltpu.make_async_copy(vectors, vec_v, sems.at[1])
    w_copy.start()
    vec_copy.start()

    @pl.when(section == 0)
    def _():
        pltpu.make_async_copy(x_in, edge_v, sems.at[2]).start()

    @pl.when(section == sections - 1)
    def _():
        pltpu.make_async_copy(cot, edge_v, sems.at[2]).start()

    @pl.when(section % 2 == 0)
    def _():
        lens_copy = pltpu.make_async_copy(lens, lens_s, sems.at[3])
        keep_copy = pltpu.make_async_copy(keep, keep_v, sems.at[4])
        lens_copy.start()
        keep_copy.start()
        key_pos = lax.broadcasted_iota(jnp.int32, (rows, rows), 0)
        query_pos = lax.broadcasted_iota(jnp.int32, (rows, rows), 1)
        lens_copy.wait()
        keep_copy.wait()
        for slot in range(micro_count):
            key_seg, query_seg, end = 0, 0, 0
            for k in range(lens.shape[1]):
                end = end + lens_s[slot, k]
                key_seg = key_seg + (key_pos >= end).astype(jnp.int32)
                query_seg = query_seg + (query_pos >= end).astype(jnp.int32)
            kept = jnp.broadcast_to(keep_v[slot : slot + 1, :].astype(f32), (rows, rows)).T > 0.5
            allowed = (key_seg == query_seg) & (kept | (key_pos == query_pos))
            bias[slot * rows : (slot + 1) * rows, :] = jnp.where(allowed, 0.0, neg_big)

    w_copy.wait()
    vec_copy.wait()

    @pl.when((section == 0) | (section == sections - 1))
    def _():
        pltpu.make_async_copy(x_in, edge_v, sems.at[2]).wait()


def own_down_kernel(down, out, token, sems):
    half = down.shape[0]
    token[...] = jnp.zeros_like(token)

    @pl.when(lax.axis_index("section") % 2 == 1)
    def _():
        copy = pltpu.make_async_copy(down, out.at[pl.ds(half, half), :], sems.at[0])
        copy.start()
        copy.wait()


def join_down_kernel(spread_out, places, *refs):
    out = refs[-1]

    @pl.when(lax.axis_index("section") % 2 == 1)
    def _():
        for block, (other_half, other_core, part, parts, lead) in zip(refs[: len(places)], places):
            size = block.shape[0] - lead
            at = quarter(spread_out, other_half, other_core) * parts + part
            out[pl.ds(pl.multiple_of(at * size, 16), size), :] = block[lead:, :]


TAIL = 16


def core_half(kept):
    core = lax.axis_index("dp") % 2
    return core if kept else 1 - core


def down_grad_kernel(kept, sa, db, out):
    width = db.shape[1]

    @pl.when(lax.axis_index("section") % 2 == 1)
    def _():
        half = core_half(kept)
        for part in range(2):
            at = pl.multiple_of((2 * part + half) * width, LANES)
            out[part] = dot_tn(sa[:, pl.ds(at, width)], db[...]).astype(bf16)


def in_grad_kernel(kind, kept, micro_count, xs, sa, dr, db, vg, *refs):
    out = refs[-1]
    width = xs.shape[1]

    @pl.when(lax.axis_index("section") % 2 == kind)
    def _():
        half = core_half(kept)
        out[width:, :] = jnp.zeros((TAIL, 2 * width), bf16)
        for k in range(2):
            right = dr[:, pl.ds(pl.multiple_of((2 * half + k) * width, LANES), width)]
            left = xs[...]
            if kind == 0 and k == 1:
                left = jnp.where(half == 1, sa[:, 3 * width :], left)
            here = slice(k * width, (k + 1) * width)
            out[:width, here] = dot_tn(left, right).astype(bf16)
            if k == 0:
                other = total_rows(db[...].astype(f32)) if kind else jnp.zeros((1, width), f32)
            else:
                other = jnp.zeros((1, width), f32)
            norm = sum(vg[8 * m + k : 8 * m + k + 1, :] for m in range(micro_count))
            sums = total_rows(right.astype(f32))
            both = jnp.concatenate([sums, jnp.where(half == 0, norm, other)], 0)
            out[width : width + 2, here] = both.astype(bf16)


def bit_of(bit):
    return (lax.axis_index("dp") >> bit) % 2


def added(a, b):
    return (a.astype(f32) + b.astype(f32)).astype(bf16)


def halve(kept, got, outs, bit, tail, cut=slice(None)):
    rows = (kept.shape[-2] - tail) // 2
    mine = bit_of(bit)
    for out, half in zip(outs, (mine, 1 - mine)):
        at = pl.ds(pl.multiple_of(half * rows, 16), rows)
        if kept.ndim == 3:
            out[...] = added(kept[:, at, cut], got[:, at, cut])
        else:
            out[:rows, :] = added(kept[at, cut], got[at, cut])
    if tail:
        last = slice(2 * rows, 2 * rows + tail)
        total = added(kept[last, cut], got[last, cut])
        for out in outs:
            out[rows:, :] = total


def first_add_kernel(live, bits, tail, kept, got, *outs):
    columns = kept.shape[-1] // 2

    @pl.when(live())
    def _():
        for stream in range(2):
            cut = slice(stream * columns, (stream + 1) * columns)
            halve(kept, got, outs[2 * stream : 2 * stream + 2], bits[stream], tail, cut)


def next_add_kernel(live, bits, tail, *refs):
    ins, outs = refs[:4], refs[4:]

    @pl.when(live())
    def _():
        for stream in range(2):
            halve(*ins[2 * stream : 2 * stream + 2], outs[2 * stream : 2 * stream + 2], bits[stream], tail)


def last_down_kernel(keep_a, got_a, keep_b, got_b, up, low):
    columns = keep_a.shape[-1]

    @pl.when(on_ffn())
    def _():
        for part, out in enumerate((up, low)):
            out[:, :columns] = added(keep_a[part], got_a[part])
            out[:, columns:] = added(keep_b[part], got_b[part])


def last_in_kernel(keep_a, got_a, keep_b, got_b, handed, low, pack_a, pack_b, tails):
    rows = pack_a.shape[0]
    wide = keep_a.shape[1]
    columns = low.shape[1] // 2
    for stream, (kept, got, out) in enumerate(((keep_a, got_a, pack_a), (keep_b, got_b, pack_b))):
        cut = slice(stream * columns, (stream + 1) * columns)
        out[:, :wide] = added(kept[:rows, :], got[:rows, :])
        out[:, wide:] = jnp.where(on_ffn(), low[:, cut], handed[:, cut])
        tails[stream] = added(kept[rows:, :], got[rows:, :])


def stack_kernel(upper, lower, out):
    rows = upper.shape[0]
    out[:rows, :] = upper[...]
    out[rows:, :] = lower[...]


def on_ffn():
    return lax.axis_index("section") % 2 == 1


def everywhere():
    return True


def swap(value, mask, only=None):
    count, sections = lax.axis_size("dp"), lax.axis_size("section")
    if only is None:
        return lax.ppermute(value, "dp", [(i, i ^ mask) for i in range(count)])
    pairs = [(i * sections + s, (i ^ mask) * sections + s) for i in range(count) for s in only]
    return lax.ppermute(value, ("dp", "section"), pairs)


def cut_shape(value, tail, columns=1):
    shape = list(value.shape)
    shape[-2] = (shape[-2] - tail) // 2 + tail
    shape[-1] //= columns
    return pltpu.VMEM(tuple(shape), value.dtype)


def reduce_streams(kept, got, orders, live, only, tail):
    outs = [cut_shape(kept, tail, 2)] * 4
    parts = kernel_call(functools.partial(first_add_kernel, live, [o[0] for o in orders], tail), outs, [kept, got])
    first = parts[0]
    for step in range(len(orders[0])):
        keep_a, send_a, keep_b, send_b = parts
        ins = [keep_a, swap(send_a, 1 << orders[0][step], only), keep_b, swap(send_b, 1 << orders[1][step], only)]
        if step + 1 < len(orders[0]):
            outs = [cut_shape(keep_a, tail)] * 4
            parts = kernel_call(
                functools.partial(next_add_kernel, live, [o[step + 1] for o in orders], tail), outs, ins
            )
    return ins, first


def far_index(owner, order):
    return sum(((owner >> bit) % 2) << (len(order) - 1 - k) for k, bit in enumerate(order))


def store_kernel(orders, masks, others, width, *refs):
    count = len(others)
    blocks = refs[:count]
    total_in, total_down, token, wide_buf, thin_buf, sems = refs[-6:]
    token[...] = jnp.zeros_like(token)
    me = lax.axis_index("dp")
    copies = []

    def send(src, dst):
        copy = pltpu.make_async_copy(src, dst, sems.at[len(copies)])
        copy.start()
        copies.append(copy)

    for n, (block, other) in enumerate(zip(blocks, others)):
        stream = n % 2
        half = (me % 2) ^ (1 if other else 0)
        size = block.shape[0] // len(masks[stream])
        thin = block.shape[1] - width
        lane = pl.multiple_of((2 * half + stream) * width, LANES)
        for k, mask in enumerate(masks[stream]):
            here = slice(k * size, (k + 1) * size)
            row = far_index(me ^ mask, orders[stream]) * size
            wide_buf[n, here, :] = block[here, :width].astype(f32)
            send(
                wide_buf.at[n, here, :],
                total_in.at[pl.ds(pl.multiple_of(row, 16), size), pl.ds(lane, width)],
            )
            thin_buf[n, here, :] = block[here, width:].astype(f32)
            send(
                thin_buf.at[n, here, :],
                total_down.at[
                    pl.ds(pl.multiple_of(half * width + row, 16), size), stream * thin : (stream + 1) * thin
                ],
            )
    for copy in copies:
        copy.wait()


def keep_kernel(acts, gin, acts_out, gin_out, sems):
    copies = [
        pltpu.make_async_copy(acts, acts_out, sems.at[0]),
        pltpu.make_async_copy(gin, gin_out, sems.at[1]),
    ]
    for copy in copies:
        copy.start()
    for copy in copies:
        copy.wait()


def vector_kernel(own, other, b2_ref, out):
    core = lax.axis_index("dp") % 2
    own, other = own[...].astype(f32), other[...].astype(f32)
    first, second = jnp.where(core == 0, own, other), jnp.where(core == 0, other, own)
    sums = [first[0, 0:1], first[1, 0:1], second[0, 0:1], second[1, 0:1]]
    norms = [first[0, 1:2], first[1, 1:2]]

    @pl.when(on_ffn())
    def _():
        out[...] = jnp.concatenate(sums + norms, 0)

    @pl.when(jnp.logical_not(on_ffn()))
    def _():
        out[...] = jnp.concatenate([sums[0], sums[2], sums[3]] + norms + [b2_ref[0, 1:2].astype(f32)], 0)


def gate_kernel(*refs):
    pass


def gate(value, *after):
    return pl.pallas_call(
        gate_kernel,
        out_shape=jax.ShapeDtypeStruct(value.shape, value.dtype),
        in_specs=[ANYWHERE] * (1 + len(after)),
        out_specs=ANYWHERE,
        input_output_aliases={0: 0},
        compiler_params=pltpu.CompilerParams(vmem_limit_bytes=1024 * 1024),
        cost_estimate=pl.CostEstimate(flops=0, bytes_accessed=0, transcendentals=0),
        name="gate",
    )(value, *after)


def local(x_in, lengths, keep_mask, w_in, w_down, vectors, cotangent):
    micro_count = lengths.shape[0]
    tokens, width = x_in.shape
    rows = tokens // micro_count
    wide = 4 * width
    count = lax.axis_size("dp")
    bits = count.bit_length() - 1
    sections = lax.axis_size("section")
    me = lax.axis_index("dp")
    ffns = tuple(range(1, sections, 2))
    down = w_down[0]
    far = list(range(1, bits))
    orders = (far, far[::-1])

    def hop(value, stage, step):
        return lax.ppermute(value, "section", [(stage, stage + step)])

    onward = [(s, s + 1) for s in range(0, sections, 2)]
    spread_out = len(far) == 2
    share = down.shape[0] // (8 if spread_out else 4)
    pieces = kernel_call(
        functools.partial(piece_kernel, spread_out),
        [pltpu.VMEM((LEAD + share, width), bf16), pltpu.VMEM((share, width), bf16)],
        [vectors[0], down],
        scratch=[pltpu.VMEM(vectors.shape[1:], bf16), pltpu.SemaphoreType.DMA((3,))],
        plain_ins=(0, 1),
        name="piece",
    )
    pieces = [lax.ppermute(piece, "section", onward) for piece in pieces]
    weights, edge, vec, bias = kernel_call(
        functools.partial(setup_kernel, sections),
        [
            pltpu.VMEM((width, wide), bf16),
            pltpu.VMEM((tokens, width), bf16),
            pltpu.VMEM(vectors.shape[1:], bf16),
            pltpu.VMEM((tokens, rows), f32),
        ],
        [lengths, keep_mask.reshape(micro_count, rows), vectors[0], x_in, cotangent, w_in[0]],
        scratch=[
            pltpu.SMEM(lengths.shape, jnp.int32),
            pltpu.VMEM((micro_count, rows), jnp.int32),
            pltpu.SemaphoreType.DMA((5,)),
        ],
        plain_ins=range(6),
        name="setup",
    )
    own_down, down_token = kernel_call(
        own_down_kernel,
        [pltpu.VMEM((wide, width), bf16), pltpu.VMEM((8, LANES), f32)],
        [down],
        scratch=[pltpu.SemaphoreType.DMA((1,))],
        plain_ins=(0,),
        name="own_down",
    )

    row_out = pltpu.VMEM((rows, width), bf16)
    state = [
        pltpu.VMEM((tokens, width), bf16),
        pltpu.VMEM((tokens, width), bf16),
        pltpu.VMEM((tokens, width), f32),
        pltpu.VMEM((tokens, LANES), f32),
        pltpu.VMEM((tokens, wide), bf16),
        pltpu.VMEM((tokens, HEADS * rows), bf16),
    ]
    saved, grads = None, None

    def attn_forward(stage, slot, source):
        nonlocal saved
        first = saved is None
        got = kernel_call(
            functools.partial(attn_forward_kernel, stage, slot, first),
            [row_out] + state,
            [bias, vec, source, weights] + (saved or []),
            {} if first else {4 + k: 1 + k for k in range(6)},
            name=f"attn_forward_{stage}_{slot}",
        )
        saved = list(got[1:])
        return got[0]

    def ffn_forward(stage, slot, source):
        nonlocal saved
        got = kernel_call(
            functools.partial(ffn_forward_kernel, stage, slot),
            [row_out] + state,
            [vec, b2, source, weights, down_full] + saved,
            {5 + k: 1 + k for k in range(6)},
            name=f"ffn_forward_{stage}_{slot}",
        )
        saved = list(got[1:])
        return got[0]

    def ffn_both(stage, slot, source):
        nonlocal saved, grads
        first = grads is None
        grad_state = [
            pltpu.VMEM((tokens, width), bf16),
            pltpu.VMEM((tokens, wide), bf16),
            pltpu.VMEM((tokens, width), bf16),
            pltpu.VMEM((8 * micro_count, width), f32),
        ]
        got = kernel_call(
            functools.partial(ffn_both_kernel, stage, slot, first),
            [row_out] + state + grad_state,
            [vec, b2, source, edge, weights, down_full] + saved + (grads or []),
            {6 + k: 1 + k for k in range(6 if first else 10)},
            name=f"ffn_both_{stage}_{slot}",
        )
        saved, grads = list(got[1:7]), list(got[7:])
        return got[0]

    def attn_backward(stage, slot, source):
        nonlocal grads
        xs, acts, nb, rb, sa, sb = saved
        gin, dr, db, vg = grads
        got = kernel_call(
            functools.partial(attn_backward_kernel, stage, slot),
            [row_out, like(gin), like(dr), like(vg)],
            [vec, source, weights, nb, rb, sa, sb, gin, dr, vg],
            {7 + k: 1 + k for k in range(3)},
            name=f"attn_backward_{stage}_{slot}",
        )
        grads = [got[1], got[2], db, got[3]]
        return got[0]

    def ffn_backward(stage, slot, source):
        nonlocal grads
        xs, acts, nb, rb, sa, sb = saved
        got = kernel_call(
            functools.partial(ffn_backward_kernel, stage, slot),
            [row_out] + [like(a) for a in grads],
            [vec, source, weights, down_full, nb, rb, sb] + grads,
            {7 + k: 1 + k for k in range(4)},
            name=f"ffn_backward_{stage}_{slot}",
        )
        grads = list(got[1:])
        return got[0]

    sent = [attn_forward(0, slot, edge) for slot in range(micro_count)]
    arrived = [hop(value, 0, 1) for value in sent]
    blocks = [gate(piece, sent[0], down_token) for piece in pieces]
    b2 = blocks[0]
    places = [(0, 0, part, 2, 0 if part else LEAD) for part in range(2)]
    if spread_out:
        blocks += [swap(block, 1 << bit, ffns) for block, bit in zip(blocks, far)]
        places += [(1, 0, part, 2, 0 if part else LEAD) for part in range(2)]
    others = []
    for n, block in enumerate(blocks):
        last = n + 1 == len(blocks)
        others.append(swap(gate(block, arrived[0], *others) if last else block, 1, ffns))
    places += [(half, 1, part, parts, lead) for half, _, part, parts, lead in places]
    (down_full,) = kernel_call(
        functools.partial(join_down_kernel, spread_out, places),
        [pltpu.VMEM((wide, width), bf16)],
        blocks + others + [own_down],
        {len(places): 0},
        name="join",
    )
    for stage in range(1, sections - 1):
        step = ffn_forward if stage % 2 else attn_forward
        arrived = [hop(step(stage, slot, arrived[slot]), stage, 1) for slot in range(micro_count)]
    last = sections - 1
    arrived = [hop(ffn_both(last, slot, arrived[slot]), last, -1) for slot in range(micro_count)]
    for stage in range(last - 1, 0, -1):
        step = ffn_backward if stage % 2 else attn_backward
        arrived = [hop(step(stage, slot, arrived[slot]), stage, -1) for slot in range(micro_count)]
    xs, acts, nb, rb, sa, sb = saved

    down_shape = pltpu.VMEM((2, width, width), bf16)
    in_shape = pltpu.VMEM((width + TAIL, 2 * width), bf16)
    (down_sent,) = kernel_call(functools.partial(down_grad_kernel, False), [down_shape], [sa, grads[2]], name="down_send")
    (down_kept,) = kernel_call(functools.partial(down_grad_kernel, True), [down_shape], [sa, grads[2]], name="down_keep")

    def in_grad(kind, kept, before=None, after=None):
        gin, dr, db, vg = grads
        ins = [xs, sa, dr, db, vg] + [value for value in (before, after) if value is not None]
        body = functools.partial(in_grad_kernel, kind, kept, micro_count)
        name = f"in_grad_{kind}_{int(kept)}"
        return kernel_call(body, [in_shape], ins, {} if before is None else {5: 0}, name=name)[0]

    in_sent = in_grad(1, False, after=down_kept)
    down_ins, first = reduce_streams(down_kept, swap(down_sent, 1, ffns), orders, on_ffn, ffns, 0)

    for slot in range(micro_count):
        attn_backward(0, slot, gate(arrived[slot], in_sent) if slot == 0 else arrived[slot])
    in_sent, in_kept = in_grad(0, False, in_sent), in_grad(0, True, in_grad(1, True))
    gin = grads[0]

    in_ins, _ = reduce_streams(in_kept, swap(in_sent, 1), orders, everywhere, None, TAIL)
    share_rows = down_kept.shape[1] // (count // 2)
    up, low = kernel_call(
        last_down_kernel, [pltpu.VMEM((share_rows, width), bf16)] * 2, down_ins, name="last_down"
    )
    backward = [(s, s - 1) for s in ffns]
    handed = lax.ppermute(up, "section", backward)
    share_rows = in_ins[0].shape[0] - TAIL
    packed = pltpu.VMEM((share_rows, width + width // 2), bf16)
    pack_a, pack_b, tails = kernel_call(
        last_in_kernel,
        [packed, packed, pltpu.VMEM((2, TAIL, width), bf16)],
        in_ins + [handed, low],
        name="last_in",
    )

    other_tails = swap(tails, 1)
    b2_part = lax.ppermute(jnp.where(me % 2 == 0, other_tails, tails), "section", backward)
    (total_vec,) = kernel_call(vector_kernel, [pltpu.VMEM((6, width), f32)], [tails, other_tails, b2_part], name="vectors")

    blocks, masks = [pack_a, pack_b], [[0], [0]]
    for step in range(len(far)):
        bit = [orders[stream][len(far) - 1 - step] for stream in range(2)]
        got = [swap(blocks[stream], 1 << bit[stream]) for stream in range(2)]
        got_masks = [[m ^ (1 << bit[stream]) for m in masks[stream]] for stream in range(2)]
        if step + 1 < len(far):
            for stream in range(2):
                rows_now, cols_now = got[stream].shape
                (blocks[stream],) = kernel_call(
                    stack_kernel, [pltpu.VMEM((2 * rows_now, cols_now), bf16)], [blocks[stream], got[stream]]
                )
                masks[stream] = masks[stream] + got_masks[stream]
    outs = [
        jax.ShapeDtypeStruct((width, wide), f32),
        jax.ShapeDtypeStruct((2 * width, width), f32),
        pltpu.VMEM((8, LANES), f32),
    ]

    def store(blocks, masks, others, totals, name):
        shape = (len(blocks), blocks[0].shape[0])
        return kernel_call(
            functools.partial(store_kernel, orders, masks, others, width),
            outs,
            blocks + totals,
            {len(blocks) + k: k for k in range(len(totals))},
            scratch=[
                pltpu.VMEM(shape + (width,), f32),
                pltpu.VMEM(shape + (width // 2,), f32),
                pltpu.SemaphoreType.DMA((2 * len(blocks) * len(masks[0]),)),
            ],
            name=name,
            plain_ins=range(len(blocks), len(blocks) + len(totals)),
            limit=STORE_LIMIT,
            flops=STORE_COST[name],
        )

    acts, gin = kernel_call(
        keep_kernel,
        [jax.ShapeDtypeStruct(a.shape, a.dtype) for a in (acts, gin)],
        [acts, gin],
        scratch=[pltpu.SemaphoreType.DMA((2,))],
        name="keep",
    )
    early = blocks + [swap(b, 1) for b in blocks]
    *totals, token = store(early, masks, (False, False, True, True), [], "store_early")
    got = [gate(g, token) for g in got]
    *totals, token = store(got, got_masks, (False, False), totals, "store_own")
    total_in, total_down, _ = store([swap(g, 1) for g in got], got_masks, (True, True), totals, "store_other")
    return (acts[None], gin[None], total_in[None], total_down[None], total_vec[None])


def solution(mesh):
    placed = (
        P("dp", None),
        P("dp", None),
        P("dp"),
        P("section", None, None),
        P("section", None, None),
        P("section", None, None),
        P("dp", None),
    )
    return jax.shard_map(
        local,
        mesh=mesh,
        in_specs=placed,
        out_specs=(
            P("section", "dp", None),
            P("section", "dp", None),
            P("section", None, None),
            P("section", None, None),
            P("section", None, None),
        ),
        check_vma=False,
    )
```

```python
import functools

import jax
import jax.numpy as jnp
from jax import lax
from jax.experimental import pallas as pl
from jax.experimental.pallas import tpu as pltpu
from jax.sharding import PartitionSpec as P

HEADS = 12
HEAD_DIM = 64
QUAD = 4 * HEAD_DIM
LANES = 128

ln_eps = 1e-05
neg_big = -1000000000.0
root_half = 0.7071067811865476
root_two_pi = 0.3989422804014327

f32 = jnp.float32
bf16 = jnp.bfloat16

IN_VMEM = pl.BlockSpec(memory_space=pltpu.VMEM)
IN_HBM = pl.BlockSpec(memory_space=pltpu.HBM)
IN_SMEM = pl.BlockSpec(memory_space=pltpu.SMEM)
ANYWHERE = pl.BlockSpec(memory_space=pl.ANY)
VMEM_LIMIT = 4 * 1024 * 1024
STORE_LIMIT = 16 * 1024 * 1024
STORE_COST = dict(store_early=8_000_000_000, store_own=60_000_000_000, store_other=0)


def dot(a, b):
    return jnp.dot(a, b, preferred_element_type=f32)


def dot_nt(a, b):
    return lax.dot_general(a, b, (((1,), (1,)), ((), ())), preferred_element_type=f32)


def dot_tn(a, b):
    return lax.dot_general(a, b, (((0,), (0,)), ((), ())), preferred_element_type=f32)


def total_rows(value):
    return jnp.sum(value, 0, keepdims=True)


def kernel_call(body, outs, ins, aliases=None, scratch=(), name=None, plain_ins=(), limit=VMEM_LIMIT, flops=0):
    specs, placed = [], []
    for n, value in enumerate(ins):
        if n in plain_ins:
            placed.append(pltpu.with_memory_space_constraint(value, pltpu.HBM))
            specs.append(IN_HBM)
            continue
        space = pltpu.SMEM if value.dtype == jnp.int32 and value.ndim == 2 and value.size < 512 else pltpu.VMEM
        placed.append(pltpu.with_memory_space_constraint(value, space))
        specs.append(IN_SMEM if space is pltpu.SMEM else IN_VMEM)
    plain = [isinstance(out, jax.ShapeDtypeStruct) for out in outs]
    return pl.pallas_call(
        body,
        out_shape=list(outs),
        in_specs=specs,
        out_specs=[ANYWHERE if p else IN_VMEM for p in plain],
        input_output_aliases=aliases or {},
        scratch_shapes=list(scratch),
        compiler_params=pltpu.CompilerParams(vmem_limit_bytes=limit),
        cost_estimate=pl.CostEstimate(flops=flops, bytes_accessed=0, transcendentals=0),
        name=name,
    )(*placed)


def like(value):
    return pltpu.VMEM(value.shape, value.dtype)


def normalise(residual):
    mean = jnp.mean(residual, -1, keepdims=True)
    centred = residual - mean
    rstd = lax.rsqrt(jnp.mean(centred * centred, -1, keepdims=True) + ln_eps)
    return centred * rstd, rstd


def norm_back(grad, normed, rstd, gain):
    e = grad * gain
    return (e - jnp.mean(e, -1, keepdims=True) - normed * jnp.mean(e * normed, -1, keepdims=True)) * rstd


def gelu_and_slope(pre):
    cdf = 0.5 + 0.5 * lax.erf(pre * root_half)
    return pre * cdf, cdf + pre * (jnp.exp(-0.5 * pre * pre) * root_two_pi)


def finish_section(residual, gain, shift, here, send, acts, nb, rb):
    normed, rstd = normalise(residual)
    out = (normed * gain + shift).astype(bf16)
    if send is not None:
        send[...] = out
    acts[here, :] = out
    nb[here, :] = normed
    rb[here, :] = jnp.broadcast_to(rstd, (rstd.shape[0], LANES))


def start_backward(grad, gain, slot, here, nb, rb, vg):
    normed = nb[here, :]
    vg[8 * slot : 8 * slot + 1, :] = total_rows(grad * normed)
    vg[8 * slot + 1 : 8 * slot + 2, :] = total_rows(grad)
    return norm_back(grad, normed, rb[here, 0:1], gain)


def attn_forward_kernel(stage, slot, first, bias_ref, vec_ref, x_src, w_ref, *refs):
    send, xs, acts, nb, rb, sa, sb = refs[0 if first else 6 :][:7]
    rows, width = send.shape
    here = slice(slot * rows, (slot + 1) * rows)

    @pl.when(lax.axis_index("section") == stage)
    def _():
        bias = bias_ref[here, :]
        x = x_src[...] if x_src.shape[0] == rows else x_src[here, :]
        xs[here, :] = x
        zero = jnp.zeros((1, width), f32)
        qkv_bias = jnp.concatenate([vec_ref[0:1, :].astype(f32), zero, vec_ref[1:2, :].astype(f32)], 1)
        sa[here, : 3 * width] = (dot(x, w_ref[:, : 3 * width]) + qkv_bias).astype(bf16)
        lane_head = lax.broadcasted_iota(jnp.int32, (1, QUAD), 1) // HEAD_DIM
        for j in range(width // QUAD):
            lo = j * QUAD
            q4 = sa[here, lo : lo + QUAD]
            k4 = sa[here, width + lo : width + lo + QUAD]
            v_turned = sa[here, 2 * width + lo : 2 * width + lo + QUAD].T
            turned = []
            for h in range(4):
                pick = jnp.where(lane_head == h, HEAD_DIM**-0.5, 0.0).astype(bf16)
                scores = dot_nt(k4, q4 * pick) + bias
                raised = jnp.exp(scores - jnp.max(scores, 0, keepdims=True))
                probs = (raised * (1.0 / total_rows(raised))).astype(bf16)
                at = (4 * j + h) * rows
                sb[here, at : at + rows] = probs
                turned.append(dot(v_turned[h * HEAD_DIM : (h + 1) * HEAD_DIM], probs))
            sa[here, 3 * width + lo : 3 * width + lo + QUAD] = jnp.concatenate(turned, 0).astype(bf16).T
        branch = dot(sa[here, 3 * width :], w_ref[:, 3 * width :]) + vec_ref[2:3, :].astype(f32)
        finish_section(
            x.astype(f32) + branch, vec_ref[3:4, :].astype(f32), vec_ref[4:5, :].astype(f32), here, send, acts, nb, rb
        )


def attn_backward_kernel(stage, slot, vec_ref, g_src, w_ref, nb, rb, sa, sb, *refs):
    send, gin, dr, vg = refs[3:7]
    rows, width = g_src.shape
    here = slice(slot * rows, (slot + 1) * rows)

    @pl.when(lax.axis_index("section") == stage)
    def _():
        d_resid = start_backward(g_src[...].astype(f32), vec_ref[3:4, :].astype(f32), slot, here, nb, rb, vg)
        d_branch = d_resid.astype(bf16)
        dr[here, 3 * width :] = d_branch
        d_context = dot_nt(d_branch, w_ref[:, 3 * width :]).astype(bf16)
        lane_head = lax.broadcasted_iota(jnp.int32, (1, QUAD), 1) // HEAD_DIM
        scale = HEAD_DIM**-0.5
        for j in range(width // QUAD):
            lo = j * QUAD
            q4 = sa[here, lo : lo + QUAD]
            k4 = sa[here, width + lo : width + lo + QUAD]
            v4 = sa[here, 2 * width + lo : 2 * width + lo + QUAD]
            c4 = d_context[:, lo : lo + QUAD]
            k_turned = k4.T
            d_scores, queries, contexts, turned = [], [], [], []
            for h in range(4):
                pick = jnp.where(lane_head == h, 1.0, 0.0).astype(bf16)
                at = (4 * j + h) * rows
                probs = sb[here, at : at + rows].astype(f32)
                picked = c4 * pick
                d_probs = dot_nt(v4, picked)
                weighed = probs * d_probs
                d_score = (weighed - probs * total_rows(weighed)).astype(bf16)
                d_scores.append(d_score)
                queries.append(q4 * pick)
                contexts.append(picked)
                turned.append(dot(k_turned[h * HEAD_DIM : (h + 1) * HEAD_DIM], d_score))
            at = 4 * j * rows
            d_key = dot(jnp.concatenate(d_scores, 1), jnp.concatenate(queries, 0))
            d_value = dot(sb[here, at : at + 4 * rows], jnp.concatenate(contexts, 0))
            d_query = (jnp.concatenate(turned, 0) * scale).astype(bf16).T
            dr[here, lo : lo + QUAD] = d_query
            dr[here, width + lo : width + lo + QUAD] = (d_key * scale).astype(bf16)
            dr[here, 2 * width + lo : 2 * width + lo + QUAD] = d_value.astype(bf16)
        d_input = (d_resid + dot_nt(dr[here, : 3 * width], w_ref[:, : 3 * width])).astype(bf16)
        send[...] = d_input
        gin[here, :] = d_input


def ffn_forward_body(x, here, vec_ref, b2_ref, w_ref, d_ref, sa, sb):
    width = w_ref.shape[0]
    cuts = [slice(c * width, (c + 1) * width) for c in range(4)]
    branch = x.astype(f32) + b2_ref[0:1, :].astype(f32)
    pre = dot(x, w_ref[:, cuts[0]])
    for c in range(4):
        later = dot(x, w_ref[:, cuts[c + 1]]) if c < 3 else None
        hidden, slope = gelu_and_slope(pre + vec_ref[c : c + 1, :].astype(f32))
        hidden = hidden.astype(bf16)
        sa[here, cuts[c]] = hidden
        sb[here, cuts[c]] = slope.astype(bf16)
        branch = branch + dot(hidden, d_ref[cuts[c], :])
        pre = later
    return branch


def ffn_backward_body(d_resid, here, w_ref, d_ref, sb, dr, db):
    width = w_ref.shape[0]
    cuts = [slice(c * width, (c + 1) * width) for c in range(4)]
    d_branch = d_resid.astype(bf16)
    db[here, :] = d_branch
    d_input = d_resid
    d_hidden = dot_nt(d_branch, d_ref[cuts[0], :])
    for c in range(4):
        later = dot_nt(d_branch, d_ref[cuts[c + 1], :]) if c < 3 else None
        d_pre = (d_hidden * sb[here, cuts[c]].astype(f32)).astype(bf16)
        dr[here, cuts[c]] = d_pre
        d_input = d_input + dot_nt(d_pre, w_ref[:, cuts[c]])
        d_hidden = later
    return d_input.astype(bf16)


def ffn_forward_kernel(stage, slot, vec_ref, b2_ref, x_src, w_ref, d_ref, *refs):
    send, xs, acts, nb, rb, sa, sb = refs[6:13]
    rows, width = x_src.shape
    here = slice(slot * rows, (slot + 1) * rows)

    @pl.when(lax.axis_index("section") == stage)
    def _():
        x = x_src[...]
        xs[here, :] = x
        residual = ffn_forward_body(x, here, vec_ref, b2_ref, w_ref, d_ref, sa, sb)
        finish_section(residual, vec_ref[4:5, :].astype(f32), vec_ref[5:6, :].astype(f32), here, send, acts, nb, rb)


def ffn_backward_kernel(stage, slot, vec_ref, g_src, w_ref, d_ref, nb, rb, sb, *refs):
    send, gin, dr, db, vg = refs[4:9]
    rows, width = g_src.shape
    here = slice(slot * rows, (slot + 1) * rows)

    @pl.when(lax.axis_index("section") == stage)
    def _():
        d_resid = start_backward(g_src[...].astype(f32), vec_ref[4:5, :].astype(f32), slot, here, nb, rb, vg)
        d_input = ffn_backward_body(d_resid, here, w_ref, d_ref, sb, dr, db)
        send[...] = d_input
        gin[here, :] = d_input


def ffn_both_kernel(stage, slot, first, vec_ref, b2_ref, x_src, cot, w_ref, d_ref, *refs):
    send, xs, acts, nb, rb, sa, sb, gin, dr, db, vg = refs[6 if first else 10 :][:11]
    rows, width = x_src.shape
    here = slice(slot * rows, (slot + 1) * rows)

    @pl.when(lax.axis_index("section") == stage)
    def _():
        x = x_src[...]
        xs[here, :] = x
        residual = ffn_forward_body(x, here, vec_ref, b2_ref, w_ref, d_ref, sa, sb)
        gain = vec_ref[4:5, :].astype(f32)
        normed, rstd = normalise(residual)
        acts[here, :] = (normed * gain + vec_ref[5:6, :].astype(f32)).astype(bf16)
        grad = cot[here, :].astype(f32)
        vg[8 * slot : 8 * slot + 1, :] = total_rows(grad * normed)
        vg[8 * slot + 1 : 8 * slot + 2, :] = total_rows(grad)
        d_resid = norm_back(grad, normed, rstd, gain)
        d_input = ffn_backward_body(d_resid, here, w_ref, d_ref, sb, dr, db)
        send[...] = d_input
        gin[here, :] = d_input


LEAD = 16


def quarter(spread_out, other_half, other_core):
    me = lax.axis_index("dp")
    core = (me % 2) ^ other_core
    if not spread_out:
        return core
    return 2 * (((me >> 1) ^ (me >> 2)) % 2 ^ other_half) + core


def piece_kernel(spread_out, vectors, down, first, second, vec_v, sems):
    size = second.shape[0]
    at = pl.multiple_of(quarter(spread_out, 0, 0) * 2 * size, 16)
    copies = [
        pltpu.make_async_copy(vectors, vec_v, sems.at[0]),
        pltpu.make_async_copy(down.at[pl.ds(at, size), :], first.at[pl.ds(LEAD, size), :], sems.at[1]),
        pltpu.make_async_copy(down.at[pl.ds(at + size, size), :], second, sems.at[2]),
    ]
    for copy in copies:
        copy.start()
    for copy in copies:
        copy.wait()
    first[:LEAD, :] = jnp.broadcast_to(vec_v[5:6, :], (LEAD, first.shape[1]))


def setup_kernel(sections, lens, keep, vectors, x_in, cot, w_in, w_v, edge_v, vec_v, bias, lens_s, keep_v, sems):
    micro_count = lens.shape[0]
    rows = bias.shape[1]
    section = lax.axis_index("section")
    w_copy = pltpu.make_async_copy(w_in, w_v, sems.at[0])
    vec_copy = pltpu.make_async_copy(vectors, vec_v, sems.at[1])
    w_copy.start()
    vec_copy.start()

    @pl.when(section == 0)
    def _():
        pltpu.make_async_copy(x_in, edge_v, sems.at[2]).start()

    @pl.when(section == sections - 1)
    def _():
        pltpu.make_async_copy(cot, edge_v, sems.at[2]).start()

    @pl.when(section % 2 == 0)
    def _():
        lens_copy = pltpu.make_async_copy(lens, lens_s, sems.at[3])
        keep_copy = pltpu.make_async_copy(keep, keep_v, sems.at[4])
        lens_copy.start()
        keep_copy.start()
        key_pos = lax.broadcasted_iota(jnp.int32, (rows, rows), 0)
        query_pos = lax.broadcasted_iota(jnp.int32, (rows, rows), 1)
        lens_copy.wait()
        keep_copy.wait()
        for slot in range(micro_count):
            key_seg, query_seg, end = 0, 0, 0
            for k in range(lens.shape[1]):
                end = end + lens_s[slot, k]
                key_seg = key_seg + (key_pos >= end).astype(jnp.int32)
                query_seg = query_seg + (query_pos >= end).astype(jnp.int32)
            kept = jnp.broadcast_to(keep_v[slot : slot + 1, :].astype(f32), (rows, rows)).T > 0.5
            allowed = (key_seg == query_seg) & (kept | (key_pos == query_pos))
            bias[slot * rows : (slot + 1) * rows, :] = jnp.where(allowed, 0.0, neg_big)

    w_copy.wait()
    vec_copy.wait()

    @pl.when((section == 0) | (section == sections - 1))
    def _():
        pltpu.make_async_copy(x_in, edge_v, sems.at[2]).wait()


def own_down_kernel(down, out, token, sems):
    half = down.shape[0]
    token[...] = jnp.zeros_like(token)

    @pl.when(lax.axis_index("section") % 2 == 1)
    def _():
        copy = pltpu.make_async_copy(down, out.at[pl.ds(half, half), :], sems.at[0])
        copy.start()
        copy.wait()


def join_down_kernel(spread_out, places, *refs):
    out = refs[-1]

    @pl.when(lax.axis_index("section") % 2 == 1)
    def _():
        for block, (other_half, other_core, part, parts, lead) in zip(refs[: len(places)], places):
            size = block.shape[0] - lead
            at = quarter(spread_out, other_half, other_core) * parts + part
            out[pl.ds(pl.multiple_of(at * size, 16), size), :] = block[lead:, :]


TAIL = 16


def core_half(kept):
    core = lax.axis_index("dp") % 2
    return core if kept else 1 - core


def down_grad_kernel(kept, sa, db, out):
    width = db.shape[1]

    @pl.when(lax.axis_index("section") % 2 == 1)
    def _():
        half = core_half(kept)
        for part in range(2):
            at = pl.multiple_of((2 * part + half) * width, LANES)
            out[part] = dot_tn(sa[:, pl.ds(at, width)], db[...]).astype(bf16)


def in_grad_kernel(kind, kept, micro_count, xs, sa, dr, db, vg, *refs):
    out = refs[-1]
    width = xs.shape[1]

    @pl.when(lax.axis_index("section") % 2 == kind)
    def _():
        half = core_half(kept)
        out[width:, :] = jnp.zeros((TAIL, 2 * width), bf16)
        for k in range(2):
            right = dr[:, pl.ds(pl.multiple_of((2 * half + k) * width, LANES), width)]
            left = xs[...]
            if kind == 0 and k == 1:
                left = jnp.where(half == 1, sa[:, 3 * width :], left)
            here = slice(k * width, (k + 1) * width)
            out[:width, here] = dot_tn(left, right).astype(bf16)
            if k == 0:
                other = total_rows(db[...].astype(f32)) if kind else jnp.zeros((1, width), f32)
            else:
                other = jnp.zeros((1, width), f32)
            norm = sum(vg[8 * m + k : 8 * m + k + 1, :] for m in range(micro_count))
            sums = total_rows(right.astype(f32))
            both = jnp.concatenate([sums, jnp.where(half == 0, norm, other)], 0)
            out[width : width + 2, here] = both.astype(bf16)


def bit_of(bit):
    return (lax.axis_index("dp") >> bit) % 2


def added(a, b):
    return (a.astype(f32) + b.astype(f32)).astype(bf16)


def halve(kept, got, outs, bit, tail, cut=slice(None)):
    rows = (kept.shape[-2] - tail) // 2
    mine = bit_of(bit)
    for out, half in zip(outs, (mine, 1 - mine)):
        at = pl.ds(pl.multiple_of(half * rows, 16), rows)
        if kept.ndim == 3:
            out[...] = added(kept[:, at, cut], got[:, at, cut])
        else:
            out[:rows, :] = added(kept[at, cut], got[at, cut])
    if tail:
        last = slice(2 * rows, 2 * rows + tail)
        total = added(kept[last, cut], got[last, cut])
        for out in outs:
            out[rows:, :] = total


def first_add_kernel(live, bits, tail, kept, got, *outs):
    columns = kept.shape[-1] // 2

    @pl.when(live())
    def _():
        for stream in range(2):
            cut = slice(stream * columns, (stream + 1) * columns)
            halve(kept, got, outs[2 * stream : 2 * stream + 2], bits[stream], tail, cut)


def next_add_kernel(live, bits, tail, *refs):
    ins, outs = refs[:4], refs[4:]

    @pl.when(live())
    def _():
        for stream in range(2):
            halve(*ins[2 * stream : 2 * stream + 2], outs[2 * stream : 2 * stream + 2], bits[stream], tail)


def last_down_kernel(keep_a, got_a, keep_b, got_b, up, low):
    columns = keep_a.shape[-1]

    @pl.when(on_ffn())
    def _():
        for part, out in enumerate((up, low)):
            out[:, :columns] = added(keep_a[part], got_a[part])
            out[:, columns:] = added(keep_b[part], got_b[part])


def last_in_kernel(keep_a, got_a, keep_b, got_b, handed, low, pack_a, pack_b, tails):
    rows = pack_a.shape[0]
    wide = keep_a.shape[1]
    columns = low.shape[1] // 2
    for stream, (kept, got, out) in enumerate(((keep_a, got_a, pack_a), (keep_b, got_b, pack_b))):
        cut = slice(stream * columns, (stream + 1) * columns)
        out[:, :wide] = added(kept[:rows, :], got[:rows, :])
        out[:, wide:] = jnp.where(on_ffn(), low[:, cut], handed[:, cut])
        tails[stream] = added(kept[rows:, :], got[rows:, :])


def stack_kernel(upper, lower, out):
    rows = upper.shape[0]
    out[:rows, :] = upper[...]
    out[rows:, :] = lower[...]


def on_ffn():
    return lax.axis_index("section") % 2 == 1


def everywhere():
    return True


def swap(value, mask, only=None):
    count, sections = lax.axis_size("dp"), lax.axis_size("section")
    if only is None:
        return lax.ppermute(value, "dp", [(i, i ^ mask) for i in range(count)])
    pairs = [(i * sections + s, (i ^ mask) * sections + s) for i in range(count) for s in only]
    return lax.ppermute(value, ("dp", "section"), pairs)


def cut_shape(value, tail, columns=1):
    shape = list(value.shape)
    shape[-2] = (shape[-2] - tail) // 2 + tail
    shape[-1] //= columns
    return pltpu.VMEM(tuple(shape), value.dtype)


def reduce_streams(kept, got, orders, live, only, tail):
    outs = [cut_shape(kept, tail, 2)] * 4
    parts = kernel_call(functools.partial(first_add_kernel, live, [o[0] for o in orders], tail), outs, [kept, got])
    first = parts[0]
    for step in range(len(orders[0])):
        keep_a, send_a, keep_b, send_b = parts
        ins = [keep_a, swap(send_a, 1 << orders[0][step], only), keep_b, swap(send_b, 1 << orders[1][step], only)]
        if step + 1 < len(orders[0]):
            outs = [cut_shape(keep_a, tail)] * 4
            parts = kernel_call(
                functools.partial(next_add_kernel, live, [o[step + 1] for o in orders], tail), outs, ins
            )
    return ins, first


def far_index(owner, order):
    return sum(((owner >> bit) % 2) << (len(order) - 1 - k) for k, bit in enumerate(order))


def widen(src, lanes, dst, start, size):
    rows = 48 if size % 48 == 0 else size

    def step(n, carry):
        at = pl.ds(pl.multiple_of(start + n * rows, 16), rows)
        dst[at, :] = src[at, lanes].astype(f32)
        return carry

    lax.fori_loop(0, size // rows, step, 0)


def store_kernel(orders, masks, others, width, *refs):
    count = len(others)
    blocks = refs[:count]
    total_in, total_down, token, wide_buf, thin_buf, sems = refs[-6:]
    token[...] = jnp.zeros_like(token)
    me = lax.axis_index("dp")
    copies = []

    def send(src, dst):
        copy = pltpu.make_async_copy(src, dst, sems.at[len(copies)])
        copy.start()
        copies.append(copy)

    for n, (block, other) in enumerate(zip(blocks, others)):
        stream = n % 2
        half = (me % 2) ^ (1 if other else 0)
        size = block.shape[0] // len(masks[stream])
        thin = block.shape[1] - width
        lane = pl.multiple_of((2 * half + stream) * width, LANES)
        for k, mask in enumerate(masks[stream]):
            here = slice(k * size, (k + 1) * size)
            row = far_index(me ^ mask, orders[stream]) * size
            widen(block, slice(0, width), wide_buf.at[n], k * size, size)
            send(
                wide_buf.at[n, here, :],
                total_in.at[pl.ds(pl.multiple_of(row, 16), size), pl.ds(lane, width)],
            )
            widen(block, slice(width, width + thin), thin_buf.at[n], k * size, size)
            send(
                thin_buf.at[n, here, :],
                total_down.at[
                    pl.ds(pl.multiple_of(half * width + row, 16), size), stream * thin : (stream + 1) * thin
                ],
            )
    for copy in copies:
        copy.wait()


def keep_kernel(acts, gin, acts_out, gin_out, sems):
    copies = [
        pltpu.make_async_copy(acts, acts_out, sems.at[0]),
        pltpu.make_async_copy(gin, gin_out, sems.at[1]),
    ]
    for copy in copies:
        copy.start()
    for copy in copies:
        copy.wait()


def vector_kernel(own, other, b2_ref, out):
    core = lax.axis_index("dp") % 2
    own, other = own[...].astype(f32), other[...].astype(f32)
    first, second = jnp.where(core == 0, own, other), jnp.where(core == 0, other, own)
    sums = [first[0, 0:1], first[1, 0:1], second[0, 0:1], second[1, 0:1]]
    norms = [first[0, 1:2], first[1, 1:2]]

    @pl.when(on_ffn())
    def _():
        out[...] = jnp.concatenate(sums + norms, 0)

    @pl.when(jnp.logical_not(on_ffn()))
    def _():
        out[...] = jnp.concatenate([sums[0], sums[2], sums[3]] + norms + [b2_ref[0, 1:2].astype(f32)], 0)


def gate_kernel(*refs):
    pass


def gate(value, *after):
    return pl.pallas_call(
        gate_kernel,
        out_shape=jax.ShapeDtypeStruct(value.shape, value.dtype),
        in_specs=[ANYWHERE] * (1 + len(after)),
        out_specs=ANYWHERE,
        input_output_aliases={0: 0},
        compiler_params=pltpu.CompilerParams(vmem_limit_bytes=1024 * 1024),
        cost_estimate=pl.CostEstimate(flops=0, bytes_accessed=0, transcendentals=0),
        name="gate",
    )(value, *after)


def local(x_in, lengths, keep_mask, w_in, w_down, vectors, cotangent):
    micro_count = lengths.shape[0]
    tokens, width = x_in.shape
    rows = tokens // micro_count
    wide = 4 * width
    count = lax.axis_size("dp")
    bits = count.bit_length() - 1
    sections = lax.axis_size("section")
    me = lax.axis_index("dp")
    ffns = tuple(range(1, sections, 2))
    down = w_down[0]
    far = list(range(1, bits))
    orders = (far, far[::-1])

    def hop(value, stage, step):
        return lax.ppermute(value, "section", [(stage, stage + step)])

    onward = [(s, s + 1) for s in range(0, sections, 2)]
    spread_out = len(far) == 2
    share = down.shape[0] // (8 if spread_out else 4)
    pieces = kernel_call(
        functools.partial(piece_kernel, spread_out),
        [pltpu.VMEM((LEAD + share, width), bf16), pltpu.VMEM((share, width), bf16)],
        [vectors[0], down],
        scratch=[pltpu.VMEM(vectors.shape[1:], bf16), pltpu.SemaphoreType.DMA((3,))],
        plain_ins=(0, 1),
        name="piece",
    )
    pieces = [lax.ppermute(piece, "section", onward) for piece in pieces]
    weights, edge, vec, bias = kernel_call(
        functools.partial(setup_kernel, sections),
        [
            pltpu.VMEM((width, wide), bf16),
            pltpu.VMEM((tokens, width), bf16),
            pltpu.VMEM(vectors.shape[1:], bf16),
            pltpu.VMEM((tokens, rows), f32),
        ],
        [lengths, keep_mask.reshape(micro_count, rows), vectors[0], x_in, cotangent, w_in[0]],
        scratch=[
            pltpu.SMEM(lengths.shape, jnp.int32),
            pltpu.VMEM((micro_count, rows), jnp.int32),
            pltpu.SemaphoreType.DMA((5,)),
        ],
        plain_ins=range(6),
        name="setup",
    )
    own_down, down_token = kernel_call(
        own_down_kernel,
        [pltpu.VMEM((wide, width), bf16), pltpu.VMEM((8, LANES), f32)],
        [down],
        scratch=[pltpu.SemaphoreType.DMA((1,))],
        plain_ins=(0,),
        name="own_down",
    )

    row_out = pltpu.VMEM((rows, width), bf16)
    state = [
        pltpu.VMEM((tokens, width), bf16),
        pltpu.VMEM((tokens, width), bf16),
        pltpu.VMEM((tokens, width), f32),
        pltpu.VMEM((tokens, LANES), f32),
        pltpu.VMEM((tokens, wide), bf16),
        pltpu.VMEM((tokens, HEADS * rows), bf16),
    ]
    saved, grads = None, None

    def attn_forward(stage, slot, source):
        nonlocal saved
        first = saved is None
        got = kernel_call(
            functools.partial(attn_forward_kernel, stage, slot, first),
            [row_out] + state,
            [bias, vec, source, weights] + (saved or []),
            {} if first else {4 + k: 1 + k for k in range(6)},
            name=f"attn_forward_{stage}_{slot}",
        )
        saved = list(got[1:])
        return got[0]

    def ffn_forward(stage, slot, source):
        nonlocal saved
        got = kernel_call(
            functools.partial(ffn_forward_kernel, stage, slot),
            [row_out] + state,
            [vec, b2, source, weights, down_full] + saved,
            {5 + k: 1 + k for k in range(6)},
            name=f"ffn_forward_{stage}_{slot}",
        )
        saved = list(got[1:])
        return got[0]

    def ffn_both(stage, slot, source):
        nonlocal saved, grads
        first = grads is None
        grad_state = [
            pltpu.VMEM((tokens, width), bf16),
            pltpu.VMEM((tokens, wide), bf16),
            pltpu.VMEM((tokens, width), bf16),
            pltpu.VMEM((8 * micro_count, width), f32),
        ]
        got = kernel_call(
            functools.partial(ffn_both_kernel, stage, slot, first),
            [row_out] + state + grad_state,
            [vec, b2, source, edge, weights, down_full] + saved + (grads or []),
            {6 + k: 1 + k for k in range(6 if first else 10)},
            name=f"ffn_both_{stage}_{slot}",
        )
        saved, grads = list(got[1:7]), list(got[7:])
        return got[0]

    def attn_backward(stage, slot, source):
        nonlocal grads
        xs, acts, nb, rb, sa, sb = saved
        gin, dr, db, vg = grads
        got = kernel_call(
            functools.partial(attn_backward_kernel, stage, slot),
            [row_out, like(gin), like(dr), like(vg)],
            [vec, source, weights, nb, rb, sa, sb, gin, dr, vg],
            {7 + k: 1 + k for k in range(3)},
            name=f"attn_backward_{stage}_{slot}",
        )
        grads = [got[1], got[2], db, got[3]]
        return got[0]

    def ffn_backward(stage, slot, source):
        nonlocal grads
        xs, acts, nb, rb, sa, sb = saved
        got = kernel_call(
            functools.partial(ffn_backward_kernel, stage, slot),
            [row_out] + [like(a) for a in grads],
            [vec, source, weights, down_full, nb, rb, sb] + grads,
            {7 + k: 1 + k for k in range(4)},
            name=f"ffn_backward_{stage}_{slot}",
        )
        grads = list(got[1:])
        return got[0]

    sent = [attn_forward(0, slot, edge) for slot in range(micro_count)]
    arrived = [hop(value, 0, 1) for value in sent]
    blocks = [gate(piece, sent[0], down_token) for piece in pieces]
    b2 = blocks[0]
    places = [(0, 0, part, 2, 0 if part else LEAD) for part in range(2)]
    if spread_out:
        blocks += [swap(block, 1 << bit, ffns) for block, bit in zip(blocks, far)]
        places += [(1, 0, part, 2, 0 if part else LEAD) for part in range(2)]
    others = []
    for n, block in enumerate(blocks):
        last = n + 1 == len(blocks)
        others.append(swap(gate(block, arrived[0], *others) if last else block, 1, ffns))
    places += [(half, 1, part, parts, lead) for half, _, part, parts, lead in places]
    (down_full,) = kernel_call(
        functools.partial(join_down_kernel, spread_out, places),
        [pltpu.VMEM((wide, width), bf16)],
        blocks + others + [own_down],
        {len(places): 0},
        name="join",
    )
    for stage in range(1, sections - 1):
        step = ffn_forward if stage % 2 else attn_forward
        arrived = [hop(step(stage, slot, arrived[slot]), stage, 1) for slot in range(micro_count)]
    last = sections - 1
    arrived = [hop(ffn_both(last, slot, arrived[slot]), last, -1) for slot in range(micro_count)]
    for stage in range(last - 1, 0, -1):
        step = ffn_backward if stage % 2 else attn_backward
        arrived = [hop(step(stage, slot, arrived[slot]), stage, -1) for slot in range(micro_count)]
    xs, acts, nb, rb, sa, sb = saved

    down_shape = pltpu.VMEM((2, width, width), bf16)
    in_shape = pltpu.VMEM((width + TAIL, 2 * width), bf16)
    (down_sent,) = kernel_call(functools.partial(down_grad_kernel, False), [down_shape], [sa, grads[2]], name="down_send")
    (down_kept,) = kernel_call(functools.partial(down_grad_kernel, True), [down_shape], [sa, grads[2]], name="down_keep")

    def in_grad(kind, kept, before=None, after=None):
        gin, dr, db, vg = grads
        ins = [xs, sa, dr, db, vg] + [value for value in (before, after) if value is not None]
        body = functools.partial(in_grad_kernel, kind, kept, micro_count)
        name = f"in_grad_{kind}_{int(kept)}"
        return kernel_call(body, [in_shape], ins, {} if before is None else {5: 0}, name=name)[0]

    in_sent = in_grad(1, False, after=down_kept)
    down_ins, first = reduce_streams(down_kept, swap(down_sent, 1, ffns), orders, on_ffn, ffns, 0)

    for slot in range(micro_count):
        attn_backward(0, slot, gate(arrived[slot], in_sent) if slot == 0 else arrived[slot])
    in_sent, in_kept = in_grad(0, False, in_sent), in_grad(0, True, in_grad(1, True))
    gin = grads[0]

    in_ins, _ = reduce_streams(in_kept, swap(in_sent, 1), orders, everywhere, None, TAIL)
    share_rows = down_kept.shape[1] // (count // 2)
    up, low = kernel_call(
        last_down_kernel, [pltpu.VMEM((share_rows, width), bf16)] * 2, down_ins, name="last_down"
    )
    backward = [(s, s - 1) for s in ffns]
    handed = lax.ppermute(up, "section", backward)
    share_rows = in_ins[0].shape[0] - TAIL
    packed = pltpu.VMEM((share_rows, width + width // 2), bf16)
    pack_a, pack_b, tails = kernel_call(
        last_in_kernel,
        [packed, packed, pltpu.VMEM((2, TAIL, width), bf16)],
        in_ins + [handed, low],
        name="last_in",
    )

    other_tails = swap(tails, 1)
    b2_part = lax.ppermute(jnp.where(me % 2 == 0, other_tails, tails), "section", backward)
    (total_vec,) = kernel_call(vector_kernel, [pltpu.VMEM((6, width), f32)], [tails, other_tails, b2_part], name="vectors")

    blocks, masks = [pack_a, pack_b], [[0], [0]]
    for step in range(len(far)):
        bit = [orders[stream][len(far) - 1 - step] for stream in range(2)]
        got = [swap(blocks[stream], 1 << bit[stream]) for stream in range(2)]
        got_masks = [[m ^ (1 << bit[stream]) for m in masks[stream]] for stream in range(2)]
        if step + 1 < len(far):
            for stream in range(2):
                rows_now, cols_now = got[stream].shape
                (blocks[stream],) = kernel_call(
                    stack_kernel, [pltpu.VMEM((2 * rows_now, cols_now), bf16)], [blocks[stream], got[stream]]
                )
                masks[stream] = masks[stream] + got_masks[stream]
    outs = [
        jax.ShapeDtypeStruct((width, wide), f32),
        jax.ShapeDtypeStruct((2 * width, width), f32),
        pltpu.VMEM((8, LANES), f32),
    ]

    def store(blocks, masks, others, totals, name):
        shape = (len(blocks), blocks[0].shape[0])
        return kernel_call(
            functools.partial(store_kernel, orders, masks, others, width),
            outs,
            blocks + totals,
            {len(blocks) + k: k for k in range(len(totals))},
            scratch=[
                pltpu.VMEM(shape + (width,), f32),
                pltpu.VMEM(shape + (width // 2,), f32),
                pltpu.SemaphoreType.DMA((2 * len(blocks) * len(masks[0]),)),
            ],
            name=name,
            plain_ins=range(len(blocks), len(blocks) + len(totals)),
            limit=STORE_LIMIT,
            flops=STORE_COST[name],
        )

    acts, gin = kernel_call(
        keep_kernel,
        [jax.ShapeDtypeStruct(a.shape, a.dtype) for a in (acts, gin)],
        [acts, gin],
        scratch=[pltpu.SemaphoreType.DMA((2,))],
        name="keep",
    )
    early = blocks + [swap(b, 1) for b in blocks]
    *totals, token = store(early, masks, (False, False, True, True), [], "store_early")
    got = [gate(g, token) for g in got]
    *totals, token = store(got, got_masks, (False, False), totals, "store_own")
    total_in, total_down, _ = store([swap(g, 1) for g in got], got_masks, (True, True), totals, "store_other")
    return (acts[None], gin[None], total_in[None], total_down[None], total_vec[None])


def solution(mesh):
    placed = (
        P("dp", None),
        P("dp", None),
        P("dp"),
        P("section", None, None),
        P("section", None, None),
        P("section", None, None),
        P("dp", None),
    )
    return jax.shard_map(
        local,
        mesh=mesh,
        in_specs=placed,
        out_specs=(
            P("section", "dp", None),
            P("section", "dp", None),
            P("section", None, None),
            P("section", None, None),
            P("section", None, None),
        ),
        check_vma=False,
    )
```
